32 devices in a mesh: dp: 16 (over z, x, core), tensor: 2 (over y).
Axes of the slice: x: 2, y: 2, z: 4, core: 2. Of those that a mesh axis runs over, the one named last changes fastest.
Arguments:
- big_patches: bfloat16 [64, 1024, 768], P('dp'), may hold values from -6 to 6
- small_patches: bfloat16 [64, 256, 768], P('dp'), may hold values from -6 to 6
- big_visible: int32 [64, 256], P('dp'), may hold values from 0 to 1023, as said below
- small_visible: int32 [64, 64], P('dp'), may hold values from 0 to 255, as said below
- big_cot: bfloat16 [64, 256, 768], P('dp'), may hold values from -6 to 6
- small_cot: bfloat16 [64, 64, 768], P('dp'), may hold values from -6 to 6
- qkv_weight: float32 [768, 3, 768], P('dp', None, 'tensor'), may hold values from -0.21875 to 0.21875
- qkv_first: float32 [768, 3, 768], P('dp', None, 'tensor'), may hold values from -96 to 96
- qkv_second: float32 [768, 3, 768], P('dp', None, 'tensor'), may hold values from 4.096 to 163.84
- out_weight: float32 [768, 768], P('dp', 'tensor'), may hold values from -0.875 to 0.875
- out_first: float32 [768, 768], P('dp', 'tensor'), may hold values from -28 to 28
- out_second: float32 [768, 768], P('dp', 'tensor'), may hold values from 0.9216 to 14.7456
- up_weight: float32 [768, 3072], P('dp', 'tensor'), may hold values from -0.21875 to 0.21875
- up_first: float32 [768, 3072], P('dp', 'tensor'), may hold values from -24 to 24
- up_second: float32 [768, 3072], P('dp', 'tensor'), may hold values from 0.6144 to 10.24
- down_weight: float32 [768, 3072], P('dp', 'tensor'), may hold values from -0.109375 to 0.109375
- down_first: float32 [768, 3072], P('dp', 'tensor'), may hold values from -56 to 56
- down_second: float32 [768, 3072], P('dp', 'tensor'), may hold values from 3.6864 to 59.392
- up_bias: float32 [2, 1536], P('tensor', 'dp'), may hold values from -1.75 to 1.75
- up_bias_first: float32 [2, 1536], P('tensor', 'dp'), may hold values from -24 to 24
- up_bias_second: float32 [2, 1536], P('tensor', 'dp'), may hold values from 0.6144 to 10.24
- norm_vectors: float32 [6, 768], P(None, 'dp')
- norm_first: float32 [6, 768], P(None, 'dp'), may hold values from -64 to 64
- norm_second: float32 [6, 768], P(None, 'dp'), may hold values from 5.12 to 81.92
Outputs:
- big_out: bfloat16 [64, 256, 768], P('dp')
- small_out: bfloat16 [64, 64, 768], P('dp')
- big_grad: float32 [64, 1024, 768], P('dp')
- small_grad: float32 [64, 256, 768], P('dp')
- qkv_weight_new: float32 [768, 3, 768], P('dp', None, 'tensor')
- qkv_first_new: float32 [768, 3, 768], P('dp', None, 'tensor')
- qkv_second_new: float32 [768, 3, 768], P('dp', None, 'tensor')
- out_weight_new: float32 [768, 768], P('dp', 'tensor')
- out_first_new: float32 [768, 768], P('dp', 'tensor')
- out_second_new: float32 [768, 768], P('dp', 'tensor')
- up_weight_new: float32 [768, 3072], P('dp', 'tensor')
- up_first_new: float32 [768, 3072], P('dp', 'tensor')
- up_second_new: float32 [768, 3072], P('dp', 'tensor')
- down_weight_new: float32 [768, 3072], P('dp', 'tensor')
- down_first_new: float32 [768, 3072], P('dp', 'tensor')
- down_second_new: float32 [768, 3072], P('dp', 'tensor')
- up_bias_new: float32 [2, 1536], P('tensor', 'dp')
- up_bias_first_new: float32 [2, 1536], P('tensor', 'dp')
- up_bias_second_new: float32 [2, 1536], P('tensor', 'dp')
- norm_vectors_new: float32 [6, 768], P(None, 'dp')
- norm_first_new: float32 [6, 768], P(None, 'dp')
- norm_second_new: float32 [6, 768], P(None, 'dp')
The draws below stay inside these ranges and needn't reach their ends.
Inputs may be any that keep to these rules, and one draw needn't show every extreme that they name: `big_visible`: each row lists 256 different patch positions of its chip, in no particular order. `small_visible`: each row lists 64 different patch positions of its chip, in no particular order.
All inputs are finite; a program needn't handle non-finite values.
Results may differ from the reference program's by a relative error of at most 0.015.
Values may be sent and summed in bfloat16 or wider, within the bound.
A program may use at most 192 MiB of HBM per device.

```python
import math
import jax
import jax.numpy as jnp
from jax import lax

D = 768
HEADS = 12
HD = 64
FF = 3072
BIG_PATCH = 1024
SMALL_PATCH = 256
STEP_NUMBER = 10
BIG_VIS = 256
SMALL_VIS = 64
NBIG = 64
NSMALL = 64
TOKENS = 20480
N_TENSOR = 2


def choose_visible(key, chips, patches, keeping):
    scores = jax.random.randint(key, (chips, patches), 0, 2 ** 20, dtype=jnp.int32) * patches
    scores = scores + jnp.arange(patches, dtype=jnp.int32)[None, :]
    order = jnp.argsort(scores, axis=1, stable=True)
    return order[:, :keeping].astype(jnp.int32)


def draw_big_visible(key, part):
    key = jax.random.fold_in(key, 11)
    return choose_visible(key, NBIG, BIG_PATCH, BIG_VIS)


def draw_small_visible(key, part):
    key = jax.random.fold_in(key, 12)
    return choose_visible(key, NSMALL, SMALL_PATCH, SMALL_VIS)


def draw_norm_vectors(key, part):
    key = jax.random.fold_in(key, 13)
    gain_key, shift_key = jax.random.split(key)
    gains = 1.0 + 0.15 * jax.random.normal(gain_key, (2, D), jnp.float32)
    shifts = 0.3 * jax.random.normal(shift_key, (4, D), jnp.float32)
    return jnp.stack([gains[0], shifts[0], gains[1], shifts[1], shifts[2], shifts[3]], axis=0)


def block_scale(stream_key, shape, cuts, low, high):
    def one(axis_at, blocks):
        heights = jax.random.uniform(jax.random.fold_in(jax.random.fold_in(stream_key, 6), axis_at), (blocks,), jnp.float32, low / len(cuts), high / len(cuts))
        return jnp.repeat(jnp.exp(heights), shape[axis_at] // blocks).reshape((-1,) + (1,) * (len(shape) - axis_at - 1))

    loudness = one(*cuts[0])
    for cut in cuts[1:]:
        loudness = loudness * one(*cut)
    return loudness


def normal_values(stream_key, shape, width, reach, shards=(), kind=jnp.bfloat16):
    level = block_scale(stream_key, shape, shards, -0.22, 0.18) if shards else 1.0
    drawn = jax.random.normal(stream_key, shape, jnp.float32) * width * level
    return jnp.minimum(jnp.maximum(drawn, -reach), reach).astype(kind)


def setup_inputs(seed: int = 0) -> dict:
    keys = jax.random.split(jax.random.key(seed), 25)
    return {
        "big_patches": normal_values(keys[0], (NBIG, BIG_PATCH, D), 1.0, 6.0, ((0, 16),)),
        "small_patches": normal_values(keys[1], (NSMALL, SMALL_PATCH, D), 1.0, 6.0, ((0, 16),)),
        "big_visible": draw_big_visible(jax.random.fold_in(keys[24], 71), 0),
        "small_visible": draw_small_visible(jax.random.fold_in(keys[24], 71), 0),
        "big_cot": normal_values(keys[4], (NBIG, BIG_VIS, D), 1.0, 6.0, ((0, 16),)),
        "small_cot": normal_values(keys[5], (NSMALL, SMALL_VIS, D), 1.0, 6.0, ((0, 16),)),
        "qkv_weight": normal_values(keys[6], (D, 3, D), D ** -0.5, 0.21875, ((0, 16), (2, 2)), jnp.float32),
        "qkv_first": normal_values(keys[7], (D, 3, D), (0.11 * TOKENS ** 0.5), 96.0, ((0, 16), (2, 2)), jnp.float32),
        "qkv_second": jnp.clip(jnp.exp(math.log(163.84) - 3.6888794 * jax.random.uniform(keys[8], (D, 3, D), jnp.float32) ** block_scale(keys[8], (D, 3, D), ((0, 16), (2, 2)), -0.2, 0.2)), 4.096, 163.84),
        "out_weight": normal_values(keys[9], (D, D), (D // 16) ** -0.5, 0.875, ((0, 16), (1, 2)), jnp.float32),
        "out_first": normal_values(keys[10], (D, D), (0.033 * TOKENS ** 0.5), 28.0, ((0, 16), (1, 2)), jnp.float32),
        "out_second": jnp.clip(jnp.exp(math.log(14.7456) - 2.7725887 * jax.random.uniform(keys[11], (D, D), jnp.float32) ** block_scale(keys[11], (D, D), ((0, 16), (1, 2)), -0.2, 0.2)), 0.9216, 14.7456),
        "up_weight": normal_values(keys[12], (D, FF), D ** -0.5, 0.21875, ((0, 16), (1, 2)), jnp.float32),
        "up_first": normal_values(keys[13], (D, FF), (0.028 * TOKENS ** 0.5), 24.0, ((0, 16), (1, 2)), jnp.float32),
        "up_second": jnp.clip(jnp.exp(math.log(10.24) - 2.81341065 * jax.random.uniform(keys[14], (D, FF), jnp.float32) ** block_scale(keys[14], (D, FF), ((0, 16), (1, 2)), -0.2, 0.2)), 0.6144, 10.24),
        "down_weight": normal_values(keys[15], (D, FF), FF ** -0.5, 0.109375, ((0, 16), (1, 2)), jnp.float32),
        "down_first": normal_values(keys[16], (D, FF), (0.066 * TOKENS ** 0.5), 56.0, ((0, 16), (1, 2)), jnp.float32),
        "down_second": jnp.clip(jnp.exp(math.log(59.392) - 2.779509 * jax.random.uniform(keys[17], (D, FF), jnp.float32) ** block_scale(keys[17], (D, FF), ((0, 16), (1, 2)), -0.2, 0.2)), 3.6864, 59.392),
        "up_bias": normal_values(keys[18], (N_TENSOR, FF // N_TENSOR), 0.3, 1.75, ((0, 2), (1, 16)), jnp.float32),
        "up_bias_first": normal_values(keys[19], (N_TENSOR, FF // N_TENSOR), (0.028 * TOKENS ** 0.5), 24.0, ((0, 2), (1, 16)), jnp.float32),
        "up_bias_second": jnp.clip(jnp.exp(math.log(10.24) - 2.81341065 * jax.random.uniform(keys[20], (N_TENSOR, FF // N_TENSOR), jnp.float32) ** block_scale(keys[20], (N_TENSOR, FF // N_TENSOR), ((0, 2), (1, 16)), -0.2, 0.2)), 0.6144, 10.24),
        "norm_vectors": draw_norm_vectors(jax.random.fold_in(keys[24], 71), 0),
        "norm_first": normal_values(keys[22], (6, D), (0.077 * TOKENS ** 0.5), 64.0, ((1, 16),), jnp.float32),
        "norm_second": jnp.clip(jnp.exp(math.log(81.92) - 2.7725887 * jax.random.uniform(keys[23], (6, D), jnp.float32) ** block_scale(keys[23], (6, D), ((1, 16),), -0.2, 0.2)), 5.12, 81.92),
    }


PRECISE = lax.Precision.HIGHEST
LEARN_RATES = (0.03, 0.1, 0.03, 0.015, 0.2, 0.2)
DECAYS = (0.05, 0.05, 0.05, 0.05, 0.0, 0.0)

@jax.custom_vjp
def low(v):
    return lax.optimization_barrier(v.astype(jnp.bfloat16)).astype(jnp.float32)

@jax.custom_vjp
def low_back(v):
    return v

def low_keep(v):
    return (low(v), None)

def low_pass(kept, grad):
    return (grad,)

def back_keep(v):
    return (v, None)

def back_low(kept, grad):
    return (low(grad),)
low.defvjp(low_keep, low_pass)
low_back.defvjp(back_keep, back_low)

def layer_norm(row_data, norm_gain, norm_shift):
    centred = row_data - lax.optimization_barrier(jnp.mean(row_data, axis=-1, keepdims=True))
    spread = lax.optimization_barrier(jnp.mean(centred * centred, axis=-1, keepdims=True))
    return centred * lax.rsqrt(spread + 1e-05) * norm_gain + norm_shift

def attend_group(qkv_rows):
    chips, length = (qkv_rows.shape[0], qkv_rows.shape[1])
    pieces = qkv_rows.reshape(chips, length, 3, HEADS, HD)
    raw_scores = jnp.einsum('bqhd,bkhd->bhqk', pieces[:, :, 0], pieces[:, :, 1], precision=PRECISE) * HD ** (-0.5)
    attn_prob = low(jax.nn.softmax(low_back(raw_scores), axis=-1))
    mixture = jnp.einsum('bhqk,bkhd->bqhd', attn_prob, pieces[:, :, 2], precision=PRECISE)
    return mixture.reshape(chips, length, HEADS * HD)

def attend_all(qkv_rows):
    chips, length = (qkv_rows.shape[0], qkv_rows.shape[1])
    per_batch = math.gcd(chips, max(1, 4096 // length))
    grouped = qkv_rows.reshape(chips // per_batch, per_batch, length, 3, HEADS * HD)
    mixture = lax.map(jax.checkpoint(attend_group), grouped)
    return mixture.reshape(chips * length, HEADS * HD)

def pick_rows(row_data, places):
    return row_data[places]

def adam_step(weight, moment_one, moment_two, gradient, step_rate, decay_rate):
    moment_one = 0.9 * moment_one + 0.1 * gradient
    moment_two = 0.999 * moment_two + 0.001 * gradient * gradient
    fixed_one = moment_one / (1.0 - 0.9 ** STEP_NUMBER)
    fixed_two = moment_two / (1.0 - 0.999 ** STEP_NUMBER)
    update = fixed_one / (jnp.sqrt(fixed_two) + 1e-08) + decay_rate * weight
    return (weight - step_rate * update, moment_one, moment_two)

def reference(big_patches, small_patches, big_visible, small_visible, big_cot, small_cot, qkv_weight, qkv_first, qkv_second, out_weight, out_first, out_second, up_weight, up_first, up_second, down_weight, down_first, down_second, up_bias, up_bias_first, up_bias_second, norm_vectors, norm_first, norm_second):
    big_count, big_len = big_visible.shape
    small_count, small_len = small_visible.shape
    cut_at = big_count * big_len

    def forward(big_rows, small_rows, qkv_w, out_w, up_w, down_w, bias_up, vectors):
        qkv_w = low(qkv_w)
        out_w = low(out_w)
        up_w = low(up_w)
        down_w = low(down_w)
        bias_up = low(bias_up)
        vectors = low(vectors)
        big_taken = jax.vmap(pick_rows)(big_rows, big_visible)
        small_taken = jax.vmap(pick_rows)(small_rows, small_visible)
        rows_in = jnp.concatenate([big_taken.reshape(cut_at, D), small_taken.reshape(small_count * small_len, D)], axis=0)
        normed_one = low(layer_norm(rows_in, vectors[0], vectors[1]))
        qkv_rows = low_back(low(jnp.einsum('td,dcj->tcj', normed_one, qkv_w, precision=PRECISE)))
        heads_big = attend_all(qkv_rows[:cut_at].reshape(big_count, big_len, 3, D))
        heads_small = attend_all(qkv_rows[cut_at:].reshape(small_count, small_len, 3, D))
        heads_low = low_back(low(jnp.concatenate([heads_big, heads_small], axis=0)))
        attended = low_back(jnp.einsum('ti,oi->to', heads_low, out_w, precision=PRECISE))
        middle = rows_in + attended + vectors[4]
        normed_two = low(layer_norm(middle, vectors[2], vectors[3]))
        pre_act = low_back(jnp.dot(normed_two, up_w, precision=PRECISE) + bias_up.reshape(FF))
        activated = low(jax.nn.gelu(pre_act, approximate=False))
        output = middle + jnp.einsum('tf,of->to', activated, down_w, precision=PRECISE) + vectors[5]
        return (output[:cut_at].reshape(big_count, big_len, D), output[cut_at:].reshape(small_count, small_len, D))
    (big_y, small_y), pull = jax.vjp(forward, big_patches.astype(jnp.float32), small_patches.astype(jnp.float32), qkv_weight, out_weight, up_weight, down_weight, up_bias, norm_vectors)
    grads = pull((big_cot.astype(jnp.float32), small_cot.astype(jnp.float32)))
    qkv_new = adam_step(qkv_weight, qkv_first, qkv_second, grads[2], LEARN_RATES[0], DECAYS[0])
    out_new = adam_step(out_weight, out_first, out_second, grads[3], LEARN_RATES[1], DECAYS[1])
    up_new = adam_step(up_weight, up_first, up_second, grads[4], LEARN_RATES[2], DECAYS[2])
    down_new = adam_step(down_weight, down_first, down_second, grads[5], LEARN_RATES[3], DECAYS[3])
    bias_new = adam_step(up_bias, up_bias_first, up_bias_second, grads[6], LEARN_RATES[4], DECAYS[4])
    norm_new = adam_step(norm_vectors, norm_first, norm_second, grads[7], LEARN_RATES[5], DECAYS[5])
    return (big_y.astype(jnp.bfloat16), small_y.astype(jnp.bfloat16), grads[0], grads[1], qkv_new[0], qkv_new[1], qkv_new[2], out_new[0], out_new[1], out_new[2], up_new[0], up_new[1], up_new[2], down_new[0], down_new[1], down_new[2], bias_new[0], bias_new[1], bias_new[2], norm_new[0], norm_new[1], norm_new[2])
```

```python
import functools

import jax
import jax.numpy as jnp
from jax import lax
from jax.experimental import pallas as pl
from jax.experimental.pallas import tpu as pltpu
from jax.sharding import PartitionSpec as P

HD = 64
STEP_NUMBER = 10
BF, F32 = jnp.bfloat16, jnp.float32
MESH = pl.DeviceIdType.MESH
MIB = 2**20

LEARN_RATES = (0.03, 0.1, 0.03, 0.015, 0.2, 0.2)
DECAYS = (0.05, 0.05, 0.05, 0.05, 0.0, 0.0)

Z1, Z2, X, Y = 1, 2, 4, 8
DIMS = (Z1, Z2, X, Y)
ORDERS = ((Z1, Z2, X, Y), (Z1, Z2, Y, X))


def place(code, other_core=False):
    d, t = lax.axis_index("dp"), lax.axis_index("tensor")
    z, x, c = d // 4, (d // 2) % 2, d % 2
    if code & Z1:
        z = z + 1 - 2 * (z % 2)
    if code & Z2:
        z = z + 2 - 4 * (z // 2)
    if code & X:
        x = 1 - x
    if code & Y:
        t = 1 - t
    if other_core:
        c = 1 - c
    return z * 4 + x * 2 + c, t


def greet():
    barrier = pltpu.get_barrier_semaphore()
    for dim in DIMS:
        pl.semaphore_signal(barrier, inc=1, device_id=place(dim), device_id_type=MESH)
    pl.semaphore_signal(barrier, inc=1, device_id=place(0, True), device_id_type=MESH)
    pl.semaphore_wait(barrier, 5)


def bits(code):
    return bin(code).count("1")


def top_of(order, code):
    return max([order.index(k) for k in DIMS if code & k], default=-1)


def halves(cols):
    half = cols // 256 * 128
    return (pl.ds(0, half), pl.ds(half, cols - half))


def gather_kernel(p_ref, w_ref, send, recv, csend, crecv, own):
    groups, _, cols = p_ref.shape
    parts = tuple(zip(ORDERS, halves(cols)))
    greet()
    d, t = place(0)
    started = []

    def put(g, part, code, dim):
        pd, pt = place(code)
        span = parts[part][1]
        source = p_ref.at[g, :, span] if code == 0 else w_ref.at[g, pt, pd, :, span]
        move = pltpu.make_async_remote_copy(
            source,
            w_ref.at[g, pt, pd, :, span],
            send.at[g, part, DIMS.index(dim), code],
            recv.at[g, part, code ^ dim],
            device_id=place(dim),
            device_id_type=MESH,
        )
        move.start()
        started.append(move)

    def core_move(g, part, code, mine):
        pd, pt = place(code, not mine)
        span = parts[part][1]
        target = w_ref.at[g, pt, pd, :, span]
        source = p_ref.at[g, :, span] if code == 0 and mine else target
        return pltpu.make_async_remote_copy(
            source,
            target,
            csend.at[g, part, code],
            crecv.at[g, part, code],
            device_id=place(0, True),
            device_id_type=MESH,
        )

    def forward(g, part, code):
        order = parts[part][0]
        for dim in order[top_of(order, code) + 1 :]:
            put(g, part, code, dim)
        move = core_move(g, part, code, True)
        move.start()
        started.append(move)

    local = pltpu.make_async_copy(p_ref, w_ref.at[:, t, d], own)
    local.start()
    for g in range(groups):
        for part in range(2):
            forward(g, part, 0)
        for code in sorted(range(1, 16), key=bits):
            for part in range(2):
                order, span = parts[part]
                dim = order[top_of(order, code)]
                pd, pt = place(code)
                ref = w_ref.at[g, pt, pd, :, span]
                pltpu.make_async_remote_copy(
                    ref,
                    ref,
                    send.at[g, part, DIMS.index(dim), code ^ dim],
                    recv.at[g, part, code],
                    device_id=place(dim),
                    device_id_type=MESH,
                ).wait_recv()
                forward(g, part, code)
    local.wait()
    for g in range(groups):
        for part in range(2):
            for code in range(16):
                core_move(g, part, code, False).wait_recv()
    for move in started:
        move.wait_send()


def gather_weights(piece):
    groups, rows, cols = piece.shape
    return pl.pallas_call(
        gather_kernel,
        out_shape=jax.ShapeDtypeStruct((groups, 2, 16, rows, cols), piece.dtype),
        in_specs=[pl.BlockSpec(memory_space=pl.ANY)],
        out_specs=pl.BlockSpec(memory_space=pl.ANY),
        scratch_shapes=[
            pltpu.SemaphoreType.DMA((groups, 2, 4, 16)),
            pltpu.SemaphoreType.DMA((groups, 2, 16)),
            pltpu.SemaphoreType.DMA((groups, 2, 16)),
            pltpu.SemaphoreType.DMA((groups, 2, 16)),
            pltpu.SemaphoreType.DMA,
        ],
        compiler_params=pltpu.CompilerParams(collective_id=0, has_side_effects=True),
        name="gather_weights",
    )(piece)


def reduce_kernel(
    g_ref, rows_ref, out_ref, both_ref, total, from_core, from_chip, load, csend, crecv, send, recv, rsend, rrecv, own
):
    groups, _, _, rows, cols = g_ref.shape
    parts = tuple(zip(ORDERS, halves(cols)))
    slots = []
    for order in ORDERS:
        names = {}
        for at, dim in enumerate(order):
            for code in range(16):
                if top_of(order, code) < at:
                    names[code, dim] = len(names)
        slots.append(names)
    loads = [pltpu.make_async_copy(g_ref.at[g], total.at[g], load.at[g]) for g in range(groups)]
    for copy in loads:
        copy.start()
    greet()
    t = lax.axis_index("tensor")
    started = []
    swap = pltpu.make_async_remote_copy(
        rows_ref, both_ref.at[t], rsend, rrecv, device_id=place(Y), device_id_type=MESH
    )
    swap.start()
    local = pltpu.make_async_copy(rows_ref, both_ref.at[t], own)
    local.start()

    def core_move(g, code):
        pd, pt = place(code, True)
        return pltpu.make_async_remote_copy(
            total.at[g, pt, pd],
            from_core.at[g, code],
            csend.at[g, code],
            crecv.at[g, code],
            device_id=place(0, True),
            device_id_type=MESH,
        )

    def chip_move(g, part, code, dim, sending):
        pd, pt = place(code)
        span = parts[part][1]
        there = code ^ dim if sending else code
        slot = slots[part][there, dim]
        return pltpu.make_async_remote_copy(
            total.at[g, pt, pd, :, span],
            from_chip.at[g, slot, :, span],
            send.at[g, part, slot],
            recv.at[g, part, slot],
            device_id=place(dim),
            device_id_type=MESH,
        )

    codes = sorted(range(16), key=lambda code: -bits(code))
    for g in range(groups):
        loads[g].wait()
        for code in codes:
            move = core_move(g, code)
            move.start()
            started.append(move)
    for g in range(groups):
        for code in codes:
            pd, pt = place(code)
            core_move(g, code).wait_recv()
            for part in range(2):
                order, span = parts[part]
                value = total[g, pt, pd, :, span].astype(F32) + from_core[g, code, :, span].astype(F32)
                at = top_of(order, code)
                for dim in reversed(order[at + 1 :]):
                    chip_move(g, part, code, dim, False).wait_recv()
                    value = value + from_chip[g, slots[part][code, dim], :, span].astype(F32)
                if code == 0:
                    out_ref[g, :, span] = value
                else:
                    total[g, pt, pd, :, span] = value.astype(BF)
                    move = chip_move(g, part, code, order[at], True)
                    move.start()
                    started.append(move)
    local.wait()
    swap.wait_recv()
    swap.wait_send()
    for move in started:
        move.wait_send()


def reduce_grads(grads, rows_pair):
    groups, _, _, rows, cols = grads.shape
    return pl.pallas_call(
        reduce_kernel,
        out_shape=(
            jax.ShapeDtypeStruct((groups, rows, cols), F32),
            jax.ShapeDtypeStruct((2,) + rows_pair.shape, BF),
        ),
        in_specs=[pl.BlockSpec(memory_space=pl.ANY)] * 2,
        out_specs=(pl.BlockSpec(memory_space=pltpu.VMEM), pl.BlockSpec(memory_space=pl.ANY)),
        scratch_shapes=[
            pltpu.VMEM(grads.shape, BF),
            pltpu.VMEM((groups, 16, rows, cols), BF),
            pltpu.VMEM((groups, 15, rows, cols), BF),
            pltpu.SemaphoreType.DMA((groups,)),
            pltpu.SemaphoreType.DMA((groups, 16)),
            pltpu.SemaphoreType.DMA((groups, 16)),
            pltpu.SemaphoreType.DMA((groups, 2, 15)),
            pltpu.SemaphoreType.DMA((groups, 2, 15)),
            pltpu.SemaphoreType.DMA,
            pltpu.SemaphoreType.DMA,
            pltpu.SemaphoreType.DMA,
        ],
        compiler_params=pltpu.CompilerParams(
            collective_id=1, has_side_effects=True, vmem_limit_bytes=56 * MIB
        ),
        name="reduce_grads",
    )(grads, rows_pair)


def dot(a, b):
    return jnp.dot(a, b, preferred_element_type=F32)


def dot_nt(a, b):
    return lax.dot_general(a, b, (((1,), (1,)), ((), ())), preferred_element_type=F32)


def normed(v):
    centred = v - jnp.mean(v, axis=-1, keepdims=True)
    r = lax.rsqrt(jnp.mean(centred * centred, axis=-1, keepdims=True) + 1e-05)
    return centred * r, r


def norm_back(e, xhat, r, gain):
    eg = e * gain
    return r * (eg - jnp.mean(eg, axis=-1, keepdims=True) - xhat * jnp.mean(eg * xhat, axis=-1, keepdims=True))


def column_of(row):
    wide = jnp.broadcast_to(row.astype(F32), (128, row.shape[1]))
    return jnp.transpose(wide).astype(jnp.int32)


def layer_kernel(
    shape,
    big_ref, small_ref, bvis_ref, svis_ref, bcot_ref, scot_ref, w_ref, vec_ref, bias_ref,
    out_ref, back_ref, g_ref, vgrad_ref, bgrad_ref,
    w, patch, patch_small, x, n1, n1t, qkv, prob, prob_small, heads, mid, n2, n2t, act, slope, cot, cott, dqkv, acc,
    w_sem, p_sem, c_sem, g_sem,
):
    nb, bl, ns, sl, wide = shape
    cut = nb * bl
    tokens = cut + ns * sl
    half = 768 // 2
    pairs = half // 128
    t = lax.axis_index("tensor")
    block = 128
    steps = tokens // block

    loads = [[pltpu.make_async_copy(w_ref.at[g, k], w.at[g, k], w_sem.at[g, k]) for k in range(2)] for g in range(3)]
    ploads = [pltpu.make_async_copy(big_ref.at[t * nb + i], patch.at[i], p_sem.at[i]) for i in range(nb)]
    ploads += [pltpu.make_async_copy(small_ref.at[t * ns + i], patch_small.at[i], p_sem.at[nb + i]) for i in range(ns)]
    cloads = [
        pltpu.make_async_copy(bcot_ref.at[t * nb + i], cot.at[pl.ds(i * bl, bl)], c_sem.at[i]) for i in range(nb)
    ]
    cloads += [
        pltpu.make_async_copy(scot_ref.at[t * ns + i], cot.at[pl.ds(cut + i * sl, sl)], c_sem.at[nb + i])
        for i in range(ns)
    ]
    for copy in ploads + loads[0] + cloads + loads[1] + loads[2]:
        copy.start()

    def pick(vis_ref, row, source, length):
        column = column_of(vis_ref[row])
        lane = lax.broadcasted_iota(jnp.int32, column.shape, 1)
        hot = jnp.concatenate([(column == lane + k * 128).astype(BF) for k in range(length // 128)], axis=1)
        return dot(hot, source).astype(BF)

    for i in range(nb):
        ploads[i].wait()
        x[pl.ds(i * bl, bl), :] = pick(bvis_ref, t * nb + i, patch[i], patch.shape[1])
    for i in range(ns):
        ploads[nb + i].wait()
        x[pl.ds(cut + i * sl, sl), :] = pick(svis_ref, t * ns + i, patch_small[i], patch_small.shape[1])

    def vec(i):
        return vec_ref[i : i + 1, :]

    def rows_of(i):
        return pl.ds(pl.multiple_of(i * block, block), block)

    @pl.loop(0, steps)
    def _(i):
        xhat, r = normed(x[rows_of(i), :].astype(F32))
        value = xhat * vec(0) + vec(1)
        n1[rows_of(i), :] = value.astype(BF)
        n1t[:, rows_of(i)] = jnp.transpose(value).astype(BF)

    for copy in loads[0]:
        copy.wait()

    @pl.loop(0, 6)
    def _(i):
        k, c = i // 3, i % 3
        span = pl.ds(pl.multiple_of(c * half, half), half)
        qkv[k, :, span] = dot(n1[...], w[0, k, :, span]).astype(BF)

    lane = lax.broadcasted_iota(jnp.int32, (1, 128), 1)
    first = lane < HD

    def softmax(scores):
        e = jnp.exp(scores - jnp.max(scores, axis=-1, keepdims=True))
        return e / jnp.sum(e, axis=-1, keepdims=True)

    small_rows = ns * sl
    same = (
        lax.broadcasted_iota(jnp.int32, (small_rows, small_rows), 0) // sl
        == lax.broadcasted_iota(jnp.int32, (small_rows, small_rows), 1) // sl
    )
    spans = [(i, pl.ds(i * bl, bl)) for i in range(nb)] + [(nb, pl.ds(cut, small_rows))]

    def pair_spans(pair):
        k, j = pair // pairs, pair % pairs
        return k, [pl.ds(pl.multiple_of(c * half + j * 128, 128), 128) for c in range(3)]

    zero = jnp.zeros((), BF)

    @pl.loop(0, 2 * pairs)
    def _(pair):
        k, lanes = pair_spans(pair)
        for i, rows in spans:
            q, key, value = (qkv[k, rows, lanes[c]] for c in range(3))
            mixed = []
            for h in range(2):
                q_head = jnp.where(first if h == 0 else ~first, q, zero)
                scores = dot_nt(q_head, key) * HD ** (-0.5)
                if i == nb:
                    scores = jnp.where(same, scores, -jnp.inf)
                p = softmax(scores).astype(BF)
                if i == nb:
                    prob_small[pair, h] = p
                else:
                    prob[pair, i, h] = p
                mixed.append(dot(p, value))
            heads[rows, pl.ds(pl.multiple_of(pair * 128, 128), 128)] = jnp.where(first, mixed[0], mixed[1]).astype(BF)

    @pl.loop(0, 3)
    def _(i):
        span = pl.ds(pl.multiple_of(i * 256, 256), 256)
        mid[:, span] = dot_nt(heads[:, :half], w[0, 0, span, pl.ds(1152, half)]) + dot_nt(
            heads[:, half:], w[0, 1, span, pl.ds(1152, half)]
        )

    @pl.loop(0, steps)
    def _(i):
        middle = x[rows_of(i), :].astype(F32) + mid[rows_of(i), :] + vec(4)
        mid[rows_of(i), :] = middle
        xhat, r = normed(middle)
        value = xhat * vec(2) + vec(3)
        n2[rows_of(i), :] = value.astype(BF)
        n2t[:, rows_of(i)] = jnp.transpose(value).astype(BF)
        acc[rows_of(i), :] = middle + vec(5)

    for copy in loads[1]:
        copy.wait()
    tiles = 2 * (wide // 256)

    def tile_of(i):
        return i // (tiles // 2), pl.ds(pl.multiple_of((i % (tiles // 2)) * 256, 256), 256)

    @pl.loop(0, tiles)
    def _(i):
        k, span = tile_of(i)
        acc_pre = dot(n2[...], w[1, k, :, span]) + bias_ref[i]
        cdf = 0.5 * (1.0 + lax.erf(acc_pre * 0.7071067811865476))
        act[i] = (acc_pre * cdf).astype(BF)
        slope[i] = (cdf + acc_pre * jnp.exp(-0.5 * acc_pre * acc_pre) * 0.3989422804014327).astype(BF)

    for copy in loads[2]:
        copy.wait()

    @pl.loop(0, tiles)
    def _(i):
        k, span = tile_of(i)
        acc[...] += dot_nt(act[i], w[2, k, :, span])

    out_ref[...] = acc[...].astype(BF)

    for copy in cloads:
        copy.wait()

    @pl.loop(0, steps)
    def _(i):
        value = cot[rows_of(i), :].astype(F32)
        cott[:, rows_of(i)] = jnp.transpose(value).astype(BF)

    acc[...] = jnp.zeros_like(acc)

    @pl.loop(0, tiles)
    def _(i):
        k, span = tile_of(i)
        back = (slope[i].astype(F32) * dot(cot[...], w[2, k, :, span])).astype(BF)
        bgrad_ref[i] = jnp.sum(back.astype(F32), axis=0, keepdims=True)
        w[2, k, :, span] = dot(cott[...], act[i]).astype(BF)
        acc[...] += dot_nt(back, w[1, k, :, span])
        w[1, k, :, span] = dot(n2t[...], back).astype(BF)

    saves = [
        [pltpu.make_async_copy(w.at[g, k], g_ref.at[g, k], g_sem.at[g, k]) for k in range(2)] for g in range(3)
    ]
    for copy in saves[1] + saves[2]:
        copy.start()

    back_attn, back_attn_t, back_heads = n2, n2t, x
    vgrad_ref[...] = jnp.zeros_like(vgrad_ref)

    @pl.loop(0, steps)
    def _(i):
        e = acc[rows_of(i), :]
        xhat, r = normed(mid[rows_of(i), :])
        back_out = cot[rows_of(i), :].astype(F32)
        back_middle = back_out + norm_back(e, xhat, r, vec(2))
        acc[rows_of(i), :] = back_middle
        back_attn[rows_of(i), :] = back_middle.astype(BF)
        back_attn_t[:, rows_of(i)] = jnp.transpose(back_middle).astype(BF)
        vgrad_ref[2:3, :] += jnp.sum(e * xhat, axis=0, keepdims=True)
        vgrad_ref[3:4, :] += jnp.sum(e, axis=0, keepdims=True)
        vgrad_ref[4:5, :] += jnp.sum(back_middle, axis=0, keepdims=True)
        vgrad_ref[5:6, :] += jnp.sum(back_out, axis=0, keepdims=True)

    dheads = cot
    for k in range(2):
        span = pl.ds(1152, half)
        dheads[:, pl.ds(k * half, half)] = dot(back_attn[...], w[0, k, :, span]).astype(BF)
        w[0, k, :, span] = dot(back_attn_t[...], heads[:, pl.ds(k * half, half)]).astype(BF)

    @pl.loop(0, 2 * pairs)
    def _(pair):
        k, lanes = pair_spans(pair)
        for i, rows in spans:
            q, key, value = (qkv[k, rows, lanes[c]] for c in range(3))
            dh = dheads[rows, pl.ds(pl.multiple_of(pair * 128, 128), 128)]
            dh_t = jnp.transpose(dh.astype(F32)).astype(BF)
            q_t = jnp.transpose(q.astype(F32)).astype(BF)
            dq, dk_t, dv_t = [], [], []
            for h in range(2):
                p = prob_small[pair, h] if i == nb else prob[pair, i, h]
                dh_head = jnp.where(first if h == 0 else ~first, dh, zero)
                dp = dot_nt(dh_head, value)
                pf = p.astype(F32)
                ds = (pf * (dp - jnp.sum(pf * dp, axis=-1, keepdims=True))).astype(BF)
                dq.append(dot(ds, key))
                dk_t.append(dot(q_t[h * HD : (h + 1) * HD], ds))
                dv_t.append(dot(dh_t[h * HD : (h + 1) * HD], p))
            scale = HD ** (-0.5)
            dqkv[k, rows, lanes[0]] = (jnp.where(first, dq[0], dq[1]) * scale).astype(BF)
            dqkv[k, rows, lanes[1]] = jnp.transpose(jnp.concatenate(dk_t, axis=0) * scale).astype(BF)
            dqkv[k, rows, lanes[2]] = jnp.transpose(jnp.concatenate(dv_t, axis=0)).astype(BF)

    @pl.loop(0, 3)
    def _(i):
        span = pl.ds(pl.multiple_of(i * 256, 256), 256)
        mid[:, span] = dot_nt(dqkv[0], w[0, 0, span, pl.ds(0, 1152)]) + dot_nt(
            dqkv[1], w[0, 1, span, pl.ds(0, 1152)]
        )

    @pl.loop(0, 6)
    def _(i):
        k, c = i // 3, i % 3
        span = pl.ds(pl.multiple_of(c * half, half), half)
        w[0, k, :, span] = dot(n1t[...], dqkv[k, :, span]).astype(BF)

    for copy in saves[0]:
        copy.start()

    @pl.loop(0, steps)
    def _(i):
        e = mid[rows_of(i), :]
        xhat, r = normed(x[rows_of(i), :].astype(F32))
        back_in = acc[rows_of(i), :] + norm_back(e, xhat, r, vec(0))
        back_ref[rows_of(i), :] = back_in.astype(BF)
        vgrad_ref[0:1, :] += jnp.sum(e * xhat, axis=0, keepdims=True)
        vgrad_ref[1:2, :] += jnp.sum(e, axis=0, keepdims=True)

    for copy in saves[0] + saves[1] + saves[2]:
        copy.wait()


def run_layer(big, small, bvis, svis, bcot, scot, w, vectors, bias, parts):
    nb, bl = bvis.shape[0] // parts, bvis.shape[2]
    ns, sl = svis.shape[0] // parts, svis.shape[2]
    tokens = nb * bl + ns * sl
    feat = big.shape[2]
    wide = w.shape[3]
    tiles = 2 * (wide // 256)
    pairs = feat // 128
    vm, hbm = pl.BlockSpec(memory_space=pltpu.VMEM), pl.BlockSpec(memory_space=pl.ANY)
    return pl.pallas_call(
        functools.partial(layer_kernel, (nb, bl, ns, sl, wide)),
        out_shape=(
            jax.ShapeDtypeStruct((tokens, feat), BF),
            jax.ShapeDtypeStruct((tokens, feat), BF),
            jax.ShapeDtypeStruct(w.shape, BF),
            jax.ShapeDtypeStruct((8, feat), F32),
            jax.ShapeDtypeStruct((tiles, 1, 256), F32),
        ),
        in_specs=[hbm, hbm, vm, vm, hbm, hbm, hbm, vm, vm],
        out_specs=(vm, vm, hbm, vm, vm),
        scratch_shapes=[
            pltpu.VMEM(w.shape, BF),
            pltpu.VMEM((nb,) + big.shape[1:], BF),
            pltpu.VMEM((ns,) + small.shape[1:], BF),
            pltpu.VMEM((tokens, feat), BF),
            pltpu.VMEM((tokens, feat), BF),
            pltpu.VMEM((feat, tokens), BF),
            pltpu.VMEM((2, tokens, 3 * feat // 2), BF),
            pltpu.VMEM((pairs, nb, 2, bl, bl), BF),
            pltpu.VMEM((pairs, 2, ns * sl, ns * sl), BF),
            pltpu.VMEM((tokens, feat), BF),
            pltpu.VMEM((tokens, feat), F32),
            pltpu.VMEM((tokens, feat), BF),
            pltpu.VMEM((feat, tokens), BF),
            pltpu.VMEM((tiles, tokens, 256), BF),
            pltpu.VMEM((tiles, tokens, 256), BF),
            pltpu.VMEM((tokens, feat), BF),
            pltpu.VMEM((feat, tokens), BF),
            pltpu.VMEM((2, tokens, 3 * feat // 2), BF),
            pltpu.VMEM((tokens, feat), F32),
            pltpu.SemaphoreType.DMA((3, 2)),
            pltpu.SemaphoreType.DMA((nb + ns,)),
            pltpu.SemaphoreType.DMA((nb + ns,)),
            pltpu.SemaphoreType.DMA((3, 2)),
        ],
        compiler_params=pltpu.CompilerParams(vmem_limit_bytes=60 * MIB),
        name="layer",
    )(big, small, bvis, svis, bcot, scot, w, vectors, bias)


def scatter_kernel(bvis_ref, svis_ref, brow_ref, srow_ref, big_ref, small_ref):
    def spread(vis, rows, length):
        hot = lax.broadcasted_iota(jnp.int32, (length, vis.shape[1]), 0) == vis
        return dot(hot.astype(BF), rows)

    big_ref[...] = spread(bvis_ref[...], brow_ref[...], big_ref.shape[0])
    small_ref[...] = spread(svis_ref[...], srow_ref[...], small_ref.shape[0])


def scatter_rows(bvis, svis, rows, big_len, small_len):
    parts = rows.shape[0]
    nb, _, bl = bvis.shape
    ns, _, sl = svis.shape
    feat = rows.shape[2]
    share = nb // parts
    first_small = share * bl // sl
    return pl.pallas_call(
        scatter_kernel,
        grid=(nb,),
        out_shape=(
            jax.ShapeDtypeStruct((nb, big_len, feat), F32),
            jax.ShapeDtypeStruct((ns, small_len, feat), F32),
        ),
        in_specs=[
            pl.BlockSpec((None, 1, bl), lambda i: (i, 0, 0)),
            pl.BlockSpec((None, 1, sl), lambda i: (i, 0, 0)),
            pl.BlockSpec((None, bl, feat), lambda i: (i // share, i % share, 0)),
            pl.BlockSpec((None, sl, feat), lambda i: (i // share, first_small + i % share, 0)),
        ],
        out_specs=(
            pl.BlockSpec((None, big_len, feat), lambda i: (i, 0, 0)),
            pl.BlockSpec((None, small_len, feat), lambda i: (i, 0, 0)),
        ),
        compiler_params=pltpu.CompilerParams(vmem_limit_bytes=40 * MIB),
        name="scatter_rows",
    )(bvis, svis, rows, rows)


def adam_step(weight, moment_one, moment_two, gradient, step_rate, decay_rate):
    moment_one = 0.9 * moment_one + 0.1 * gradient
    moment_two = 0.999 * moment_two + 0.001 * gradient * gradient
    fixed_one = moment_one / (1.0 - 0.9**STEP_NUMBER)
    fixed_two = moment_two / (1.0 - 0.999**STEP_NUMBER)
    update = fixed_one / (jnp.sqrt(fixed_two) + 1e-08) + decay_rate * weight
    return (weight - step_rate * update, moment_one, moment_two)


def on_device(
    special,
    big_patches, small_patches, big_visible, small_visible, big_cot, small_cot,
    qkv_weight, qkv_first, qkv_second, out_weight, out_first, out_second,
    up_weight, up_first, up_second, down_weight, down_first, down_second,
    up_bias, up_bias_first, up_bias_second, norm_vectors, norm_first, norm_second,
):
    rows, half = out_weight.shape
    wide = up_weight.shape[1]
    feat = big_patches.shape[2]
    parts = feat // half
    piece = jnp.stack(
        [
            jnp.concatenate([qkv_weight.reshape(rows, 3 * half), out_weight], axis=1).astype(BF),
            up_weight.astype(BF),
            down_weight.astype(BF),
        ]
    )
    if special:
        w = gather_weights(piece).reshape(3, parts, feat, wide)
    else:
        w = lax.all_gather(lax.all_gather(piece, "dp", axis=1, tiled=True), "tensor", axis=1)
    vectors = lax.all_gather(norm_vectors.astype(BF), "dp", axis=1, tiled=True).astype(F32)
    vectors = jnp.concatenate([vectors, jnp.zeros((2, feat), F32)], axis=0)
    bias = lax.all_gather(up_bias.astype(BF), "dp", axis=1, tiled=True)
    bias = lax.all_gather(bias, "tensor", axis=0, tiled=True).astype(F32)
    bias = bias.reshape(2 * (wide // 256), 1, 256)

    bvis, svis = big_visible[:, None, :], small_visible[:, None, :]
    out_rows, back_rows, grads, vgrad, bgrad = run_layer(
        big_patches, small_patches, bvis, svis, big_cot, small_cot, w, vectors, bias, parts
    )
    pair = jnp.stack([out_rows, back_rows])
    if special:
        share, both = reduce_grads(grads.reshape(3, parts, -1, rows, wide), pair)
    else:
        share = lax.psum_scatter(grads, "tensor", scatter_dimension=1)
        share = lax.psum_scatter(share, "dp", scatter_dimension=1, tiled=True).astype(F32)
        both = lax.all_gather(pair, "tensor", axis=0)
    vgrad = lax.psum(vgrad[:6], "tensor")
    norm_share = lax.psum_scatter(vgrad, "dp", scatter_dimension=1, tiled=True)
    bias_share = lax.psum_scatter(bgrad.reshape(parts, wide), "tensor", scatter_dimension=0, tiled=True)
    bias_share = lax.psum_scatter(bias_share, "dp", scatter_dimension=1, tiled=True)
    big_count, big_len = big_visible.shape
    small_count, small_len = small_visible.shape
    cut = big_count // parts * big_len
    big_out = both[:, 0, :cut].reshape(big_count, big_len, feat)
    small_out = both[:, 0, cut:].reshape(small_count, small_len, feat)
    big_grad, small_grad = scatter_rows(bvis, svis, both[:, 1], big_patches.shape[1], small_patches.shape[1])

    qkv_share = share[0, :, : 3 * half].reshape(rows, 3, half)
    new = []
    for at, (weight, one, two, gradient) in enumerate(
        (
            (qkv_weight, qkv_first, qkv_second, qkv_share),
            (out_weight, out_first, out_second, share[0, :, 3 * half :]),
            (up_weight, up_first, up_second, share[1]),
            (down_weight, down_first, down_second, share[2]),
            (up_bias, up_bias_first, up_bias_second, bias_share),
            (norm_vectors, norm_first, norm_second, norm_share),
        )
    ):
        new.extend(adam_step(weight, one, two, gradient, LEARN_RATES[at], DECAYS[at]))
    return (big_out, small_out, big_grad, small_grad, *new)


def solution(mesh):
    special = mesh.shape["dp"] == 16 and mesh.shape["tensor"] == 2
    chips = P("dp", None, None)
    matrix, qkv = P("dp", "tensor"), P("dp", None, "tensor")
    states = (qkv,) * 3 + (matrix,) * 9 + (P("tensor", "dp"),) * 3 + (P(None, "dp"),) * 3
    return jax.shard_map(
        functools.partial(on_device, special),
        mesh=mesh,
        in_specs=(chips, chips, P("dp", None), P("dp", None), chips, chips) + states,
        out_specs=(chips,) * 4 + states,
        check_vma=False,
    )
```

```python
import functools

import jax
import jax.numpy as jnp
from jax import lax
from jax.experimental import pallas as pl
from jax.experimental.pallas import tpu as pltpu
from jax.sharding import PartitionSpec as P

HD = 64
STEP_NUMBER = 10
BF, F32 = jnp.bfloat16, jnp.float32
MESH = pl.DeviceIdType.MESH
MIB = 2**20

LEARN_RATES = (0.03, 0.1, 0.03, 0.015, 0.2, 0.2)
DECAYS = (0.05, 0.05, 0.05, 0.05, 0.0, 0.0)

Z1, Z2, X, Y = 1, 2, 4, 8
DIMS = (Z1, Z2, X, Y)
ORDERS = ((Z1, Z2, X, Y), (Z1, Z2, Y, X))


def place(code, other_core=False):
    d, t = lax.axis_index("dp"), lax.axis_index("tensor")
    z, x, c = d // 4, (d // 2) % 2, d % 2
    if code & Z1:
        z = z + 1 - 2 * (z % 2)
    if code & Z2:
        z = z + 2 - 4 * (z // 2)
    if code & X:
        x = 1 - x
    if code & Y:
        t = 1 - t
    if other_core:
        c = 1 - c
    return z * 4 + x * 2 + c, t


def greet():
    barrier = pltpu.get_barrier_semaphore()
    for dim in DIMS:
        pl.semaphore_signal(barrier, inc=1, device_id=place(dim), device_id_type=MESH)
    pl.semaphore_signal(barrier, inc=1, device_id=place(0, True), device_id_type=MESH)
    pl.semaphore_wait(barrier, 5)


def bits(code):
    return bin(code).count("1")


def top_of(order, code):
    return max([order.index(k) for k in DIMS if code & k], default=-1)


def dot(a, b):
    return jnp.dot(a, b, preferred_element_type=F32)


def dot_nt(a, b):
    return lax.dot_general(a, b, (((1,), (1,)), ((), ())), preferred_element_type=F32)


def normed(v):
    centred = v - jnp.mean(v, axis=-1, keepdims=True)
    r = lax.rsqrt(jnp.mean(centred * centred, axis=-1, keepdims=True) + 1e-05)
    return centred * r, r


def norm_back(e, xhat, r, gain):
    eg = e * gain
    return r * (eg - jnp.mean(eg, axis=-1, keepdims=True) - xhat * jnp.mean(eg * xhat, axis=-1, keepdims=True))


def column_of(row):
    wide = jnp.broadcast_to(row.astype(F32), (128, row.shape[1]))
    return jnp.transpose(wide).astype(jnp.int32)


GATHER_ORDERS = ((ORDERS[0], ORDERS[1]),) * 3
REDUCE_ORDERS = ((ORDERS[0], ORDERS[1]),) * 3
SLOTS = {}
for _order in ORDERS:
    SLOTS[_order] = {}
    for _at, _dim in enumerate(_order):
        for _code in range(16):
            if top_of(_order, _code) < _at:
                SLOTS[_order][_code, _dim] = len(SLOTS[_order])
RISING = sorted(range(1, 16), key=bits)
FALLING = sorted(range(16), key=lambda code: -bits(code))


def cut_columns(orders, cols):
    width = cols // len(orders)
    return [(order, pl.ds(at * width, width)) for at, order in enumerate(orders)]


class Links:
    def __init__(self, piece, w, gd, from_core, from_chip, share, sems):
        self.piece, self.w, self.gd = piece, w, gd
        self.from_core, self.from_chip, self.share = from_core, from_chip, share
        (
            self.asend, self.arecv, self.acsend, self.acrecv,
            self.rsend, self.rrecv, self.rcsend, self.rcrecv, self.own,
        ) = sems
        _, self.rows, self.cols = piece.shape
        self.groups = piece.shape[0]

    def rows_at(self, d):
        return pl.ds(pl.multiple_of(d * self.rows, self.rows), self.rows)

    def own_copy(self):
        d, t = place(0)
        return [
            pltpu.make_async_copy(self.piece.at[g], self.w.at[g, t, self.rows_at(d)], self.own.at[g])
            for g in range(self.groups)
        ]

    def weight_move(self, g, part, code, dim):
        pd, pt = place(code)
        span = cut_columns(GATHER_ORDERS[g], self.cols)[part][1]
        target = self.w.at[g, pt, self.rows_at(pd), span]
        return pltpu.make_async_remote_copy(
            self.piece.at[g, :, span] if code == 0 else target,
            target,
            self.asend.at[g, part, code ^ dim],
            self.arecv.at[g, part, code ^ dim],
            device_id=place(dim),
            device_id_type=MESH,
        )

    def weight_core_move(self, g, code, mine=True):
        pd, pt = place(code, not mine)
        target = self.w.at[g, pt, self.rows_at(pd)]
        return pltpu.make_async_remote_copy(
            self.piece.at[g] if code == 0 and mine else target,
            target,
            self.acsend.at[g, code],
            self.acrecv.at[g, code],
            device_id=place(0, True),
            device_id_type=MESH,
        )

    def weight_forward(self, g, code):
        for part, order in enumerate(GATHER_ORDERS[g]):
            at = top_of(order, code)
            if code:
                self.weight_arrival(g, part, code, order[at]).wait_recv()
            for dim in order[at + 1 :]:
                self.weight_move(g, part, code, dim).start()
        self.weight_core_move(g, code).start()

    def weight_arrival(self, g, part, code, dim):
        pd, pt = place(code)
        span = cut_columns(GATHER_ORDERS[g], self.cols)[part][1]
        target = self.w.at[g, pt, self.rows_at(pd), span]
        return pltpu.make_async_remote_copy(
            target, target, self.asend.at[g, part, code], self.arecv.at[g, part, code],
            device_id=place(dim), device_id_type=MESH,
        )

    def weights_complete(self, g):
        for code in range(16):
            self.weight_core_move(g, code, False).wait_recv()

    def weights_sent(self, g):
        for part, order in enumerate(GATHER_ORDERS[g]):
            for code in range(16):
                for dim in order[top_of(order, code) + 1 :]:
                    self.weight_move(g, part, code, dim).wait_send()
        for code in range(16):
            self.weight_core_move(g, code).wait_send()

    def grad(self, g, code, core=False, span=None):
        pd, pt = place(code, core)
        where = (pt, self.rows_at(pd)) if span is None else (pt, self.rows_at(pd), span)
        return (self.gd, where) if g == 2 else (self.w, (g,) + where)

    def grad_core_move(self, g, code):
        ref, where = self.grad(g, code, True)
        return pltpu.make_async_remote_copy(
            ref.at[where],
            self.from_core.at[g, code],
            self.rcsend.at[g, code],
            self.rcrecv.at[g, code],
            device_id=place(0, True),
            device_id_type=MESH,
        )

    def grad_move(self, g, part, code, dim, sending):
        order, span = cut_columns(REDUCE_ORDERS[g], self.cols)[part]
        ref, where = self.grad(g, code, span=span)
        slot = SLOTS[order][code ^ dim if sending else code, dim]
        return pltpu.make_async_remote_copy(
            ref.at[where],
            self.from_chip.at[g, slot, :, span],
            self.rsend.at[g, part, slot],
            self.rrecv.at[g, part, slot],
            device_id=place(dim),
            device_id_type=MESH,
        )

    def grads_to_core(self, g):
        for code in FALLING:
            self.grad_core_move(g, code).start()

    def grad_step(self, g, code):
        self.grad_core_move(g, code).wait_recv()
        for part, (order, span) in enumerate(cut_columns(REDUCE_ORDERS[g], self.cols)):
            at = top_of(order, code)
            ref, where = self.grad(g, code, span=span)
            value = ref[where].astype(F32) + self.from_core[g, code, :, span].astype(F32)
            for dim in reversed(order[at + 1 :]):
                self.grad_move(g, part, code, dim, False).wait_recv()
                value = value + self.from_chip[g, SLOTS[order][code, dim], :, span].astype(F32)
            if code == 0:
                self.share[g, :, span] = value
            else:
                ref[where] = value.astype(BF)
                self.grad_move(g, part, code, order[at], True).start()

    def grads_sent(self, g):
        for code in range(16):
            self.grad_core_move(g, code).wait_send()
            for part, order in enumerate(REDUCE_ORDERS[g]):
                if code:
                    self.grad_move(g, part, code, order[top_of(order, code)], True).wait_send()


def small_place(code):
    return place(code >> 1, bool(code & 1))


def looped(count, body, events=()):
    events = list(events)

    @pl.loop(0, count)
    def _(i):
        body(i)
        for at in range(count):
            mine = events[len(events) * at // count : len(events) * (at + 1) // count]
            if mine:

                @pl.when(i == at)
                def _():
                    for event in mine:
                        event()


def layer_kernel(
    shape,
    linked,
    big_ref, small_ref, bvis_ref, svis_ref, bcot_ref, scot_ref, w_ref, vec_ref, bias_ref,
    out_ref, back_ref, share, vshare,
    w, gd, from_core, from_chip, x, na, n1t, n2t, qkv, prob, prob_small, heads, mid, acc, act, slope, cot, cott,
    vecs, bias, vgrad, bgrad, small, small_abs, small_sum, small_in,
    asend, arecv, acsend, acrecv, rsend, rrecv, rcsend, rcrecv, own, p_sem, c_sem, o_sem, s_sem,
):
    nb, bl, ns, sl = shape
    feat, wide = w.shape[2:]
    cut = nb * bl
    tokens = cut + ns * sl
    half = feat // 2
    pairs = half // 128
    d, t = lax.axis_index("dp"), lax.axis_index("tensor")
    block = 128
    steps = tokens // block
    tiles = 2 * (wide // 256)
    per = tiles // 2
    small_rows = ns * sl
    spans = [(i, i * bl, bl) for i in range(nb)] + [(nb, cut, small_rows)]
    chunk = 512
    strips = feat // 256

    cloads = [
        pltpu.make_async_copy(bcot_ref.at[t * nb + i], cot.at[pl.ds(i * bl, bl)], c_sem.at[i]) for i in range(nb)
    ]
    cloads += [
        pltpu.make_async_copy(scot_ref.at[t * ns + i], cot.at[pl.ds(cut + i * sl, sl)], c_sem.at[nb + i])
        for i in range(ns)
    ]
    big_len, small_len = big_ref.shape[1], small_ref.shape[1]
    ploads = []
    for i in range(nb):
        for at in range(big_len // chunk):
            source = big_ref.at[t * nb + i, pl.ds(at * chunk, chunk)]
            ploads.append((i, at, source, chunk, (bvis_ref, t * nb + i, i * bl, bl)))
    for i in range(ns):
        ploads.append((nb + i, 0, small_ref.at[t * ns + i], small_len, (svis_ref, t * ns + i, cut + i * sl, sl)))

    def pload(at):
        _, _, source, length, _ = ploads[at]
        return [
            pltpu.make_async_copy(
                source.at[:, pl.ds(c * 256, 256)], act.at[at % 2 * strips + c, pl.ds(0, length)], p_sem.at[at, c]
            )
            for c in range(strips)
        ]

    for copy in pload(0):
        copy.start()
    for copy in cloads:
        copy.start()

    if linked:
        link = Links(
            w_ref, w, gd, from_core, from_chip, share, (asend, arecv, acsend, acrecv, rsend, rrecv, rcsend, rcrecv, own)
        )
        owns = link.own_copy()
        for copy in owns:
            copy.start()
        small[0] = vec_ref[...]
        greet()
    else:
        wloads = [
            [pltpu.make_async_copy(w_ref.at[g, k], w.at[g, k], acsend.at[g, k]) for k in range(2)] for g in range(3)
        ]
        for copy in sum(wloads, []):
            copy.start()

    def small_move(k):
        return pltpu.make_async_remote_copy(
            small.at[pl.ds(0, 2**k)],
            small.at[pl.ds(2**k, 2**k)],
            s_sem.at[0, k],
            s_sem.at[1, k],
            device_id=small_place(2**k),
            device_id_type=MESH,
        )

    def small_step(k):
        def go():
            if k:
                small_move(k - 1).wait()
            if k < 5:
                small_move(k).start()

        return go

    def set_vectors():
        for code in range(32):
            pd, pt = small_place(code)
            small_abs[pt, pd] = small[code]
        vec_sum, bias_sum = 0.0, [0.0, 0.0]
        parts = feat // 48 if linked else 0
        for at in range(parts):
            for k in range(2):
                value = small_abs[k, at].astype(F32)
                if k == 0:
                    padded = jnp.concatenate([value, jnp.zeros((16, feat - 128), F32)], axis=1)
                    vec_sum = vec_sum + (pltpu.roll(padded, at * 48, 1) if at else padded)
                padded = jnp.concatenate([value[:8], jnp.zeros((8, wide - 128), F32)], axis=1)
                bias_sum[k] = bias_sum[k] + (pltpu.roll(padded, at * 96, 1) if at else padded)
        vecs[...] = vec_sum[:8]
        for k in range(2):
            bias[k] = bias_sum[k]

    def vec(i):
        return vecs[i : i + 1, :]

    def rows_of(i):
        return pl.ds(pl.multiple_of(i * block, block), block)

    def pick(at):
        def go():
            chip, part, _, length, (vis_ref, row, first_row, count) = ploads[at]
            for copy in pload(at):
                copy.wait()
            if at + 1 < len(ploads):
                for copy in pload(at + 1):
                    copy.start()
            column = column_of(vis_ref[row]) - part * length
            lane = lax.broadcasted_iota(jnp.int32, column.shape, 1)
            hot = jnp.concatenate([(column == lane + k * 128).astype(BF) for k in range(length // 128)], axis=1)
            rows = pl.ds(first_row, count)
            for c in range(strips):
                picked = dot(hot, act[at % 2 * strips + c, :length])
                span = pl.ds(c * 256, 256)
                if part:
                    picked = picked + x[rows, span].astype(F32)
                x[rows, span] = picked.astype(BF)

        return go

    picks = [pick(at) for at in range(len(ploads))]

    def weight_event(g, code):
        return lambda: link.weight_forward(g, code)

    if linked:
        order = sorted(
            [(bits(code) + AHEAD * g, g, n, code) for g in range(3) for n, code in enumerate([0] + RISING)]
        )
        sequence = [(g, weight_event(g, code)) for _, g, _, code in order]
        last = [max(i for i, (g, _) in enumerate(sequence) if g == k) for k in range(3)]
        weight_events = [[e for _, e in sequence[lo : hi + 1]] for lo, hi in zip([0] + [i + 1 for i in last], last)]
        mixed = [e for e in weight_events[0][:1]]
        queue = weight_events[0][1:]
        smalls = [small_step(k) for k in range(6)]
        mixed += smalls[:1]
        smalls = smalls[1:]
        work = list(picks)
        while queue or smalls or work:
            if smalls:
                mixed.append(smalls.pop(0))
            if queue:
                mixed.append(queue.pop(0))
            if work:
                mixed.append(work.pop(0))
        for event in mixed:
            event()
        set_vectors()
    else:
        weight_events = [[], [], []]
        for event in picks:
            event()
        vecs[...] = vec_ref[...]
        bias[...] = bias_ref[...]

    def weights_ready(g):
        if linked:
            owns[g].wait()
            link.weights_complete(g)
        else:
            for copy in wloads[g]:
                copy.wait()

    def norm_one(i):
        xhat, r = normed(x[rows_of(i), :].astype(F32))
        value = xhat * vec(0) + vec(1)
        na[rows_of(i), :] = value.astype(BF)
        n1t[:, rows_of(i)] = jnp.transpose(value).astype(BF)

    looped(steps, norm_one)
    weights_ready(0)
    events = weight_events[1]
    lot = len(events) // 3

    def make_qkv(i):
        k, c = i // 3, i % 3
        span = pl.ds(pl.multiple_of(c * half, half), half)
        qkv[k, :, span] = dot(na[...], w[0, k, :, span]).astype(BF)

    looped(6, make_qkv, events[:lot])

    lane = lax.broadcasted_iota(jnp.int32, (1, 128), 1)
    first = lane < HD
    zero = jnp.zeros((), BF)

    def softmax(scores):
        e = jnp.exp(scores - jnp.max(scores, axis=-1, keepdims=True))
        return e / jnp.sum(e, axis=-1, keepdims=True)

    same = (
        lax.broadcasted_iota(jnp.int32, (small_rows, small_rows), 0) // sl
        == lax.broadcasted_iota(jnp.int32, (small_rows, small_rows), 1) // sl
    )

    def pair_spans(pair):
        k, j = pair // pairs, pair % pairs
        return k, [pl.ds(pl.multiple_of(c * half + j * 128, 128), 128) for c in range(3)]

    def attention(pair):
        k, lanes = pair_spans(pair)
        for i, start, count in spans:
            rows = pl.ds(start, count)
            q, key, value = (qkv[k, rows, lanes[c]] for c in range(3))
            mixed = []
            for h in range(2):
                q_head = jnp.where(first if h == 0 else ~first, q, zero)
                scores = dot_nt(q_head, key) * HD ** (-0.5)
                if i == nb:
                    scores = jnp.where(same, scores, -jnp.inf)
                p = softmax(scores).astype(BF)
                if i == nb:
                    prob_small[pair, h] = p
                else:
                    prob[pair, i, h] = p
                mixed.append(dot(p, value))
            heads[rows, pl.ds(pl.multiple_of(pair * 128, 128), 128)] = jnp.where(first, mixed[0], mixed[1]).astype(BF)

    looped(2 * pairs, attention, events[lot:])

    out_span = pl.ds(3 * half, half)

    def project(i):
        span = pl.ds(pl.multiple_of(i * 256, 256), 256)
        mid[:, span] = dot_nt(heads[:, :half], w[0, 0, span, out_span]) + dot_nt(heads[:, half:], w[0, 1, span, out_span])

    looped(feat // 256, project)

    def norm_two(i):
        middle = x[rows_of(i), :].astype(F32) + mid[rows_of(i), :] + vec(4)
        mid[rows_of(i), :] = middle
        xhat, r = normed(middle)
        value = xhat * vec(2) + vec(3)
        na[rows_of(i), :] = value.astype(BF)
        n2t[:, rows_of(i)] = jnp.transpose(value).astype(BF)
        acc[rows_of(i), :] = middle + vec(5)

    looped(steps, norm_two)
    for copy in cloads:
        copy.wait()

    def turn_cot(i):
        cott[:, rows_of(i)] = jnp.transpose(cot[rows_of(i), :].astype(F32)).astype(BF)

    looped(steps, turn_cot)
    weights_ready(1)
    events = weight_events[2]
    lot = len(events) * 2 // 3

    def tile_of(i):
        return i // per, pl.ds(pl.multiple_of((i % per) * 256, 256), 256)

    def up(i):
        k, span = tile_of(i)
        pre = dot(na[...], w[1, k, :, span]) + bias[k, 6:7, span]
        cdf = 0.5 * (1.0 + lax.erf(pre * 0.7071067811865476))
        act[i] = (pre * cdf).astype(BF)
        slope[i] = (cdf + pre * jnp.exp(-0.5 * pre * pre) * 0.3989422804014327).astype(BF)

    looped(tiles, up, events[:lot])

    def grad_down(i):
        k, span = tile_of(i)
        gd[k, :, span] = dot(cott[...], act[i]).astype(BF)

    looped(tiles, grad_down, events[lot:])
    if linked:
        link.grads_to_core(2)
    weights_ready(2)

    def down(i):
        k, span = tile_of(i)
        acc[...] += dot_nt(act[i], w[2, k, :, span])

    looped(tiles, down)
    na[...] = acc[...].astype(BF)

    def row_moves(kind, start, count, n):
        target = (out_ref if kind == 0 else back_ref).at[t, pl.ds(start, count)] if linked else (
            out_ref if kind == 0 else back_ref
        ).at[pl.ds(start, count)]
        source = (na if kind == 0 else cot).at[pl.ds(start, count)]
        near = pltpu.make_async_copy(source, target, o_sem.at[0, kind, n])
        if not linked:
            return [near], None
        far = pltpu.make_async_remote_copy(
            source, target, o_sem.at[1, kind, n], o_sem.at[2, kind, n], device_id=place(Y), device_id_type=MESH
        )
        return [near, far], far

    for move in row_moves(0, 0, tokens, 0)[0]:
        move.start()

    acc[...] = jnp.zeros_like(acc)
    if linked:
        for g in range(3):
            link.weights_sent(g)

    def grad_events(g, codes):
        if not linked:
            return []
        return [functools.partial(link.grad_step, g, code) for code in codes]

    def back_up(i):
        k, span = tile_of(i)
        back = (slope[i].astype(F32) * dot(cot[...], w[2, k, :, span])).astype(BF)
        bgrad[k, 6:7, span] = jnp.sum(back.astype(F32), axis=0, keepdims=True)
        acc[...] += dot_nt(back, w[1, k, :, span])
        w[1, k, :, span] = dot(n2t[...], back).astype(BF)

    bgrad[...] = jnp.zeros_like(bgrad)
    looped(tiles, back_up, grad_events(2, FALLING[:8]))
    if linked:
        link.grads_to_core(1)

    vgrad[...] = jnp.zeros_like(vgrad)

    def norm_two_back(i):
        e = acc[rows_of(i), :]
        xhat, r = normed(mid[rows_of(i), :])
        back_out = cot[rows_of(i), :].astype(F32)
        back_middle = back_out + norm_back(e, xhat, r, vec(2))
        acc[rows_of(i), :] = back_middle
        cot[rows_of(i), :] = back_middle.astype(BF)
        n2t[:, rows_of(i)] = jnp.transpose(back_middle).astype(BF)
        vgrad[2:3, :] += jnp.sum(e * xhat, axis=0, keepdims=True)
        vgrad[3:4, :] += jnp.sum(e, axis=0, keepdims=True)
        vgrad[4:5, :] += jnp.sum(back_middle, axis=0, keepdims=True)
        vgrad[5:6, :] += jnp.sum(back_out, axis=0, keepdims=True)

    looped(steps, norm_two_back, grad_events(2, FALLING[8:12]))

    dheads = heads
    for k in range(2):
        here = pl.ds(k * half, half)
        grad = dot(n2t[...], heads[:, here]).astype(BF)
        dheads[:, here] = dot(cot[...], w[0, k, :, out_span]).astype(BF)
        w[0, k, :, out_span] = grad

    def attention_back(i, rows, pair):
        k, lanes = pair_spans(pair)
        q, key, value = (qkv[k, rows, lanes[c]] for c in range(3))
        dh = dheads[rows, pl.ds(pl.multiple_of(pair * 128, 128), 128)]
        dh_t = jnp.transpose(dh.astype(F32)).astype(BF)
        q_t = jnp.transpose(q.astype(F32)).astype(BF)
        dq, dk_t, dv_t = [], [], []
        for h in range(2):
            p = prob_small[pair, h] if i == nb else prob[pair, i, h]
            dh_head = jnp.where(first if h == 0 else ~first, dh, zero)
            dp = dot_nt(dh_head, value)
            pf = p.astype(F32)
            ds = (pf * (dp - jnp.sum(pf * dp, axis=-1, keepdims=True))).astype(BF)
            dq.append(dot(ds, key))
            dk_t.append(dot(q_t[h * HD : (h + 1) * HD], ds))
            dv_t.append(dot(dh_t[h * HD : (h + 1) * HD], p))
        scale = HD ** (-0.5)
        qkv[k, rows, lanes[0]] = (jnp.where(first, dq[0], dq[1]) * scale).astype(BF)
        qkv[k, rows, lanes[1]] = jnp.transpose(jnp.concatenate(dk_t, axis=0) * scale).astype(BF)
        qkv[k, rows, lanes[2]] = jnp.transpose(jnp.concatenate(dv_t, axis=0)).astype(BF)

    during = [
        grad_events(2, FALLING[12:]) + grad_events(1, FALLING[:2]),
        grad_events(1, FALLING[2:8]),
        grad_events(1, FALLING[8:11]),
    ]
    for at, (i, start, count) in enumerate(spans):
        rows = pl.ds(start, count)
        looped(2 * pairs, lambda pair: attention_back(i, rows, pair), during[min(at, 2)] if at < 3 else [])

        def back_first(n):
            span = pl.ds(pl.multiple_of(n * 256, 256), 256)
            both = pl.ds(0, 3 * half)
            mid[rows, span] = dot_nt(qkv[0, rows, both], w[0, 0, span, both]) + dot_nt(
                qkv[1, rows, both], w[0, 1, span, both]
            )

        looped(feat // 256, back_first)

        def norm_one_back(n):
            here = pl.ds(pl.multiple_of(start + n * block, block), block)
            e = mid[here, :]
            xhat, r = normed(x[here, :].astype(F32))
            back_in = acc[here, :] + norm_back(e, xhat, r, vec(0))
            cot[here, :] = back_in.astype(BF)
            vgrad[0:1, :] += jnp.sum(e * xhat, axis=0, keepdims=True)
            vgrad[1:2, :] += jnp.sum(e, axis=0, keepdims=True)

        looped(count // block, norm_one_back)
        for move in row_moves(1, start, count, at)[0]:
            move.start()

    def grad_qkv(i):
        k, c = i // 3, i % 3
        span = pl.ds(pl.multiple_of(c * half, half), half)
        w[0, k, :, span] = dot(n1t[...], qkv[k, :, span]).astype(BF)

    looped(6, grad_qkv, grad_events(1, FALLING[11:]))

    def cut_small():
        low = lax.broadcasted_iota(jnp.int32, (8, 128), 1)
        row = lax.broadcasted_iota(jnp.int32, (8, 128), 0)
        for at in range(feat // 48):
            value = vgrad[...]
            if at:
                value = pltpu.roll(value, feat - at * 48, 1)
            value = jnp.where((low < 48) & (row < 6), value[:, :128], 0.0)
            for k in range(2):
                more = bgrad[k]
                if at:
                    more = pltpu.roll(more, wide - at * 96, 1)
                small_abs_sum[k, at] = value + jnp.where((low < 96) & (row == 6), more[:, :128], 0.0)
        for code in range(32):
            pd, pt = small_place(code)
            small_sum[code] = small_abs_sum[pt, pd]

    small_abs_sum = small_in[1]
    small_got = small_in[0]

    def sum_move(k):
        return pltpu.make_async_remote_copy(
            small_sum.at[pl.ds(2**k, 2**k)],
            small_got.at[pl.ds(2**k, 2**k)],
            s_sem.at[2, k],
            s_sem.at[3, k],
            device_id=small_place(2**k),
            device_id_type=MESH,
        )

    def sum_step(k):
        def go():
            if k < 4:
                sum_move(k + 1).wait()
                here = pl.ds(0, 2 ** (k + 1))
                small_sum[here] = small_sum[here] + small_got[pl.ds(2 ** (k + 1), 2 ** (k + 1))]
            if k >= 0:
                sum_move(k).start()

        return go

    if linked:
        link.grads_to_core(0)
        cut_small()
        last_events = grad_events(0, FALLING)
        sums = [sum_step(k) for k in range(4, -2, -1)]
        while last_events or sums:
            if sums:
                sums.pop(0)()
            for event in last_events[:2]:
                event()
            last_events = last_events[2:]
        vshare[...] = small_sum[0]
        for g in range(3):
            link.grads_sent(g)
    else:
        saves = []
        for g in range(3):
            for k in range(2):
                source = gd.at[k] if g == 2 else w.at[g, k]
                saves.append(pltpu.make_async_copy(source, share.at[g, k], acsend.at[g, k]))
        for copy in saves:
            copy.start()
        for copy in saves:
            copy.wait()
        vshare[pl.ds(0, 8), pl.ds(0, feat)] = vgrad[...]
        for k in range(2):
            vshare[pl.ds(8 + 8 * k, 8), :] = bgrad[k]
    for move in row_moves(0, 0, tokens, 0)[0]:
        move.wait()
    for at, (i, start, count) in enumerate(spans):
        near, far = row_moves(1, start, count, at)[0][0], row_moves(1, start, count, at)[1]
        near.wait()
        if linked:
            far.wait()


AHEAD = 3
VLIM = 60


def run_layer(linked, big, small, bvis, svis, bcot, scot, w, vectors, bias, parts, wide):
    nb, bl = bvis.shape[0] // parts, bvis.shape[2]
    ns, sl = svis.shape[0] // parts, svis.shape[2]
    tokens = nb * bl + ns * sl
    feat = big.shape[2]
    tiles = 2 * (wide // 256)
    pairs = feat // 128
    rows = w.shape[1] if linked else 48
    vm, hbm = pl.BlockSpec(memory_space=pltpu.VMEM), pl.BlockSpec(memory_space=pl.ANY)
    pair = (2, tokens, feat) if linked else (tokens, feat)
    dma = pltpu.SemaphoreType.DMA
    link = (lambda *shape: pltpu.VMEM(shape, BF)) if linked else (lambda *shape: pltpu.VMEM((16, 128), BF))
    loads = nb * (big.shape[1] // 512) + ns
    return pl.pallas_call(
        functools.partial(layer_kernel, (nb, bl, ns, sl), linked),
        out_shape=(
            jax.ShapeDtypeStruct(pair, BF),
            jax.ShapeDtypeStruct(pair, BF),
            jax.ShapeDtypeStruct((3, rows, wide) if linked else w.shape, F32 if linked else BF),
            jax.ShapeDtypeStruct((8, 128) if linked else (24, wide), F32),
        ),
        in_specs=[hbm, hbm, vm, vm, hbm, hbm, hbm, vm, vm],
        out_specs=(hbm, hbm, vm if linked else hbm, vm),
        scratch_shapes=[
            pltpu.VMEM((3, 2, feat, wide), BF),
            pltpu.VMEM((2, feat, wide), BF),
            link(3, 16, rows, wide),
            link(3, 15, rows, wide),
            pltpu.VMEM((tokens, feat), BF),
            pltpu.VMEM((tokens, feat), BF),
            pltpu.VMEM((feat, tokens), BF),
            pltpu.VMEM((feat, tokens), BF),
            pltpu.VMEM((2, tokens, 3 * feat // 2), BF),
            pltpu.VMEM((pairs, nb, 2, bl, bl), BF),
            pltpu.VMEM((pairs, 2, ns * sl, ns * sl), BF),
            pltpu.VMEM((tokens, feat), BF),
            pltpu.VMEM((tokens, feat), F32),
            pltpu.VMEM((tokens, feat), F32),
            pltpu.VMEM((tiles, tokens, 256), BF),
            pltpu.VMEM((tiles, tokens, 256), BF),
            pltpu.VMEM((tokens, feat), BF),
            pltpu.VMEM((feat, tokens), BF),
            pltpu.VMEM((8, feat), F32),
            pltpu.VMEM((2, 8, wide), F32),
            pltpu.VMEM((8, feat), F32),
            pltpu.VMEM((2, 8, wide), F32),
            pltpu.VMEM((32, 16, 128), BF),
            pltpu.VMEM((2, 16, 16, 128), BF),
            pltpu.VMEM((32, 8, 128), F32),
            [pltpu.VMEM((32, 8, 128), F32), pltpu.VMEM((2, 16, 8, 128), F32)],
            dma((3, 2, 16)),
            dma((3, 2, 16)),
            dma((3, 16)),
            dma((3, 16)),
            dma((3, 2, 15)),
            dma((3, 2, 15)),
            dma((3, 16)),
            dma((3, 16)),
            dma((3,)),
            dma((loads, feat // 256)),
            dma((nb + ns,)),
            dma((3, 2, nb + 1)),
            dma((4, 5)),
        ],
        compiler_params=pltpu.CompilerParams(
            collective_id=0 if linked else None, has_side_effects=linked, vmem_limit_bytes=VLIM * MIB
        ),
        name="layer",
    )(big, small, bvis, svis, bcot, scot, w, vectors, bias)


def scatter_kernel(bvis_ref, svis_ref, brow_ref, srow_ref, big_ref, small_ref):
    def spread(vis, rows, length):
        hot = lax.broadcasted_iota(jnp.int32, (length, vis.shape[1]), 0) == vis
        return dot(hot.astype(BF), rows)

    big_ref[...] = spread(bvis_ref[...], brow_ref[...], big_ref.shape[0])
    small_ref[...] = spread(svis_ref[...], srow_ref[...], small_ref.shape[0])


def scatter_rows(bvis, svis, rows, big_len, small_len):
    parts = rows.shape[0]
    nb, _, bl = bvis.shape
    ns, _, sl = svis.shape
    feat = rows.shape[2]
    share = nb // parts
    first_small = share * bl // sl
    return pl.pallas_call(
        scatter_kernel,
        grid=(nb,),
        out_shape=(
            jax.ShapeDtypeStruct((nb, big_len, feat), F32),
            jax.ShapeDtypeStruct((ns, small_len, feat), F32),
        ),
        in_specs=[
            pl.BlockSpec((None, 1, bl), lambda i: (i, 0, 0)),
            pl.BlockSpec((None, 1, sl), lambda i: (i, 0, 0)),
            pl.BlockSpec((None, bl, feat), lambda i: (i // share, i % share, 0)),
            pl.BlockSpec((None, sl, feat), lambda i: (i // share, first_small + i % share, 0)),
        ],
        out_specs=(
            pl.BlockSpec((None, big_len, feat), lambda i: (i, 0, 0)),
            pl.BlockSpec((None, small_len, feat), lambda i: (i, 0, 0)),
        ),
        compiler_params=pltpu.CompilerParams(vmem_limit_bytes=40 * MIB),
        name="scatter_rows",
    )(bvis, svis, rows, rows)


def adam_step(weight, moment_one, moment_two, gradient, step_rate, decay_rate):
    moment_one = 0.9 * moment_one + 0.1 * gradient
    moment_two = 0.999 * moment_two + 0.001 * gradient * gradient
    fixed_one = moment_one / (1.0 - 0.9**STEP_NUMBER)
    fixed_two = moment_two / (1.0 - 0.999**STEP_NUMBER)
    update = fixed_one / (jnp.sqrt(fixed_two) + 1e-08) + decay_rate * weight
    return (weight - step_rate * update, moment_one, moment_two)


def on_device(
    special,
    big_patches, small_patches, big_visible, small_visible, big_cot, small_cot,
    qkv_weight, qkv_first, qkv_second, out_weight, out_first, out_second,
    up_weight, up_first, up_second, down_weight, down_first, down_second,
    up_bias, up_bias_first, up_bias_second, norm_vectors, norm_first, norm_second,
):
    rows, half = out_weight.shape
    wide = up_weight.shape[1]
    feat = big_patches.shape[2]
    parts = feat // half
    piece = jnp.stack(
        [
            jnp.concatenate([qkv_weight.reshape(rows, 3 * half), out_weight], axis=1).astype(BF),
            up_weight.astype(BF),
            down_weight.astype(BF),
        ]
    )
    bvis, svis = big_visible[:, None, :], small_visible[:, None, :]
    chips = (big_patches, small_patches, bvis, svis, big_cot, small_cot)
    if special:
        few = jnp.concatenate(
            [
                jnp.pad(norm_vectors, ((0, 0), (0, 128 - norm_vectors.shape[1]))),
                jnp.pad(up_bias, ((0, 9), (0, 128 - up_bias.shape[1]))),
            ]
        ).astype(BF)
        out_both, back_both, share, vshare = run_layer(True, *chips, piece, few, few, parts, wide)
        norm_share = vshare[:6, : norm_vectors.shape[1]]
        bias_share = vshare[6:7, : up_bias.shape[1]]
    else:
        w = lax.all_gather(lax.all_gather(piece, "dp", axis=1, tiled=True), "tensor", axis=1)
        vectors = lax.all_gather(norm_vectors.astype(BF), "dp", axis=1, tiled=True).astype(F32)
        bias = lax.all_gather(up_bias.astype(BF), "dp", axis=1, tiled=True)
        bias = lax.all_gather(bias, "tensor", axis=0).astype(F32)
        out_rows, back_rows, grads, few = run_layer(
            False, *chips, w, jnp.pad(vectors, ((0, 2), (0, 0))), jnp.pad(bias, ((0, 0), (6, 1), (0, 0))), parts, wide
        )
        share = lax.psum_scatter(grads, "tensor", scatter_dimension=1)
        share = lax.psum_scatter(share, "dp", scatter_dimension=1, tiled=True).astype(F32)
        both = lax.all_gather(jnp.stack([out_rows, back_rows]), "tensor", axis=1)
        out_both, back_both = both[0], both[1]
        norm_share = lax.psum_scatter(lax.psum(few[:6, :feat], "tensor"), "dp", scatter_dimension=1, tiled=True)
        bias_share = lax.psum_scatter(few[14::8], "tensor", scatter_dimension=0, tiled=True)
        bias_share = lax.psum_scatter(bias_share, "dp", scatter_dimension=1, tiled=True)
    big_count, big_len = big_visible.shape
    small_count, small_len = small_visible.shape
    cut = big_count // parts * big_len
    big_out = out_both[:, :cut].reshape(big_count, big_len, feat)
    small_out = out_both[:, cut:].reshape(small_count, small_len, feat)
    big_grad, small_grad = scatter_rows(bvis, svis, back_both, big_patches.shape[1], small_patches.shape[1])

    qkv_share = share[0, :, : 3 * half].reshape(rows, 3, half)
    new = []
    for at, (weight, one, two, gradient) in enumerate(
        (
            (qkv_weight, qkv_first, qkv_second, qkv_share),
            (out_weight, out_first, out_second, share[0, :, 3 * half :]),
            (up_weight, up_first, up_second, share[1]),
            (down_weight, down_first, down_second, share[2]),
            (up_bias, up_bias_first, up_bias_second, bias_share),
            (norm_vectors, norm_first, norm_second, norm_share),
        )
    ):
        new.extend(adam_step(weight, one, two, gradient, LEARN_RATES[at], DECAYS[at]))
    return (big_out, small_out, big_grad, small_grad, *new)


def solution(mesh):
    special = mesh.shape["dp"] == 16 and mesh.shape["tensor"] == 2
    chips = P("dp", None, None)
    matrix, qkv = P("dp", "tensor"), P("dp", None, "tensor")
    states = (qkv,) * 3 + (matrix,) * 9 + (P("tensor", "dp"),) * 3 + (P(None, "dp"),) * 3
    return jax.shard_map(
        functools.partial(on_device, special),
        mesh=mesh,
        in_specs=(chips, chips, P("dp", None), P("dp", None), chips, chips) + states,
        out_specs=(chips,) * 4 + states,
        check_vma=False,
    )
```

```python
import functools

import jax
import jax.numpy as jnp
from jax import lax
from jax.experimental import pallas as pl
from jax.experimental.pallas import tpu as pltpu
from jax.sharding import PartitionSpec as P

HD = 64
STEP_NUMBER = 10
BF, F32 = jnp.bfloat16, jnp.float32
MESH = pl.DeviceIdType.MESH
MIB = 2**20

LEARN_RATES = (0.03, 0.1, 0.03, 0.015, 0.2, 0.2)
DECAYS = (0.05, 0.05, 0.05, 0.05, 0.0, 0.0)

Z1, Z2, X, Y = 1, 2, 4, 8
DIMS = (Z1, Z2, X, Y)
def place(code, other_core=False):
    d, t = lax.axis_index("dp"), lax.axis_index("tensor")
    z, x, c = lax.div(d, 4), lax.rem(lax.div(d, 2), 2), lax.rem(d, 2)
    if code & Z1:
        z = z + 1 - 2 * lax.rem(z, 2)
    if code & Z2:
        z = z + 2 - 4 * lax.div(z, 2)
    if code & X:
        x = 1 - x
    if code & Y:
        t = 1 - t
    if other_core:
        c = 1 - c
    return z * 4 + x * 2 + c, t


def greet(place):
    barrier = pltpu.get_barrier_semaphore()
    for dim in DIMS:
        pl.semaphore_signal(barrier, inc=1, device_id=place(dim), device_id_type=MESH)
    pl.semaphore_signal(barrier, inc=1, device_id=place(0, True), device_id_type=MESH)
    pl.semaphore_wait(barrier, 5)


def bits(code):
    return bin(code).count("1")


def top_of(order, code):
    return max([order.index(k) for k in DIMS if code & k], default=-1)


def dot(a, b):
    return jnp.dot(a, b, preferred_element_type=F32)


def dot_nt(a, b):
    return lax.dot_general(a, b, (((1,), (1,)), ((), ())), preferred_element_type=F32)


def dot_tn(a, b):
    return lax.dot_general(a, b, (((0,), (0,)), ((), ())), preferred_element_type=F32)


def normed(v):
    centred = v - jnp.mean(v, axis=-1, keepdims=True)
    r = lax.rsqrt(jnp.mean(centred * centred, axis=-1, keepdims=True) + 1e-05)
    return centred * r, r


def norm_back(e, xhat, r, gain):
    eg = e * gain
    return r * (eg - jnp.mean(eg, axis=-1, keepdims=True) - xhat * jnp.mean(eg * xhat, axis=-1, keepdims=True))


def column_of(row):
    wide = jnp.broadcast_to(row.astype(F32), (128, row.shape[1]))
    return jnp.transpose(wide).astype(jnp.int32)


T, PP, Q, R = (Z2, Z1, X, Y), (Z2, Z1, Y, X), (Z2, Y, X, Z1), (Y, Z2, X, Z1)
GATHER_ORDERS = ((T, PP), (T, PP), (T, PP))
AHEAD = 3
DOWN, UP, OUT, QKV = range(4)
SUMS = (
    (2, ((PP, 0, 768), (R, 768, 768))),
    (1, ((PP, 0, 768), (R, 768, 768))),
    (0, ((PP, 1152, 256), (R, 1408, 128))),
    (0, ((PP, 0, 512), (R, 512, 640))),
)
SLOTS = {}
for _order in (T, PP, Q, R):
    SLOTS[_order] = {}
    for _at, _dim in enumerate(_order):
        for _code in range(16):
            if top_of(_order, _code) < _at:
                SLOTS[_order][_code, _dim] = len(SLOTS[_order])
RISING = sorted(range(1, 16), key=bits)
FALLING = sorted(range(16), key=lambda code: -bits(code))


def cut_columns(orders, cols):
    width = cols // len(orders)
    return [(order, pl.ds(at * width, width)) for at, order in enumerate(orders)]


class Links:
    def __init__(self, piece, w, gd, from_core, from_chip, share, sems):
        self.piece, self.w, self.gd = piece, w, gd
        self.from_core, self.from_chip, self.share = from_core, from_chip, share
        (
            self.asend, self.arecv, self.acsend, self.acrecv,
            self.rsend, self.rrecv, self.rcsend, self.rcrecv, self.own,
        ) = sems
        _, self.rows, self.cols = piece.shape
        self.groups = piece.shape[0]

        self.places = {(code, core): place(code, core) for code in range(16) for core in (False, True)}
        self.spans = {at: pl.ds(pl.multiple_of(d * self.rows, self.rows), self.rows) for at, (d, _) in self.places.items()}

    def place(self, code, core=False):
        return self.places[code, core]

    def at(self, code, core=False):
        return self.places[code, core][1], self.spans[code, core]

    def own_copy(self):
        return [
            pltpu.make_async_copy(self.piece.at[g], self.w.at[(g,) + self.at(0)], self.own.at[g])
            for g in range(self.groups)
        ]

    def weight_move(self, g, part, code, dim):
        span = cut_columns(GATHER_ORDERS[g], self.cols)[part][1]
        target = self.w.at[(g,) + self.at(code) + (span,)]
        return pltpu.make_async_remote_copy(
            self.piece.at[g, :, span] if code == 0 else target,
            target,
            self.asend.at[g, part, code ^ dim],
            self.arecv.at[g, part, code ^ dim],
            device_id=self.place(dim),
            device_id_type=MESH,
        )

    def weight_core_move(self, g, code, mine=True):
        target = self.w.at[(g,) + self.at(code, not mine)]
        return pltpu.make_async_remote_copy(
            self.piece.at[g] if code == 0 and mine else target,
            target,
            self.acsend.at[g, code],
            self.acrecv.at[g, code],
            device_id=self.place(0, True),
            device_id_type=MESH,
        )

    def weight_forward(self, g, code):
        for part, order in enumerate(GATHER_ORDERS[g]):
            at = top_of(order, code)
            if code:
                self.weight_arrival(g, part, code, order[at]).wait_recv()
            for dim in order[at + 1 :]:
                self.weight_move(g, part, code, dim).start()
        self.weight_core_move(g, code).start()

    def weight_arrival(self, g, part, code, dim):
        span = cut_columns(GATHER_ORDERS[g], self.cols)[part][1]
        target = self.w.at[(g,) + self.at(code) + (span,)]
        return pltpu.make_async_remote_copy(
            target, target, self.asend.at[g, part, code], self.arecv.at[g, part, code],
            device_id=self.place(dim), device_id_type=MESH,
        )

    def weights_complete(self, g):
        for code in range(16):
            self.weight_core_move(g, code, False).wait_recv()

    def weights_sent(self, g):
        for part, order in enumerate(GATHER_ORDERS[g]):
            for code in range(16):
                for dim in order[top_of(order, code) + 1 :]:
                    self.weight_move(g, part, code, dim).wait_send()
        for code in range(16):
            self.weight_core_move(g, code).wait_send()

    def grad(self, n, code, core, start, width):
        g = SUMS[n][0]
        where = self.at(code, core) + (pl.ds(start, width),)
        return (self.gd, where) if g == 2 else (self.w, (g,) + where)

    def grad_core_move(self, n, code):
        g, parts = SUMS[n]
        start, width = parts[0][1], sum(part[2] for part in parts)
        ref, where = self.grad(n, code, True, start, width)
        return pltpu.make_async_remote_copy(
            ref.at[where],
            self.from_core.at[g, code, :, pl.ds(start, width)],
            self.rcsend.at[n, code],
            self.rcrecv.at[n, code],
            device_id=self.place(0, True),
            device_id_type=MESH,
        )

    def grad_move(self, n, part, code, dim, sending):
        g, parts = SUMS[n]
        order, start, width = parts[part]
        ref, where = self.grad(n, code, False, start, width)
        slot = SLOTS[order][code ^ dim if sending else code, dim]
        return pltpu.make_async_remote_copy(
            ref.at[where],
            self.from_chip.at[g, slot, :, pl.ds(start, width)],
            self.rsend.at[n, part, slot],
            self.rrecv.at[n, part, slot],
            device_id=self.place(dim),
            device_id_type=MESH,
        )

    def grads_to_core(self, n):
        for code in FALLING:
            self.grad_core_move(n, code).start()

    def grad_step(self, n, code):
        g, parts = SUMS[n]
        self.grad_core_move(n, code).wait_recv()
        for part, (order, start, width) in enumerate(parts):
            at = top_of(order, code)
            span = pl.ds(start, width)
            ref, where = self.grad(n, code, False, start, width)
            value = ref[where].astype(F32) + self.from_core[g, code, :, span].astype(F32)
            for dim in reversed(order[at + 1 :]):
                self.grad_move(n, part, code, dim, False).wait_recv()
                value = value + self.from_chip[g, SLOTS[order][code, dim], :, span].astype(F32)
            if code == 0:
                self.share[g, :, span] = value
            else:
                ref[where] = value.astype(BF)
                self.grad_move(n, part, code, order[at], True).start()

    def grads_sent(self, n):
        for code in range(16):
            self.grad_core_move(n, code).wait_send()
            for part, (order, _, _) in enumerate(SUMS[n][1]):
                if code:
                    self.grad_move(n, part, code, order[top_of(order, code)], True).wait_send()


def looped(count, body, events=()):
    events = list(events)

    @pl.loop(0, count)
    def _(i):
        body(i)
        for at in range(count):
            mine = events[len(events) * at // count : len(events) * (at + 1) // count]
            if mine:

                @pl.when(i == at)
                def _():
                    for event in mine:
                        event()


def layer_kernel(
    shape,
    linked,
    big_ref, small_ref, bvis_ref, svis_ref, bcot_ref, scot_ref, w_ref, vec_ref, bias_ref,
    out_ref, back_ref, share, vshare,
    w, gd, from_core, from_chip, x, n1, n2, qkv, prob, prob_small, heads, mid, acc, act, slope, cot, out_rows,
    vecs, bias, vgrad, bgrad, small, small_abs, small_sum, small_in,
    asend, arecv, acsend, acrecv, rsend, rrecv, rcsend, rcrecv, own, p_sem, c_sem, o_sem, s_sem,
):
    nb, bl, ns, sl = shape
    feat, wide = w.shape[2:]
    cut = nb * bl
    tokens = cut + ns * sl
    half = feat // 2
    pairs = half // 128
    d, t = lax.axis_index("dp"), lax.axis_index("tensor")
    block = 128
    steps = tokens // block
    tile = act.shape[2]
    tiles = act.shape[0]
    per = tiles // 2
    small_rows = ns * sl
    spans = [(i, i * bl, bl) for i in range(nb)] + [(nb, cut, small_rows)]
    chunk = 512
    strips = [(at, min(tile, feat - at)) for at in range(0, feat, tile)]

    cloads = [
        pltpu.make_async_copy(bcot_ref.at[t * nb + i], cot.at[pl.ds(i * bl, bl)], c_sem.at[i]) for i in range(nb)
    ]
    cloads += [
        pltpu.make_async_copy(scot_ref.at[t * ns + i], cot.at[pl.ds(cut + i * sl, sl)], c_sem.at[nb + i])
        for i in range(ns)
    ]
    big_len, small_len = big_ref.shape[1], small_ref.shape[1]
    ploads = []
    for i in range(nb):
        for at in range(big_len // chunk):
            source = big_ref.at[t * nb + i, pl.ds(at * chunk, chunk)]
            ploads.append((i, at, source, chunk, (bvis_ref, t * nb + i, i * bl, bl)))
    for i in range(ns):
        ploads.append((nb + i, 0, small_ref.at[t * ns + i], small_len, (svis_ref, t * ns + i, cut + i * sl, sl)))

    def pload(at):
        _, _, source, length, _ = ploads[at]
        return [
            pltpu.make_async_copy(
                source.at[:, pl.ds(start, width)],
                act.at[at % 2 * len(strips) + c, pl.ds(0, length), pl.ds(0, width)],
                p_sem.at[at, c],
            )
            for c, (start, width) in enumerate(strips)
        ]

    for copy in pload(0):
        copy.start()
    for copy in cloads:
        copy.start()

    if linked:
        link = Links(
            w_ref, w, gd, from_core, from_chip, share, (asend, arecv, acsend, acrecv, rsend, rrecv, rcsend, rcrecv, own)
        )
        owns = link.own_copy()
        for copy in owns:
            copy.start()

        def small_place(code):
            return link.place(code >> 1, bool(code & 1))

        small[0] = vec_ref[...]
        greet(link.place)
    else:
        wloads = [
            [pltpu.make_async_copy(w_ref.at[g, k], w.at[g, k], acsend.at[g, k]) for k in range(2)] for g in range(3)
        ]
        for copy in sum(wloads, []):
            copy.start()

    def small_move(k):
        return pltpu.make_async_remote_copy(
            small.at[pl.ds(0, 2**k)],
            small.at[pl.ds(2**k, 2**k)],
            s_sem.at[0, k],
            s_sem.at[1, k],
            device_id=small_place(2**k),
            device_id_type=MESH,
        )

    def small_step(k):
        def go():
            if k:
                small_move(k - 1).wait()
            if k < 5:
                small_move(k).start()

        return go

    def set_vectors():
        for code in range(32):
            pd, pt = small_place(code)
            small_abs[pt, pd] = small[code]
        vec_sum, bias_sum = 0.0, [0.0, 0.0]
        parts = feat // 48 if linked else 0
        for at in range(parts):
            for k in range(2):
                value = small_abs[k, at].astype(F32)
                if k == 0:
                    padded = jnp.concatenate([value, jnp.zeros((16, feat - 128), F32)], axis=1)
                    vec_sum = vec_sum + (pltpu.roll(padded, at * 48, 1) if at else padded)
                padded = jnp.concatenate([value[:8], jnp.zeros((8, wide - 128), F32)], axis=1)
                bias_sum[k] = bias_sum[k] + (pltpu.roll(padded, at * 96, 1) if at else padded)
        vecs[...] = vec_sum[:8]
        for k in range(2):
            bias[k] = bias_sum[k]

    def vec(i):
        return vecs[i : i + 1, :]

    def rows_of(i):
        return pl.ds(pl.multiple_of(i * block, block), block)

    def pick(at):
        def go():
            chip, part, _, length, (vis_ref, row, first_row, count) = ploads[at]
            for copy in pload(at):
                copy.wait()
            if at + 1 < len(ploads):
                for copy in pload(at + 1):
                    copy.start()
            column = column_of(vis_ref[row]) - part * length
            lane = lax.broadcasted_iota(jnp.int32, column.shape, 1)
            hot = jnp.concatenate([(column == lane + k * 128).astype(BF) for k in range(length // 128)], axis=1)
            rows = pl.ds(first_row, count)
            for c, (start, width) in enumerate(strips):
                picked = dot(hot, act[at % 2 * len(strips) + c, :length, :width])
                span = pl.ds(start, width)
                if part:
                    picked = picked + x[rows, span].astype(F32)
                x[rows, span] = picked.astype(BF)

        return go

    picks = [pick(at) for at in range(len(ploads))]

    def weight_event(g, code):
        return lambda: link.weight_forward(g, code)

    if linked:
        order = sorted(
            [(bits(code) + AHEAD * g, g, n, code) for g in range(3) for n, code in enumerate([0] + RISING)]
        )
        sequence = [(g, weight_event(g, code)) for _, g, _, code in order]
        last = [max(i for i, (g, _) in enumerate(sequence) if g == k) for k in range(3)]
        weight_events = [[e for _, e in sequence[lo : hi + 1]] for lo, hi in zip([0] + [i + 1 for i in last], last)]
        smalls = [small_step(k) for k in range(6)]
        mixed = [weight_events[0][0], smalls[0], picks[0], picks[1]] + weight_events[0][1:3] + [smalls[1], picks[2]]
        mixed += weight_events[0][3:5] + [picks[3], smalls[2]] + weight_events[0][5:8] + [picks[4], smalls[3]]
        mixed += weight_events[0][8:11] + picks[5:] + [smalls[4]] + weight_events[0][11:14] + [smalls[5]]
        mixed += weight_events[0][14:]
        for event in mixed:
            event()
        set_vectors()
    else:
        weight_events = [[], [], []]
        for event in picks:
            event()
        vecs[...] = vec_ref[...]
        bias[...] = bias_ref[...]

    def weights_ready(g):
        if linked:
            link.own_copy()[g].wait()
            link.weights_complete(g)
        else:
            for copy in wloads[g]:
                copy.wait()

    def norm_one(i):
        xhat, r = normed(x[rows_of(i), :].astype(F32))
        value = xhat * vec(0) + vec(1)
        n1[rows_of(i), :] = value.astype(BF)

    looped(steps, norm_one)
    weights_ready(0)
    events = weight_events[1]
    lot = len(events) // 3

    def make_qkv(i):
        k, c = i // 3, i % 3
        span = pl.ds(pl.multiple_of(c * half, half), half)
        qkv[k, :, span] = dot(n1[...], w[0, k, :, span]).astype(BF)

    looped(6, make_qkv, events[:lot])

    lane = lax.broadcasted_iota(jnp.int32, (1, 128), 1)
    first = lane < HD
    zero = jnp.zeros((), BF)

    def softmax(scores):
        e = jnp.exp(scores - jnp.max(scores, axis=-1, keepdims=True))
        return e / jnp.sum(e, axis=-1, keepdims=True)

    same = (
        lax.broadcasted_iota(jnp.int32, (small_rows, small_rows), 0) // sl
        == lax.broadcasted_iota(jnp.int32, (small_rows, small_rows), 1) // sl
    )

    def pair_spans(pair):
        k, j = pair // pairs, pair % pairs
        return k, [pl.ds(pl.multiple_of(c * half + j * 128, 128), 128) for c in range(3)]

    def attention(pair):
        k, lanes = pair_spans(pair)
        for i, start, count in spans:
            rows = pl.ds(start, count)
            q, key, value = (qkv[k, rows, lanes[c]] for c in range(3))
            mixed = []
            for h in range(2):
                q_head = jnp.where(first if h == 0 else ~first, q, zero)
                scores = dot_nt(q_head, key) * HD ** (-0.5)
                if i == nb:
                    scores = jnp.where(same, scores, -jnp.inf)
                p = softmax(scores).astype(BF)
                if i == nb:
                    prob_small[pair, h] = p
                else:
                    prob[pair, i, h] = p
                mixed.append(dot(p, value))
            heads[rows, pl.ds(pl.multiple_of(pair * 128, 128), 128)] = jnp.where(first, mixed[0], mixed[1]).astype(BF)

    looped(2 * pairs, attention, events[lot:])

    out_span = pl.ds(3 * half, half)

    def project(i):
        span = pl.ds(pl.multiple_of(i * 256, 256), 256)
        mid[:, span] = dot_nt(heads[:, :half], w[0, 0, span, out_span]) + dot_nt(heads[:, half:], w[0, 1, span, out_span])

    looped(feat // 256, project)

    def norm_two(i):
        middle = x[rows_of(i), :].astype(F32) + mid[rows_of(i), :] + vec(4)
        mid[rows_of(i), :] = middle
        xhat, r = normed(middle)
        value = xhat * vec(2) + vec(3)
        n2[rows_of(i), :] = value.astype(BF)
        acc[rows_of(i), :] = middle + vec(5)

    looped(steps, norm_two)
    for copy in cloads:
        copy.wait()

    weights_ready(1)
    events = weight_events[2]
    lot = len(events) * 2 // 3

    def grad_events(n, lo, hi):
        if not linked:
            return []
        return [functools.partial(link.grad_step, n, code) for code in FALLING[lo:hi]]

    def woven(*lists):
        keyed = [((n + 0.5) / len(events), at, event) for at, events in enumerate(lists) for n, event in enumerate(events)]
        return [event for _, _, event in sorted(keyed, key=lambda one: one[:2])]

    def tile_of(i):
        return i // per, pl.ds(pl.multiple_of((i % per) * tile, tile), tile)

    def up(i):
        k, span = tile_of(i)
        pre = dot(n2[...], w[1, k, :, span]) + bias[k, 6:7, span]
        cdf = 0.5 * (1.0 + lax.erf(pre * 0.7071067811865476))
        act[i] = (pre * cdf).astype(BF)
        slope[i] = (cdf + pre * jnp.exp(-0.5 * pre * pre) * 0.3989422804014327).astype(BF)

    looped(tiles, up, events[:lot])

    def grad_down(i):
        k, span = tile_of(i)
        gd[k, :, span] = dot_tn(cot[...], act[i]).astype(BF)

    looped(tiles, grad_down, events[lot:])
    if linked:
        link.grads_to_core(DOWN)
    weights_ready(2)

    def down(i):
        k, span = tile_of(i)
        acc[...] += dot_nt(act[i], w[2, k, :, span])

    looped(tiles, down, grad_events(DOWN, 0, 3))
    out_rows[...] = acc[...].astype(BF)

    def row_moves(kind, n):
        rows = pl.ds(n * 64, 64)
        source = (out_rows if kind == 0 else n2).at[rows]
        target = out_ref if kind == 0 else back_ref
        target = target.at[t, rows] if linked else target.at[rows]
        near = pltpu.make_async_copy(source, target, o_sem.at[0, kind, n])
        if not linked:
            return [near]
        far = pltpu.make_async_remote_copy(
            source, target, o_sem.at[1, kind, n], o_sem.at[2, kind, n], device_id=link.place(Y), device_id_type=MESH
        )
        return [near, far]

    def row_event(kind, n):
        def go():
            for move in row_moves(kind, n):
                move.start()

        return go

    outs = [row_event(0, n) for n in range(tokens // 64)]

    acc[...] = jnp.zeros_like(acc)
    if linked:
        for g in range(3):
            link.weights_sent(g)

    def back_up(i):
        k, span = tile_of(i)
        back = (slope[i].astype(F32) * dot(cot[...], w[2, k, :, span])).astype(BF)
        bgrad[k, 6:7, span] = jnp.sum(back.astype(F32), axis=0, keepdims=True)
        acc[...] += dot_nt(back, w[1, k, :, span])
        w[1, k, :, span] = dot_tn(n2[...], back).astype(BF)

    bgrad[...] = jnp.zeros_like(bgrad)
    looped(tiles, back_up, woven(grad_events(DOWN, 3, 9), outs[:5]))
    if linked:
        link.grads_to_core(UP)

    vgrad[...] = jnp.zeros_like(vgrad)

    def norm_two_back(i):
        e = acc[rows_of(i), :]
        xhat, r = normed(mid[rows_of(i), :])
        back_out = cot[rows_of(i), :].astype(F32)
        back_middle = back_out + norm_back(e, xhat, r, vec(2))
        acc[rows_of(i), :] = back_middle
        cot[rows_of(i), :] = back_middle.astype(BF)
        vgrad[2:3, :] += jnp.sum(e * xhat, axis=0, keepdims=True)
        vgrad[3:4, :] += jnp.sum(e, axis=0, keepdims=True)
        vgrad[4:5, :] += jnp.sum(back_middle, axis=0, keepdims=True)
        vgrad[5:6, :] += jnp.sum(back_out, axis=0, keepdims=True)

    looped(steps, norm_two_back, woven(grad_events(DOWN, 9, 12), outs[5:7]))

    dheads = heads
    for k in range(2):
        here = pl.ds(k * half, half)
        grad = dot_tn(cot[...], heads[:, here]).astype(BF)
        dheads[:, here] = dot(cot[...], w[0, k, :, out_span]).astype(BF)
        w[0, k, :, out_span] = grad

    if linked:
        link.grads_to_core(OUT)

    def attention_back(i, rows, some):
        stage = []
        for pair in some:
            k, lanes = pair_spans(pair)
            q, key, value = (qkv[k, rows, lanes[c]] for c in range(3))
            dh = dheads[rows, pl.ds(pl.multiple_of(pair * 128, 128), 128)]
            p = [prob_small[pair, h] if i == nb else prob[pair, i, h] for h in range(2)]
            dp = [dot_nt(jnp.where(first if h == 0 else ~first, dh, zero), value) for h in range(2)]
            ds = []
            for h in range(2):
                pf = p[h].astype(F32)
                ds.append((pf * (dp[h] - jnp.sum(pf * dp[h], axis=-1, keepdims=True))).astype(BF))
            stage.append((k, lanes, q, key, dh, p, ds))
        done = []
        scale = HD ** (-0.5)
        for k, lanes, q, key, dh, p, ds in stage:
            dq, dk, dv = [dot(one, key) for one in ds], [dot_tn(one, q) for one in ds], [dot_tn(one, dh) for one in p]
            done.append((k, lanes[0], jnp.where(first, dq[0], dq[1]) * scale))
            done.append((k, lanes[1], jnp.where(first, dk[0], dk[1]) * scale))
            done.append((k, lanes[2], jnp.where(first, dv[0], dv[1])))
        for k, here, value in done:
            qkv[k, rows, here] = value.astype(BF)

    during = [
        woven(grad_events(DOWN, 12, 16), outs[7:9]),
        woven(grad_events(UP, 0, 3), outs[9:]),
        grad_events(UP, 3, 5),
    ]
    backs = []
    for at, (i, start, count) in enumerate(spans):
        rows = pl.ds(start, count)
        looped(
            2,
            lambda n: attention_back(i, rows, [n * pairs + j for j in range(pairs)]),
            during[at] if at < 3 else [],
        )

        def back_first(n):
            span = pl.ds(pl.multiple_of(n * 256, 256), 256)
            both = pl.ds(0, 3 * half)
            mid[rows, span] = dot_nt(qkv[0, rows, both], w[0, 0, span, both]) + dot_nt(
                qkv[1, rows, both], w[0, 1, span, both]
            )

        looped(feat // 256, back_first)

        def norm_one_back(n):
            here = pl.ds(pl.multiple_of(start + n * block, block), block)
            e = mid[here, :]
            xhat, r = normed(x[here, :].astype(F32))
            back_in = acc[here, :] + norm_back(e, xhat, r, vec(0))
            n2[here, :] = back_in.astype(BF)
            vgrad[0:1, :] += jnp.sum(e * xhat, axis=0, keepdims=True)
            vgrad[1:2, :] += jnp.sum(e, axis=0, keepdims=True)

        looped(count // block, norm_one_back)
        mine = [row_event(1, n) for n in range(start // 64, (start + count) // 64)]
        mine[0]()
        backs += mine[1:]

    def grad_qkv(i):
        k, c = i // 3, i % 3
        span = pl.ds(pl.multiple_of(c * half, half), half)
        w[0, k, :, span] = dot_tn(n1[...], qkv[k, :, span]).astype(BF)

    looped(6, grad_qkv, woven(grad_events(UP, 5, 8), backs[:2]))

    def cut_small():
        low = lax.broadcasted_iota(jnp.int32, (8, 128), 1)
        row = lax.broadcasted_iota(jnp.int32, (8, 128), 0)
        for at in range(feat // 48):
            value = vgrad[...]
            if at:
                value = pltpu.roll(value, feat - at * 48, 1)
            value = jnp.where((low < 48) & (row < 6), value[:, :128], 0.0)
            for k in range(2):
                more = bgrad[k]
                if at:
                    more = pltpu.roll(more, wide - at * 96, 1)
                small_abs_sum[k, at] = value + jnp.where((low < 96) & (row == 6), more[:, :128], 0.0)
        for code in range(32):
            pd, pt = small_place(code)
            small_sum[code] = small_abs_sum[pt, pd]

    small_abs_sum = small_in[1]
    small_got = small_in[0]

    def sum_move(k):
        return pltpu.make_async_remote_copy(
            small_sum.at[pl.ds(2**k, 2**k)],
            small_got.at[pl.ds(2**k, 2**k)],
            s_sem.at[2, k],
            s_sem.at[3, k],
            device_id=small_place(2**k),
            device_id_type=MESH,
        )

    def sum_step(k):
        def go():
            if k < 4:
                sum_move(k + 1).wait()
                here = pl.ds(0, 2 ** (k + 1))
                small_sum[here] = small_sum[here] + small_got[pl.ds(2 ** (k + 1), 2 ** (k + 1))]
            if k >= 0:
                sum_move(k).start()

        return go

    if linked:
        link.grads_to_core(QKV)
        cut_small()
        sums = [sum_step(k) for k in range(4, -2, -1)]
        first_half = woven(grad_events(UP, 8, 16), grad_events(OUT, 0, 12), grad_events(QKV, 0, 5), sums[:3], backs[2:5])
        second = woven(grad_events(OUT, 12, 16) + grad_events(QKV, 5, 16), sums[3:], backs[5:])
        for event in first_half + second:
            event()
        vshare[...] = small_sum[0]
        for n in range(4):
            link.grads_sent(n)
    else:
        for event in backs:
            event()
        saves = []
        for g in range(3):
            for k in range(2):
                source = gd.at[k] if g == 2 else w.at[g, k]
                saves.append(pltpu.make_async_copy(source, share.at[g, k], acsend.at[g, k]))
        for copy in saves:
            copy.start()
        for copy in saves:
            copy.wait()
        vshare[pl.ds(0, 8), pl.ds(0, feat)] = vgrad[...]
        for k in range(2):
            vshare[pl.ds(8 + 8 * k, 8), :] = bgrad[k]
    for kind in range(2):
        for n in range(tokens // 64):
            for move in row_moves(kind, n):
                move.wait()


VLIM = 60


def run_layer(linked, big, small, bvis, svis, bcot, scot, w, vectors, bias, parts, wide):
    nb, bl = bvis.shape[0] // parts, bvis.shape[2]
    ns, sl = svis.shape[0] // parts, svis.shape[2]
    tokens = nb * bl + ns * sl
    feat = big.shape[2]
    tile = wide // 3
    tiles = 6
    pairs = feat // 128
    rows = w.shape[1] if linked else 48
    vm, hbm = pl.BlockSpec(memory_space=pltpu.VMEM), pl.BlockSpec(memory_space=pl.ANY)
    pair = (2, tokens, feat) if linked else (tokens, feat)
    dma = pltpu.SemaphoreType.DMA
    link = (lambda *shape: pltpu.VMEM(shape, BF)) if linked else (lambda *shape: pltpu.VMEM((16, 128), BF))
    loads = nb * (big.shape[1] // 512) + ns
    return pl.pallas_call(
        functools.partial(layer_kernel, (nb, bl, ns, sl), linked),
        out_shape=(
            jax.ShapeDtypeStruct(pair, BF),
            jax.ShapeDtypeStruct(pair, BF),
            jax.ShapeDtypeStruct((3, rows, wide) if linked else w.shape, F32 if linked else BF),
            jax.ShapeDtypeStruct((8, 128) if linked else (24, wide), F32),
        ),
        in_specs=[hbm, hbm, vm, vm, hbm, hbm, hbm, vm, vm],
        out_specs=(hbm, hbm, vm if linked else hbm, vm),
        scratch_shapes=[
            pltpu.VMEM((3, 2, feat, wide), BF),
            pltpu.VMEM((2, feat, wide), BF),
            link(3, 16, rows, wide),
            link(3, 15, rows, wide),
            pltpu.VMEM((tokens, feat), BF),
            pltpu.VMEM((tokens, feat), BF),
            pltpu.VMEM((tokens, feat), BF),
            pltpu.VMEM((2, tokens, 3 * feat // 2), BF),
            pltpu.VMEM((pairs, nb, 2, bl, bl), BF),
            pltpu.VMEM((pairs, 2, ns * sl, ns * sl), BF),
            pltpu.VMEM((tokens, feat), BF),
            pltpu.VMEM((tokens, feat), F32),
            pltpu.VMEM((tokens, feat), F32),
            pltpu.VMEM((tiles, tokens, tile), BF),
            pltpu.VMEM((tiles, tokens, tile), BF),
            pltpu.VMEM((tokens, feat), BF),
            pltpu.VMEM((tokens, feat), BF),
            pltpu.VMEM((8, feat), F32),
            pltpu.VMEM((2, 8, wide), F32),
            pltpu.VMEM((8, feat), F32),
            pltpu.VMEM((2, 8, wide), F32),
            pltpu.VMEM((32, 16, 128), BF),
            pltpu.VMEM((2, 16, 16, 128), BF),
            pltpu.VMEM((32, 8, 128), F32),
            [pltpu.VMEM((32, 8, 128), F32), pltpu.VMEM((2, 16, 8, 128), F32)],
            dma((3, 2, 16)),
            dma((3, 2, 16)),
            dma((3, 16)),
            dma((3, 16)),
            dma((4, 2, 15)),
            dma((4, 2, 15)),
            dma((4, 16)),
            dma((4, 16)),
            dma((3,)),
            dma((loads, 2)),
            dma((nb + ns,)),
            dma((3, 2, tokens // 64)),
            dma((4, 5)),
        ],
        compiler_params=pltpu.CompilerParams(
            collective_id=0 if linked else None, has_side_effects=linked, vmem_limit_bytes=VLIM * MIB
        ),
        name="layer",
    )(big, small, bvis, svis, bcot, scot, w, vectors, bias)


def scatter_kernel(bvis_ref, svis_ref, brow_ref, srow_ref, big_ref, small_ref):
    def spread(vis, rows, length):
        hot = lax.broadcasted_iota(jnp.int32, (length, vis.shape[1]), 0) == vis
        return dot(hot.astype(BF), rows)

    big_ref[...] = spread(bvis_ref[...], brow_ref[...], big_ref.shape[0])
    small_ref[...] = spread(svis_ref[...], srow_ref[...], small_ref.shape[0])


def scatter_rows(bvis, svis, rows, big_len, small_len):
    parts = rows.shape[0]
    nb, _, bl = bvis.shape
    ns, _, sl = svis.shape
    feat = rows.shape[2]
    share = nb // parts
    first_small = share * bl // sl
    return pl.pallas_call(
        scatter_kernel,
        grid=(nb,),
        out_shape=(
            jax.ShapeDtypeStruct((nb, big_len, feat), F32),
            jax.ShapeDtypeStruct((ns, small_len, feat), F32),
        ),
        in_specs=[
            pl.BlockSpec((None, 1, bl), lambda i: (i, 0, 0)),
            pl.BlockSpec((None, 1, sl), lambda i: (i, 0, 0)),
            pl.BlockSpec((None, bl, feat), lambda i: (i // share, i % share, 0)),
            pl.BlockSpec((None, sl, feat), lambda i: (i // share, first_small + i % share, 0)),
        ],
        out_specs=(
            pl.BlockSpec((None, big_len, feat), lambda i: (i, 0, 0)),
            pl.BlockSpec((None, small_len, feat), lambda i: (i, 0, 0)),
        ),
        compiler_params=pltpu.CompilerParams(vmem_limit_bytes=40 * MIB),
        name="scatter_rows",
    )(bvis, svis, rows, rows)


def adam_step(weight, moment_one, moment_two, gradient, step_rate, decay_rate):
    moment_one = 0.9 * moment_one + 0.1 * gradient
    moment_two = 0.999 * moment_two + 0.001 * gradient * gradient
    fixed_one = moment_one / (1.0 - 0.9**STEP_NUMBER)
    fixed_two = moment_two / (1.0 - 0.999**STEP_NUMBER)
    update = fixed_one / (jnp.sqrt(fixed_two) + 1e-08) + decay_rate * weight
    return (weight - step_rate * update, moment_one, moment_two)


def on_device(
    special,
    big_patches, small_patches, big_visible, small_visible, big_cot, small_cot,
    qkv_weight, qkv_first, qkv_second, out_weight, out_first, out_second,
    up_weight, up_first, up_second, down_weight, down_first, down_second,
    up_bias, up_bias_first, up_bias_second, norm_vectors, norm_first, norm_second,
):
    rows, half = out_weight.shape
    wide = up_weight.shape[1]
    feat = big_patches.shape[2]
    parts = feat // half
    piece = jnp.stack(
        [
            jnp.concatenate([qkv_weight.reshape(rows, 3 * half), out_weight], axis=1).astype(BF),
            up_weight.astype(BF),
            down_weight.astype(BF),
        ]
    )
    bvis, svis = big_visible[:, None, :], small_visible[:, None, :]
    chips = (big_patches, small_patches, bvis, svis, big_cot, small_cot)
    if special:
        few = jnp.concatenate(
            [
                jnp.pad(norm_vectors, ((0, 0), (0, 128 - norm_vectors.shape[1]))),
                jnp.pad(up_bias, ((0, 9), (0, 128 - up_bias.shape[1]))),
            ]
        ).astype(BF)
        out_both, back_both, share, vshare = run_layer(True, *chips, piece, few, few, parts, wide)
        norm_share = vshare[:6, : norm_vectors.shape[1]]
        bias_share = vshare[6:7, : up_bias.shape[1]]
    else:
        w = lax.all_gather(lax.all_gather(piece, "dp", axis=1, tiled=True), "tensor", axis=1)
        vectors = lax.all_gather(norm_vectors.astype(BF), "dp", axis=1, tiled=True).astype(F32)
        bias = lax.all_gather(up_bias.astype(BF), "dp", axis=1, tiled=True)
        bias = lax.all_gather(bias, "tensor", axis=0).astype(F32)
        out_rows, back_rows, grads, few = run_layer(
            False, *chips, w, jnp.pad(vectors, ((0, 2), (0, 0))), jnp.pad(bias, ((0, 0), (6, 1), (0, 0))), parts, wide
        )
        share = lax.psum_scatter(grads, "tensor", scatter_dimension=1)
        share = lax.psum_scatter(share, "dp", scatter_dimension=1, tiled=True).astype(F32)
        both = lax.all_gather(jnp.stack([out_rows, back_rows]), "tensor", axis=1)
        out_both, back_both = both[0], both[1]
        norm_share = lax.psum_scatter(lax.psum(few[:6, :feat], "tensor"), "dp", scatter_dimension=1, tiled=True)
        bias_share = lax.psum_scatter(few[14::8], "tensor", scatter_dimension=0, tiled=True)
        bias_share = lax.psum_scatter(bias_share, "dp", scatter_dimension=1, tiled=True)
    big_count, big_len = big_visible.shape
    small_count, small_len = small_visible.shape
    cut = big_count // parts * big_len
    big_out = out_both[:, :cut].reshape(big_count, big_len, feat)
    small_out = out_both[:, cut:].reshape(small_count, small_len, feat)
    big_grad, small_grad = scatter_rows(bvis, svis, back_both, big_patches.shape[1], small_patches.shape[1])

    qkv_share = share[0, :, : 3 * half].reshape(rows, 3, half)
    new = []
    for at, (weight, one, two, gradient) in enumerate(
        (
            (qkv_weight, qkv_first, qkv_second, qkv_share),
            (out_weight, out_first, out_second, share[0, :, 3 * half :]),
            (up_weight, up_first, up_second, share[1]),
            (down_weight, down_first, down_second, share[2]),
            (up_bias, up_bias_first, up_bias_second, bias_share),
            (norm_vectors, norm_first, norm_second, norm_share),
        )
    ):
        new.extend(adam_step(weight, one, two, gradient, LEARN_RATES[at], DECAYS[at]))
    return (big_out, small_out, big_grad, small_grad, *new)


def solution(mesh):
    special = mesh.shape["dp"] == 16 and mesh.shape["tensor"] == 2
    chips = P("dp", None, None)
    matrix, qkv = P("dp", "tensor"), P("dp", None, "tensor")
    states = (qkv,) * 3 + (matrix,) * 9 + (P("tensor", "dp"),) * 3 + (P(None, "dp"),) * 3
    return jax.shard_map(
        functools.partial(on_device, special),
        mesh=mesh,
        in_specs=(chips, chips, P("dp", None), P("dp", None), chips, chips) + states,
        out_specs=(chips,) * 4 + states,
        check_vma=False,
    )
```

```python
import functools

import jax
import jax.numpy as jnp
from jax import lax
from jax.experimental import pallas as pl
from jax.experimental.pallas import tpu as pltpu
from jax.sharding import PartitionSpec as P

HD = 64
STEP_NUMBER = 10
BF, F32 = jnp.bfloat16, jnp.float32
MESH = pl.DeviceIdType.MESH
MIB = 2**20

LEARN_RATES = (0.03, 0.1, 0.03, 0.015, 0.2, 0.2)
DECAYS = (0.05, 0.05, 0.05, 0.05, 0.0, 0.0)

Z1, Z2, X, Y = 1, 2, 4, 8
DIMS = (Z1, Z2, X, Y)
def place(code, other_core=False):
    d, t = lax.axis_index("dp"), lax.axis_index("tensor")
    z, x, c = lax.div(d, 4), lax.rem(lax.div(d, 2), 2), lax.rem(d, 2)
    if code & Z1:
        z = z + 1 - 2 * lax.rem(z, 2)
    if code & Z2:
        z = z + 2 - 4 * lax.div(z, 2)
    if code & X:
        x = 1 - x
    if code & Y:
        t = 1 - t
    if other_core:
        c = 1 - c
    return z * 4 + x * 2 + c, t


def greet(place):
    barrier = pltpu.get_barrier_semaphore()
    for dim in DIMS:
        pl.semaphore_signal(barrier, inc=1, device_id=place(dim), device_id_type=MESH)
    pl.semaphore_signal(barrier, inc=1, device_id=place(0, True), device_id_type=MESH)
    pl.semaphore_wait(barrier, 5)


def bits(code):
    return bin(code).count("1")


def top_of(order, code):
    return max([order.index(k) for k in DIMS if code & k], default=-1)


def dot(a, b):
    return jnp.dot(a, b, preferred_element_type=F32)


def dot_nt(a, b):
    return lax.dot_general(a, b, (((1,), (1,)), ((), ())), preferred_element_type=F32)


def dot_tn(a, b):
    return lax.dot_general(a, b, (((0,), (0,)), ((), ())), preferred_element_type=F32)


def normed(v):
    centred = v - jnp.mean(v, axis=-1, keepdims=True)
    r = lax.rsqrt(jnp.mean(centred * centred, axis=-1, keepdims=True) + 1e-05)
    return centred * r, r


def norm_back(e, xhat, r, gain):
    eg = e * gain
    return r * (eg - jnp.mean(eg, axis=-1, keepdims=True) - xhat * jnp.mean(eg * xhat, axis=-1, keepdims=True))


def column_of(row):
    wide = jnp.broadcast_to(row.astype(F32), (128, row.shape[1]))
    return jnp.transpose(wide).astype(jnp.int32)


T, PP, Q, R = (Z2, Z1, X, Y), (Z2, Z1, Y, X), (Z2, Y, X, Z1), (Y, Z2, X, Z1)
GATHER_ORDERS = ((T, PP), (T, PP), (T, PP))
AHEAD = 2
DOWN, UP, OUT, QKV = range(4)
SUMS = (
    (2, ((PP, 0, 768), (R, 768, 768))),
    (1, ((PP, 0, 768), (R, 768, 768))),
    (0, ((PP, 1152, 256), (R, 1408, 128))),
    (0, ((PP, 0, 512), (R, 512, 640))),
)
SLOTS = {}
for _order in (T, PP, Q, R):
    SLOTS[_order] = {}
    for _at, _dim in enumerate(_order):
        for _code in range(16):
            if top_of(_order, _code) < _at:
                SLOTS[_order][_code, _dim] = len(SLOTS[_order])
RISING = sorted(range(1, 16), key=bits)
FALLING = sorted(range(16), key=lambda code: -bits(code))


def cut_columns(orders, cols):
    width = cols // len(orders)
    return [(order, pl.ds(at * width, width)) for at, order in enumerate(orders)]


class Links:
    def __init__(self, rows, w, gd, from_core, from_chip, share, sems):
        self.w, self.gd = w, gd
        self.from_core, self.from_chip, self.share = from_core, from_chip, share
        (
            self.asend, self.arecv, self.acsend, self.acrecv,
            self.rsend, self.rrecv, self.rcsend, self.rcrecv,
        ) = sems
        self.rows, self.cols = rows, w.shape[3]

        self.places = {(code, core): place(code, core) for code in range(16) for core in (False, True)}
        self.spans = {at: pl.ds(pl.multiple_of(d * self.rows, self.rows), self.rows) for at, (d, _) in self.places.items()}

    def place(self, code, core=False):
        return self.places[code, core]

    def at(self, code, core=False):
        return self.places[code, core][1], self.spans[code, core]

    def weight_move(self, g, part, code, dim):
        span = cut_columns(GATHER_ORDERS[g], self.cols)[part][1]
        target = self.w.at[(g,) + self.at(code) + (span,)]
        return pltpu.make_async_remote_copy(
            target,
            target,
            self.asend.at[g],
            self.arecv.at[g, code ^ dim],
            device_id=self.place(dim),
            device_id_type=MESH,
        )

    def weight_core_move(self, g, code, mine=True):
        target = self.w.at[(g,) + self.at(code, not mine)]
        return pltpu.make_async_remote_copy(
            target,
            target,
            self.acsend.at[g],
            self.acrecv.at[g],
            device_id=self.place(0, True),
            device_id_type=MESH,
        )

    def weight_forward(self, g, code):
        if code:
            target = self.w.at[(g,) + self.at(code)]
            pltpu.make_async_remote_copy(
                target, target, self.asend.at[g], self.arecv.at[g, code], device_id=self.place(Z1), device_id_type=MESH
            ).wait_recv()
        for part, order in enumerate(GATHER_ORDERS[g]):
            for dim in order[top_of(order, code) + 1 :]:
                self.weight_move(g, part, code, dim).start()
        self.weight_core_move(g, code).start()

    def weights_complete(self, g):
        target = self.w.at[g, 0]
        pltpu.make_async_remote_copy(
            target, target, self.acsend.at[g], self.acrecv.at[g], device_id=self.place(0, True), device_id_type=MESH
        ).wait_recv()

    def weights_sent(self, g):
        for ref, send, recv in (
            (self.from_chip.at[g], self.asend.at[g], self.arecv.at[g, 1]),
            (self.from_core.at[g], self.acsend.at[g], self.acrecv.at[g]),
        ):
            pltpu.make_async_remote_copy(
                ref, ref, send, recv, device_id=self.place(0, True), device_id_type=MESH
            ).wait_send()

    def grad(self, n, code, core, start, width):
        g = SUMS[n][0]
        where = self.at(code, core) + (pl.ds(start, width),)
        return (self.gd, where) if g == 2 else (self.w, (g,) + where)

    def grad_core_move(self, n, code):
        g, parts = SUMS[n]
        start, width = parts[0][1], sum(part[2] for part in parts)
        ref, where = self.grad(n, code, True, start, width)
        return pltpu.make_async_remote_copy(
            ref.at[where],
            self.from_core.at[g, code, :, pl.ds(start, width)],
            self.rcsend.at[n],
            self.rcrecv.at[n, code],
            device_id=self.place(0, True),
            device_id_type=MESH,
        )

    def grad_move(self, n, part, code, dim, sending):
        g, parts = SUMS[n]
        order, start, width = parts[part]
        ref, where = self.grad(n, code, False, start, width)
        slot = SLOTS[order][code ^ dim if sending else code, dim]
        return pltpu.make_async_remote_copy(
            ref.at[where],
            self.from_chip.at[g, slot, :, pl.ds(start, width)],
            self.rsend.at[n],
            self.rrecv.at[n, part, slot],
            device_id=self.place(dim),
            device_id_type=MESH,
        )

    def grads_to_core(self, n):
        for code in FALLING:
            self.grad_core_move(n, code).start()

    def grad_step(self, n, code):
        g, parts = SUMS[n]
        self.grad_core_move(n, code).wait_recv()
        for part, (order, start, width) in enumerate(parts):
            at = top_of(order, code)
            span = pl.ds(start, width)
            ref, where = self.grad(n, code, False, start, width)
            value = ref[where].astype(F32) + self.from_core[g, code, :, span].astype(F32)
            for dim in reversed(order[at + 1 :]):
                self.grad_move(n, part, code, dim, False).wait_recv()
                value = value + self.from_chip[g, SLOTS[order][code, dim], :, span].astype(F32)
            if code == 0:
                self.share[g, :, span] = value
            else:
                ref[where] = value.astype(BF)
                self.grad_move(n, part, code, order[at], True).start()

    def grads_sent(self, n):
        g, parts = SUMS[n]
        span = pl.ds(parts[0][1], sum(part[2] for part in parts))
        for ref, send, recv in (
            (self.from_chip.at[g, :, :, span], self.rsend.at[n], self.rrecv.at[n, 0, 0]),
            (self.from_core.at[g, :, :, span], self.rcsend.at[n], self.rcrecv.at[n, 0]),
        ):
            pltpu.make_async_remote_copy(
                ref, ref, send, recv, device_id=self.place(0, True), device_id_type=MESH
            ).wait_send()


def looped(count, body, events=()):
    events = list(events)

    @pl.loop(0, count)
    def _(i):
        body(i)
        for at in range(count):
            mine = events[len(events) * at // count : len(events) * (at + 1) // count]
            if mine:

                @pl.when(i == at)
                def _():
                    for event in mine:
                        event()


def layer_kernel(
    shape,
    linked,
    big_ref, small_ref, bvis_ref, svis_ref, bcot_ref, scot_ref, *refs,
):
    if linked:
        attn_ref, up_ref, down_ref, norm_ref, up_bias_ref, *refs = refs
    else:
        w_ref, vec_ref, bias_ref, *refs = refs
    run_kernel(
        shape, linked, big_ref, small_ref, bvis_ref, svis_ref, bcot_ref, scot_ref,
        (attn_ref, up_ref, down_ref, norm_ref, up_bias_ref) if linked else (w_ref, vec_ref, bias_ref), *refs,
    )


def run_kernel(
    shape,
    linked,
    big_ref, small_ref, bvis_ref, svis_ref, bcot_ref, scot_ref, weight_refs,
    out_ref, back_ref, share, vshare,
    few, w, gd, from_core, from_chip, x, n1, n2, qkv, prob, prob_small, heads, mid, acc, act, slope, cot, out_rows,
    vecs, bias, vgrad, bgrad, small, small_abs, small_sum, small_in,
    asend, arecv, acsend, acrecv, rsend, rrecv, rcsend, rcrecv, own, p_sem, c_sem, o_sem, s_sem,
):
    nb, bl, ns, sl = shape
    feat, wide = w.shape[2:]
    cut = nb * bl
    tokens = cut + ns * sl
    half = feat // 2
    pairs = half // 128
    d, t = lax.axis_index("dp"), lax.axis_index("tensor")
    block = 128
    steps = tokens // block
    tile = act.shape[2]
    tiles = act.shape[0]
    per = tiles // 2
    small_rows = ns * sl
    spans = [(i, i * bl, bl) for i in range(nb)] + [(nb, cut, small_rows)]
    chunk = 512
    strips = [(at, min(tile, feat - at)) for at in range(0, feat, tile)]

    cloads = [
        pltpu.make_async_copy(bcot_ref.at[t * nb + i], cot.at[pl.ds(i * bl, bl)], c_sem) for i in range(nb)
    ]
    cloads += [
        pltpu.make_async_copy(scot_ref.at[t * ns + i], cot.at[pl.ds(cut + i * sl, sl)], c_sem)
        for i in range(ns)
    ]
    big_len, small_len = big_ref.shape[1], small_ref.shape[1]
    ploads = []
    for i in range(nb):
        for at in range(big_len // chunk):
            source = big_ref.at[t * nb + i, pl.ds(at * chunk, chunk)]
            ploads.append((i, at, source, chunk, (bvis_ref, t * nb + i, i * bl, bl)))
    for i in range(ns):
        ploads.append((nb + i, 0, small_ref.at[t * ns + i], small_len, (svis_ref, t * ns + i, cut + i * sl, sl)))

    def pload(at):
        _, _, source, length, _ = ploads[at]
        return [
            pltpu.make_async_copy(
                source.at[:, pl.ds(start, width)],
                act.at[at % 2 * len(strips) + c, pl.ds(0, length), pl.ds(0, width)],
                p_sem.at[at, c],
            )
            for c, (start, width) in enumerate(strips)
        ]

    for copy in pload(0):
        copy.start()
    for copy in cloads:
        copy.start()

    if linked:
        attn_ref, up_ref, down_ref, norm_ref, up_bias_ref = weight_refs
        stage = [
            pltpu.make_async_copy(ref, share.at[g], own.at[g, 0]) for g, ref in ((1, up_ref), (2, down_ref))
        ]
        for copy in stage:
            copy.start()
        few[...] = jnp.zeros_like(few)
        few[: norm_ref.shape[0], : norm_ref.shape[1]] = norm_ref[...]
        few[6:7, : up_bias_ref.shape[1]] = up_bias_ref[...]
        link = Links(
            attn_ref.shape[0], w, gd, from_core, from_chip, share,
            (asend, arecv, acsend, acrecv, rsend, rrecv, rcsend, rcrecv),
        )
        w[(0,) + link.at(0)] = attn_ref[...]
        for g in (1, 2):
            stage[g - 1].wait()
            w[(g,) + link.at(0)] = share[g].astype(BF)

        def small_place(code):
            return link.place(code >> 1, bool(code & 1))

        small[0] = few[...].astype(BF)
        greet(link.place)
    else:
        w_ref, vec_ref, bias_ref = weight_refs
        wloads = [
            [pltpu.make_async_copy(w_ref.at[g, k], w.at[g, k], own.at[g, k]) for k in range(2)] for g in range(3)
        ]
        for copy in sum(wloads, []):
            copy.start()

    def small_move(k):
        return pltpu.make_async_remote_copy(
            small.at[pl.ds(0, 2**k)],
            small.at[pl.ds(2**k, 2**k)],
            s_sem.at[0, k],
            s_sem.at[1, k],
            device_id=small_place(2**k),
            device_id_type=MESH,
        )

    def small_step(k):
        def go():
            if k:
                small_move(k - 1).wait()
            if k < 5:
                small_move(k).start()

        return go

    def set_vectors():
        for code in range(32):
            pd, pt = small_place(code)
            small_abs[pt, pd] = small[code]
        vec_sum, bias_sum = 0.0, [0.0, 0.0]
        parts = feat // 48 if linked else 0
        for at in range(parts):
            for k in range(2):
                value = small_abs[k, at].astype(F32)
                if k == 0:
                    padded = jnp.concatenate([value, jnp.zeros((16, feat - 128), F32)], axis=1)
                    vec_sum = vec_sum + (pltpu.roll(padded, at * 48, 1) if at else padded)
                padded = jnp.concatenate([value[:8], jnp.zeros((8, wide - 128), F32)], axis=1)
                bias_sum[k] = bias_sum[k] + (pltpu.roll(padded, at * 96, 1) if at else padded)
        vecs[...] = vec_sum[:8]
        for k in range(2):
            bias[k] = bias_sum[k]

    def vec(i):
        return vecs[i : i + 1, :]

    def rows_of(i):
        return pl.ds(pl.multiple_of(i * block, block), block)

    def pick(at):
        def go():
            chip, part, _, length, (vis_ref, row, first_row, count) = ploads[at]
            for copy in pload(at):
                copy.wait()
            if at + 1 < len(ploads):
                for copy in pload(at + 1):
                    copy.start()
            column = column_of(vis_ref[pl.ds(row, 1), :]) - part * length
            lane = lax.broadcasted_iota(jnp.int32, column.shape, 1)
            hot = jnp.concatenate([(column == lane + k * 128).astype(BF) for k in range(length // 128)], axis=1)
            rows = pl.ds(first_row, count)
            for c, (start, width) in enumerate(strips):
                picked = dot(hot, act[at % 2 * len(strips) + c, :length, :width])
                span = pl.ds(start, width)
                if part:
                    picked = picked + x[rows, span].astype(F32)
                x[rows, span] = picked.astype(BF)

        return go

    picks = [pick(at) for at in range(len(ploads))]

    def weight_event(g, code):
        return lambda: link.weight_forward(g, code)

    if linked:
        order = sorted(
            [(bits(code) + AHEAD * g, g, n, code) for g in range(3) for n, code in enumerate([0] + RISING)]
        )
        sequence = [(g, weight_event(g, code)) for _, g, _, code in order]
        last = [max(i for i, (g, _) in enumerate(sequence) if g == k) for k in range(3)]
        weight_events = [[e for _, e in sequence[lo : hi + 1]] for lo, hi in zip([0] + [i + 1 for i in last], last)]
        smalls = [small_step(k) for k in range(6)]
        mixed = [weight_events[0][0], smalls[0], picks[0], picks[1]] + weight_events[0][1:3] + [smalls[1], picks[2]]
        mixed += weight_events[0][3:5] + [picks[3], smalls[2]] + weight_events[0][5:8] + [picks[4], smalls[3]]
        mixed += weight_events[0][8:11] + picks[5:] + [smalls[4]] + weight_events[0][11:14] + [smalls[5]]
        mixed += weight_events[0][14:]
        for event in mixed:
            event()
        set_vectors()
    else:
        weight_events = [[], [], []]
        for event in picks:
            event()
        vecs[...] = vec_ref[...]
        bias[...] = bias_ref[...]

    def weights_ready(g):
        if linked:
            link.weights_complete(g)
        else:
            for copy in wloads[g]:
                copy.wait()

    def norm_one(i):
        xhat, r = normed(x[rows_of(i), :].astype(F32))
        value = xhat * vec(0) + vec(1)
        n1[rows_of(i), :] = value.astype(BF)

    looped(steps, norm_one)
    weights_ready(0)
    events = weight_events[1]
    lot = len(events) // 3

    def make_qkv(i):
        k, c = i // 3, i % 3
        span = pl.ds(pl.multiple_of(c * half, half), half)
        qkv[k, :, span] = dot(n1[...], w[0, k, :, span]).astype(BF)

    looped(6, make_qkv, events[:lot])

    lane = lax.broadcasted_iota(jnp.int32, (1, 128), 1)
    first = lane < HD
    zero = jnp.zeros((), BF)

    def softmax(scores):
        e = jnp.exp(scores - jnp.max(scores, axis=-1, keepdims=True))
        return e / jnp.sum(e, axis=-1, keepdims=True)

    same = (
        lax.broadcasted_iota(jnp.int32, (small_rows, small_rows), 0) // sl
        == lax.broadcasted_iota(jnp.int32, (small_rows, small_rows), 1) // sl
    )

    def pair_spans(pair):
        k, j = pair // pairs, pair % pairs
        return k, [pl.ds(pl.multiple_of(c * half + j * 128, 128), 128) for c in range(3)]

    def attention(pair):
        k, lanes = pair_spans(pair)
        for i, start, count in spans:
            rows = pl.ds(start, count)
            q, key, value = (qkv[k, rows, lanes[c]] for c in range(3))
            mixed = []
            for h in range(2):
                q_head = jnp.where(first if h == 0 else ~first, q, zero)
                scores = dot_nt(q_head, key) * HD ** (-0.5)
                if i == nb:
                    scores = jnp.where(same, scores, -jnp.inf)
                p = softmax(scores).astype(BF)
                if i == nb:
                    prob_small[pair, h] = p
                else:
                    prob[pair, i, h] = p
                mixed.append(dot(p, value))
            heads[rows, pl.ds(pl.multiple_of(pair * 128, 128), 128)] = jnp.where(first, mixed[0], mixed[1]).astype(BF)

    looped(2 * pairs, attention, events[lot:])

    out_span = pl.ds(3 * half, half)

    def project(i):
        span = pl.ds(pl.multiple_of(i * 256, 256), 256)
        mid[:, span] = dot_nt(heads[:, :half], w[0, 0, span, out_span]) + dot_nt(heads[:, half:], w[0, 1, span, out_span])

    looped(feat // 256, project)

    def norm_two(i):
        middle = x[rows_of(i), :].astype(F32) + mid[rows_of(i), :] + vec(4)
        mid[rows_of(i), :] = middle
        xhat, r = normed(middle)
        value = xhat * vec(2) + vec(3)
        n2[rows_of(i), :] = value.astype(BF)
        acc[rows_of(i), :] = middle + vec(5)

    looped(steps, norm_two)
    pltpu.make_async_copy(cot, cot, c_sem).wait()

    weights_ready(1)
    events = weight_events[2]
    lot = len(events) * 2 // 3

    def grad_events(n, lo, hi):
        if not linked:
            return []
        return [functools.partial(link.grad_step, n, code) for code in FALLING[lo:hi]]

    def woven(*lists):
        keyed = [((n + 0.5) / len(events), at, event) for at, events in enumerate(lists) for n, event in enumerate(events)]
        return [event for _, _, event in sorted(keyed, key=lambda one: one[:2])]

    def tile_of(i):
        return i // per, pl.ds(pl.multiple_of((i % per) * tile, tile), tile)

    def up(i):
        at, here = i // 2, pl.ds(pl.multiple_of(i % 2 * 256, 256), 256)
        k, span = at // per, pl.ds(pl.multiple_of(at % per * tile + i % 2 * 256, 256), 256)
        pre = dot(n2[...], w[1, k, :, span]) + bias[k, 6:7, span]
        cdf = 0.5 * (1.0 + lax.erf(pre * 0.7071067811865476))
        act[at, :, here] = (pre * cdf).astype(BF)
        slope[at, :, here] = (cdf + pre * jnp.exp(-0.5 * pre * pre) * 0.3989422804014327).astype(BF)

    looped(tiles * 2, up, events[:lot])

    def grad_down(i):
        k, span = tile_of(i)
        gd[k, :, span] = dot_tn(cot[...], act[i]).astype(BF)

    looped(tiles, grad_down, events[lot:])
    if linked:
        link.grads_to_core(DOWN)
    weights_ready(2)

    def down(i):
        k, span = tile_of(i)
        acc[...] += dot_nt(act[i], w[2, k, :, span])

    looped(tiles, down, grad_events(DOWN, 0, 3))
    out_rows[...] = acc[...].astype(BF)

    def row_moves(kind, n):
        rows = pl.ds(n * 64, 64)
        source = (out_rows if kind == 0 else n2).at[rows]
        target = out_ref if kind == 0 else back_ref
        target = target.at[t, rows] if linked else target.at[rows]
        near = pltpu.make_async_copy(source, target, o_sem.at[0, kind])
        if not linked:
            return [near]
        far = pltpu.make_async_remote_copy(
            source, target, o_sem.at[1, kind], o_sem.at[2, kind], device_id=link.place(Y), device_id_type=MESH
        )
        return [near, far]

    def row_event(kind, n):
        def go():
            for move in row_moves(kind, n):
                move.start()

        return go

    outs = [row_event(0, n) for n in range(tokens // 64)]

    acc[...] = jnp.zeros_like(acc)
    if linked:
        for g in range(3):
            link.weights_sent(g)

    def back_up(i):
        k, span = tile_of(i)
        back = (slope[i].astype(F32) * dot(cot[...], w[2, k, :, span])).astype(BF)
        bgrad[k, 6:7, span] = jnp.sum(back.astype(F32), axis=0, keepdims=True)
        acc[...] += dot_nt(back, w[1, k, :, span])
        w[1, k, :, span] = dot_tn(n2[...], back).astype(BF)

    bgrad[...] = jnp.zeros_like(bgrad)
    looped(tiles, back_up, woven(grad_events(DOWN, 3, 9), outs[:5]))
    if linked:
        link.grads_to_core(UP)

    vgrad[...] = jnp.zeros_like(vgrad)

    def norm_two_back(i):
        e = acc[rows_of(i), :]
        xhat, r = normed(mid[rows_of(i), :])
        back_out = cot[rows_of(i), :].astype(F32)
        back_middle = back_out + norm_back(e, xhat, r, vec(2))
        acc[rows_of(i), :] = back_middle
        cot[rows_of(i), :] = back_middle.astype(BF)
        vgrad[2:3, :] += jnp.sum(e * xhat, axis=0, keepdims=True)
        vgrad[3:4, :] += jnp.sum(e, axis=0, keepdims=True)
        vgrad[4:5, :] += jnp.sum(back_middle, axis=0, keepdims=True)
        vgrad[5:6, :] += jnp.sum(back_out, axis=0, keepdims=True)

    looped(steps, norm_two_back, woven(grad_events(DOWN, 9, 12), outs[5:7]))

    dheads = heads
    for k in range(2):
        here = pl.ds(k * half, half)
        grad = dot_tn(cot[...], heads[:, here]).astype(BF)
        dheads[:, here] = dot(cot[...], w[0, k, :, out_span]).astype(BF)
        w[0, k, :, out_span] = grad

    if linked:
        link.grads_to_core(OUT)

    def attention_back(i, rows, some):
        stage = []
        for pair in some:
            k, lanes = pair_spans(pair)
            q, key, value = (qkv[k, rows, lanes[c]] for c in range(3))
            dh = dheads[rows, pl.ds(pl.multiple_of(pair * 128, 128), 128)]
            p = [prob_small[pair, h] if i == nb else prob[pair, i, h] for h in range(2)]
            dp = [dot_nt(jnp.where(first if h == 0 else ~first, dh, zero), value) for h in range(2)]
            ds = []
            for h in range(2):
                pf = p[h].astype(F32)
                ds.append((pf * (dp[h] - jnp.sum(pf * dp[h], axis=-1, keepdims=True))).astype(BF))
            stage.append((k, lanes, q, key, dh, p, ds))
        done = []
        scale = HD ** (-0.5)
        for k, lanes, q, key, dh, p, ds in stage:
            dq, dk, dv = [dot(one, key) for one in ds], [dot_tn(one, q) for one in ds], [dot_tn(one, dh) for one in p]
            done.append((k, lanes[0], jnp.where(first, dq[0], dq[1]) * scale))
            done.append((k, lanes[1], jnp.where(first, dk[0], dk[1]) * scale))
            done.append((k, lanes[2], jnp.where(first, dv[0], dv[1])))
        for k, here, value in done:
            qkv[k, rows, here] = value.astype(BF)

    during = [
        woven(grad_events(DOWN, 12, 16), outs[7:9]),
        woven(grad_events(UP, 0, 3), outs[9:]),
        grad_events(UP, 3, 5),
    ]
    backs = []
    for at, (i, start, count) in enumerate(spans):
        rows = pl.ds(start, count)
        looped(
            2,
            lambda n: attention_back(i, rows, [n * pairs + j for j in range(pairs)]),
            during[at] if at < 3 else [],
        )

        def back_first(n):
            span = pl.ds(pl.multiple_of(n * 256, 256), 256)
            both = pl.ds(0, 3 * half)
            mid[rows, span] = dot_nt(qkv[0, rows, both], w[0, 0, span, both]) + dot_nt(
                qkv[1, rows, both], w[0, 1, span, both]
            )

        looped(feat // 256, back_first)

        def norm_one_back(n):
            here = pl.ds(pl.multiple_of(start + n * block, block), block)
            e = mid[here, :]
            xhat, r = normed(x[here, :].astype(F32))
            back_in = acc[here, :] + norm_back(e, xhat, r, vec(0))
            n2[here, :] = back_in.astype(BF)
            vgrad[0:1, :] += jnp.sum(e * xhat, axis=0, keepdims=True)
            vgrad[1:2, :] += jnp.sum(e, axis=0, keepdims=True)

        looped(count // block, norm_one_back)
        mine = [row_event(1, n) for n in range(start // 64, (start + count) // 64)]
        mine[0]()
        backs += mine[1:]

    def grad_qkv(i):
        k, c = i // 3, i % 3
        span = pl.ds(pl.multiple_of(c * half, half), half)
        w[0, k, :, span] = dot_tn(n1[...], qkv[k, :, span]).astype(BF)

    looped(6, grad_qkv, woven(grad_events(UP, 5, 8), backs[:2]))

    def cut_small():
        low = lax.broadcasted_iota(jnp.int32, (8, 128), 1)
        row = lax.broadcasted_iota(jnp.int32, (8, 128), 0)
        for at in range(feat // 48):
            value = vgrad[...]
            if at:
                value = pltpu.roll(value, feat - at * 48, 1)
            value = jnp.where((low < 48) & (row < 6), value[:, :128], 0.0)
            for k in range(2):
                more = bgrad[k]
                if at:
                    more = pltpu.roll(more, wide - at * 96, 1)
                small_abs_sum[k, at] = value + jnp.where((low < 96) & (row == 6), more[:, :128], 0.0)
        for code in range(32):
            pd, pt = small_place(code)
            small_sum[code] = small_abs_sum[pt, pd]

    small_abs_sum = small_in[1]
    small_got = small_in[0]

    def sum_move(k):
        return pltpu.make_async_remote_copy(
            small_sum.at[pl.ds(2**k, 2**k)],
            small_got.at[pl.ds(2**k, 2**k)],
            s_sem.at[2, k],
            s_sem.at[3, k],
            device_id=small_place(2**k),
            device_id_type=MESH,
        )

    def sum_step(k):
        def go():
            if k < 4:
                sum_move(k + 1).wait()
                here = pl.ds(0, 2 ** (k + 1))
                small_sum[here] = small_sum[here] + small_got[pl.ds(2 ** (k + 1), 2 ** (k + 1))]
            if k >= 0:
                sum_move(k).start()

        return go

    if linked:
        link.grads_to_core(QKV)
        cut_small()
        sums = [sum_step(k) for k in range(4, -2, -1)]
        first_half = woven(grad_events(UP, 8, 16), grad_events(OUT, 0, 12), grad_events(QKV, 0, 5), sums[:3], backs[2:5])
        second = woven(grad_events(OUT, 12, 16) + grad_events(QKV, 5, 16), sums[3:], backs[5:])
        for event in first_half + second:
            event()
        vshare[...] = small_sum[0]
        for n in range(4):
            link.grads_sent(n)
    else:
        for event in backs:
            event()
        saves = []
        for g in range(3):
            for k in range(2):
                source = gd.at[k] if g == 2 else w.at[g, k]
                saves.append(pltpu.make_async_copy(source, share.at[g, k], own.at[g, k]))
        for copy in saves:
            copy.start()
        for copy in saves:
            copy.wait()
        vshare[pl.ds(0, 8), pl.ds(0, feat)] = vgrad[...]
        for k in range(2):
            vshare[pl.ds(8 + 8 * k, 8), :] = bgrad[k]
    for kind, ref in enumerate((out_rows, n2)):
        pltpu.make_async_copy(ref, ref, o_sem.at[0, kind]).wait()
        if linked:
            pltpu.make_async_remote_copy(
                ref, ref, o_sem.at[1, kind], o_sem.at[2, kind], device_id=link.place(Y), device_id_type=MESH
            ).wait()


VLIM = 60


def run_layer(linked, big, small, bvis, svis, bcot, scot, weights, parts, wide):
    nb, bl = bvis.shape[0] // parts, bvis.shape[1]
    ns, sl = svis.shape[0] // parts, svis.shape[1]
    tokens = nb * bl + ns * sl
    feat = big.shape[2]
    tile = wide // 3
    tiles = 6
    pairs = feat // 128
    rows = weights[0].shape[0] if linked else 48
    vm, hbm = pl.BlockSpec(memory_space=pltpu.VMEM), pl.BlockSpec(memory_space=pl.ANY)
    pair = (2, tokens, feat) if linked else (tokens, feat)
    dma = pltpu.SemaphoreType.DMA
    link = (lambda *shape: pltpu.VMEM(shape, BF)) if linked else (lambda *shape: pltpu.VMEM((16, 128), BF))
    loads = nb * (big.shape[1] // 512) + ns
    return pl.pallas_call(
        functools.partial(layer_kernel, (nb, bl, ns, sl), linked),
        out_shape=(
            jax.ShapeDtypeStruct(pair, BF),
            jax.ShapeDtypeStruct(pair, BF),
            jax.ShapeDtypeStruct((3, rows, wide) if linked else weights[0].shape, F32 if linked else BF),
            jax.ShapeDtypeStruct((8, 128) if linked else (24, wide), F32),
        ),
        in_specs=[hbm, hbm, vm, vm, hbm, hbm] + ([vm, hbm, hbm, vm, vm] if linked else [hbm, vm, vm]),
        out_specs=(hbm, hbm, vm if linked else hbm, vm),
        scratch_shapes=[
            pltpu.VMEM((16, 128), F32),
            pltpu.VMEM((3, 2, feat, wide), BF),
            pltpu.VMEM((2, feat, wide), BF),
            link(3, 16, rows, wide),
            link(3, 15, rows, wide),
            pltpu.VMEM((tokens, feat), BF),
            pltpu.VMEM((tokens, feat), BF),
            pltpu.VMEM((tokens, feat), BF),
            pltpu.VMEM((2, tokens, 3 * feat // 2), BF),
            pltpu.VMEM((pairs, nb, 2, bl, bl), BF),
            pltpu.VMEM((pairs, 2, ns * sl, ns * sl), BF),
            pltpu.VMEM((tokens, feat), BF),
            pltpu.VMEM((tokens, feat), F32),
            pltpu.VMEM((tokens, feat), F32),
            pltpu.VMEM((tiles, tokens, tile), BF),
            pltpu.VMEM((tiles, tokens, tile), BF),
            pltpu.VMEM((tokens, feat), BF),
            pltpu.VMEM((tokens, feat), BF),
            pltpu.VMEM((8, feat), F32),
            pltpu.VMEM((2, 8, wide), F32),
            pltpu.VMEM((8, feat), F32),
            pltpu.VMEM((2, 8, wide), F32),
            pltpu.VMEM((32, 16, 128), BF),
            pltpu.VMEM((2, 16, 16, 128), BF),
            pltpu.VMEM((32, 8, 128), F32),
            [pltpu.VMEM((32, 8, 128), F32), pltpu.VMEM((2, 16, 8, 128), F32)],
            dma((3,)),
            dma((3, 16)),
            dma((3,)),
            dma((3,)),
            dma((4,)),
            dma((4, 2, 15)),
            dma((4,)),
            dma((4, 16)),
            dma((3, 2)),
            dma((loads, 2)),
            dma,
            dma((3, 2)),
            dma((4, 5)),
        ],
        compiler_params=pltpu.CompilerParams(
            collective_id=0 if linked else None, has_side_effects=linked, vmem_limit_bytes=VLIM * MIB
        ),
        name="layer",
    )(big, small, bvis, svis, bcot, scot, *weights)


def adam_step(weight, moment_one, moment_two, gradient, step_rate, decay_rate):
    moment_one = 0.9 * moment_one + 0.1 * gradient
    moment_two = 0.999 * moment_two + 0.001 * gradient * gradient
    fixed_one = moment_one / (1.0 - 0.9**STEP_NUMBER)
    fixed_two = moment_two / (1.0 - 0.999**STEP_NUMBER)
    update = fixed_one / (jnp.sqrt(fixed_two) + 1e-08) + decay_rate * weight
    return (weight - step_rate * update, moment_one, moment_two)


def finish_kernel(bvis_ref, svis_ref, orow_ref, osmall_ref, brow_ref, bsmall_ref, share_ref, few_ref, *refs):
    states, (bout_ref, sout_ref, big_ref, small_ref), new = refs[:18], refs[18:22], refs[22:]
    i = pl.program_id(0)

    def spread(vis, rows, length):
        hot = lax.broadcasted_iota(jnp.int32, (length, vis.shape[1]), 0) == vis
        return dot(hot.astype(BF), rows)

    bout_ref[...] = orow_ref[...]
    sout_ref[...] = osmall_ref[...]
    big_ref[...] = spread(bvis_ref[pl.ds(i, 1), :], brow_ref[...], big_ref.shape[0])
    small_ref[...] = spread(svis_ref[pl.ds(i, 1), :], bsmall_ref[...], small_ref.shape[0])

    def update(at, gradient, where=...):
        old = [ref[where] for ref in states[3 * at : 3 * at + 3]]
        for ref, value in zip(new[3 * at :], adam_step(*old, gradient, LEARN_RATES[at], DECAYS[at])):
            ref[where] = value

    half = states[3].shape[1]

    @pl.when(i == 0)
    def _():
        update(2, share_ref[1])

    @pl.when(i == 1)
    def _():
        update(3, share_ref[2])

    @pl.when(i == 2)
    def _():
        for c in range(3):
            update(0, share_ref[0, :, c * half : (c + 1) * half], (slice(None), c, slice(None)))

    @pl.when(i == 3)
    def _():
        update(1, share_ref[0, :, 3 * half :])
        update(4, few_ref[6:7, : states[12].shape[1]])
        update(5, few_ref[:6, : states[15].shape[1]])


def finish(bvis, svis, outs, backs, share, few, states, big_len, small_len):
    parts, _, feat = outs.shape
    nb, bl = bvis.shape
    ns, sl = svis.shape
    each = nb // parts
    first_small = each * bl // sl
    vm = pl.BlockSpec(memory_space=pltpu.VMEM)
    rows = [
        pl.BlockSpec((None, bl, feat), lambda i: (lax.div(i, each), lax.rem(i, each), 0)),
        pl.BlockSpec((None, sl, feat), lambda i: (lax.div(i, each), first_small + lax.rem(i, each), 0)),
    ]
    whole = [pl.BlockSpec(one.shape, lambda i, n=one.ndim: (0,) * n) for one in (share, few, *states)]

    def chip(length):
        return pl.BlockSpec((None, length, feat), lambda i: (i, 0, 0))

    return pl.pallas_call(
        finish_kernel,
        grid=(nb,),
        out_shape=(
            jax.ShapeDtypeStruct((nb, bl, feat), BF),
            jax.ShapeDtypeStruct((ns, sl, feat), BF),
            jax.ShapeDtypeStruct((nb, big_len, feat), F32),
            jax.ShapeDtypeStruct((ns, small_len, feat), F32),
            *(jax.ShapeDtypeStruct(one.shape, F32) for one in states),
        ),
        in_specs=[vm, vm] + rows + rows + whole,
        out_specs=(chip(bl), chip(sl), chip(big_len), chip(small_len), *whole[2:]),
        compiler_params=pltpu.CompilerParams(vmem_limit_bytes=48 * MIB),
        name="finish",
    )(bvis, svis, outs, outs, backs, backs, share, few, *states)


def on_device(
    special,
    big_patches, small_patches, big_visible, small_visible, big_cot, small_cot,
    qkv_weight, qkv_first, qkv_second, out_weight, out_first, out_second,
    up_weight, up_first, up_second, down_weight, down_first, down_second,
    up_bias, up_bias_first, up_bias_second, norm_vectors, norm_first, norm_second,
):
    rows, half = out_weight.shape
    wide = up_weight.shape[1]
    feat = big_patches.shape[2]
    parts = feat // half
    chips = (big_patches, small_patches, big_visible, small_visible, big_cot, small_cot)
    attn = jnp.concatenate([qkv_weight.reshape(rows, 3 * half), out_weight], axis=1).astype(BF)
    if special:
        weights = (attn, up_weight, down_weight, norm_vectors, up_bias)
        outs, backs, share, few = run_layer(True, *chips, weights, parts, wide)
    else:
        piece = jnp.stack([attn, up_weight.astype(BF), down_weight.astype(BF)])
        w = lax.all_gather(lax.all_gather(piece, "dp", axis=1, tiled=True), "tensor", axis=1)
        vectors = lax.all_gather(norm_vectors.astype(BF), "dp", axis=1, tiled=True).astype(F32)
        bias = lax.all_gather(up_bias.astype(BF), "dp", axis=1, tiled=True)
        bias = lax.all_gather(bias, "tensor", axis=0).astype(F32)
        weights = (w, jnp.pad(vectors, ((0, 2), (0, 0))), jnp.pad(bias, ((0, 0), (6, 1), (0, 0))))
        out_rows, back_rows, grads, few = run_layer(False, *chips, weights, parts, wide)
        share = lax.psum_scatter(grads, "tensor", scatter_dimension=1)
        share = lax.psum_scatter(share, "dp", scatter_dimension=1, tiled=True).astype(F32)
        both = lax.all_gather(jnp.stack([out_rows, back_rows]), "tensor", axis=1)
        outs, backs = both[0], both[1]
        norm_share = lax.psum_scatter(lax.psum(few[:6, :feat], "tensor"), "dp", scatter_dimension=1, tiled=True)
        bias_share = lax.psum_scatter(few[14::8], "tensor", scatter_dimension=0, tiled=True)
        bias_share = lax.psum_scatter(bias_share, "dp", scatter_dimension=1, tiled=True)
        few = jnp.concatenate(
            [
                jnp.pad(norm_share, ((0, 0), (0, 128 - norm_share.shape[1]))),
                jnp.pad(bias_share, ((0, 1), (0, 128 - bias_share.shape[1]))),
            ]
        )
    states = (
        qkv_weight, qkv_first, qkv_second, out_weight, out_first, out_second,
        up_weight, up_first, up_second, down_weight, down_first, down_second,
        up_bias, up_bias_first, up_bias_second, norm_vectors, norm_first, norm_second,
    )
    return finish(
        big_visible, small_visible, outs, backs, share, few, states, big_patches.shape[1], small_patches.shape[1]
    )


def solution(mesh):
    special = mesh.shape["dp"] == 16 and mesh.shape["tensor"] == 2
    chips = P("dp", None, None)
    matrix, qkv = P("dp", "tensor"), P("dp", None, "tensor")
    states = (qkv,) * 3 + (matrix,) * 9 + (P("tensor", "dp"),) * 3 + (P(None, "dp"),) * 3
    return jax.shard_map(
        functools.partial(on_device, special),
        mesh=mesh,
        in_specs=(chips, chips, P("dp", None), P("dp", None), chips, chips) + states,
        out_specs=(chips,) * 4 + states,
        check_vma=False,
    )
```

```python
import functools

import jax
import jax.numpy as jnp
from jax import lax
from jax.experimental import pallas as pl
from jax.experimental.pallas import tpu as pltpu
from jax.sharding import PartitionSpec as P

HD = 64
STEP_NUMBER = 10
BF, F32 = jnp.bfloat16, jnp.float32
MESH = pl.DeviceIdType.MESH
MIB = 2**20

LEARN_RATES = (0.03, 0.1, 0.03, 0.015, 0.2, 0.2)
DECAYS = (0.05, 0.05, 0.05, 0.05, 0.0, 0.0)

Z1, Z2, X, Y = 1, 2, 4, 8
DIMS = (Z1, Z2, X, Y)
def place(code, other_core=False):
    d, t = lax.axis_index("dp"), lax.axis_index("tensor")
    z, x, c = lax.div(d, 4), lax.rem(lax.div(d, 2), 2), lax.rem(d, 2)
    if code & Z1:
        z = z + 1 - 2 * lax.rem(z, 2)
    if code & Z2:
        z = z + 2 - 4 * lax.div(z, 2)
    if code & X:
        x = 1 - x
    if code & Y:
        t = 1 - t
    if other_core:
        c = 1 - c
    return z * 4 + x * 2 + c, t


def greet(place):
    barrier = pltpu.get_barrier_semaphore()
    for dim in DIMS:
        pl.semaphore_signal(barrier, inc=1, device_id=place(dim), device_id_type=MESH)
    pl.semaphore_signal(barrier, inc=1, device_id=place(0, True), device_id_type=MESH)


def await_greetings():
    pl.semaphore_wait(pltpu.get_barrier_semaphore(), 5)


def bits(code):
    return bin(code).count("1")


def top_of(order, code):
    return max([order.index(k) for k in DIMS if code & k], default=-1)


def dot(a, b):
    return jnp.dot(a, b, preferred_element_type=F32)


def dot_nt(a, b):
    return lax.dot_general(a, b, (((1,), (1,)), ((), ())), preferred_element_type=F32)


def dot_tn(a, b):
    return lax.dot_general(a, b, (((0,), (0,)), ((), ())), preferred_element_type=F32)


def normed(v):
    centred = v - jnp.mean(v, axis=-1, keepdims=True)
    r = lax.rsqrt(jnp.mean(centred * centred, axis=-1, keepdims=True) + 1e-05)
    return centred * r, r


def norm_back(e, xhat, r, gain):
    eg = e * gain
    return r * (eg - jnp.mean(eg, axis=-1, keepdims=True) - xhat * jnp.mean(eg * xhat, axis=-1, keepdims=True))


def column_of(row):
    wide = jnp.broadcast_to(row.astype(F32), (128, row.shape[1]))
    return jnp.transpose(wide).astype(jnp.int32)


T, PP, Q, R = (Z2, Z1, X, Y), (Z2, Z1, Y, X), (Z2, Y, X, Z1), (Y, Z2, X, Z1)
GATHER_ORDERS = ((T, PP), (T, PP), (T, PP))
AHEAD = 2
DOWN, UP, OUT, QKV = range(4)
SUMS = (
    (2, ((PP, 0, 768), (R, 768, 768))),
    (1, ((PP, 0, 768), (R, 768, 768))),
    (0, ((PP, 1152, 256), (R, 1408, 128))),
    (0, ((PP, 0, 512), (R, 512, 640))),
)
SLOTS = {}
for _order in (T, PP, Q, R):
    SLOTS[_order] = {}
    for _at, _dim in enumerate(_order):
        for _code in range(16):
            if top_of(_order, _code) < _at:
                SLOTS[_order][_code, _dim] = len(SLOTS[_order])
RISING = sorted(range(1, 16), key=bits)
FALLING = sorted(range(16), key=lambda code: -bits(code))


def cut_columns(orders, cols):
    width = cols // len(orders)
    return [(order, pl.ds(at * width, width)) for at, order in enumerate(orders)]


class Links:
    def __init__(self, rows, w, gd, from_core, from_chip, share, sems):
        self.w, self.gd = w, gd
        self.from_core, self.from_chip, self.share = from_core, from_chip, share
        (
            self.asend, self.arecv, self.acsend, self.acrecv,
            self.rsend, self.rrecv, self.rcsend, self.rcrecv,
        ) = sems
        self.rows, self.cols = rows, w.shape[3]

        self.places = {(code, core): place(code, core) for code in range(16) for core in (False, True)}
        self.spans = {at: pl.ds(pl.multiple_of(d * self.rows, self.rows), self.rows) for at, (d, _) in self.places.items()}

    def place(self, code, core=False):
        return self.places[code, core]

    def at(self, code, core=False):
        return self.places[code, core][1], self.spans[code, core]

    def weight_move(self, g, part, code, dim):
        span = cut_columns(GATHER_ORDERS[g], self.cols)[part][1]
        target = self.w.at[(g,) + self.at(code) + (span,)]
        return pltpu.make_async_remote_copy(
            target,
            target,
            self.asend.at[g],
            self.arecv.at[g, code ^ dim],
            device_id=self.place(dim),
            device_id_type=MESH,
        )

    def weight_core_move(self, g, code, mine=True):
        target = self.w.at[(g,) + self.at(code, not mine)]
        return pltpu.make_async_remote_copy(
            target,
            target,
            self.acsend.at[g],
            self.acrecv.at[g],
            device_id=self.place(0, True),
            device_id_type=MESH,
        )

    def weight_forward(self, g, code):
        if code:
            target = self.w.at[(g,) + self.at(code)]
            pltpu.make_async_remote_copy(
                target, target, self.asend.at[g], self.arecv.at[g, code], device_id=self.place(Z1), device_id_type=MESH
            ).wait_recv()
        for part, order in enumerate(GATHER_ORDERS[g]):
            for dim in order[top_of(order, code) + 1 :]:
                self.weight_move(g, part, code, dim).start()
        self.weight_core_move(g, code).start()

    def weights_complete(self, g):
        target = self.w.at[g, 0]
        pltpu.make_async_remote_copy(
            target, target, self.acsend.at[g], self.acrecv.at[g], device_id=self.place(0, True), device_id_type=MESH
        ).wait_recv()

    def weights_sent(self, g):
        for ref, send, recv in (
            (self.from_chip.at[g], self.asend.at[g], self.arecv.at[g, 1]),
            (self.from_core.at[g], self.acsend.at[g], self.acrecv.at[g]),
        ):
            pltpu.make_async_remote_copy(
                ref, ref, send, recv, device_id=self.place(0, True), device_id_type=MESH
            ).wait_send()

    def grad(self, n, code, core, start, width):
        g = SUMS[n][0]
        where = self.at(code, core) + (pl.ds(start, width),)
        return (self.gd, where) if g == 2 else (self.w, (g,) + where)

    def grad_core_move(self, n, code):
        g, parts = SUMS[n]
        start, width = parts[0][1], sum(part[2] for part in parts)
        ref, where = self.grad(n, code, True, start, width)
        return pltpu.make_async_remote_copy(
            ref.at[where],
            self.from_core.at[g, code, :, pl.ds(start, width)],
            self.rcsend.at[n],
            self.rcrecv.at[n, code],
            device_id=self.place(0, True),
            device_id_type=MESH,
        )

    def grad_move(self, n, part, code, dim, sending):
        g, parts = SUMS[n]
        order, start, width = parts[part]
        ref, where = self.grad(n, code, False, start, width)
        slot = SLOTS[order][code ^ dim if sending else code, dim]
        return pltpu.make_async_remote_copy(
            ref.at[where],
            self.from_chip.at[g, slot, :, pl.ds(start, width)],
            self.rsend.at[n],
            self.rrecv.at[n, part, slot],
            device_id=self.place(dim),
            device_id_type=MESH,
        )

    def grads_to_core(self, n):
        for code in FALLING:
            self.grad_core_move(n, code).start()

    def grad_step(self, n, code):
        g, parts = SUMS[n]
        self.grad_core_move(n, code).wait_recv()
        for part, (order, start, width) in enumerate(parts):
            at = top_of(order, code)
            span = pl.ds(start, width)
            ref, where = self.grad(n, code, False, start, width)
            value = ref[where].astype(F32) + self.from_core[g, code, :, span].astype(F32)
            for dim in reversed(order[at + 1 :]):
                self.grad_move(n, part, code, dim, False).wait_recv()
                value = value + self.from_chip[g, SLOTS[order][code, dim], :, span].astype(F32)
            if code == 0:
                self.share[g, :, span] = value
            else:
                ref[where] = value.astype(BF)
                self.grad_move(n, part, code, order[at], True).start()

    def grads_sent(self, n):
        g, parts = SUMS[n]
        span = pl.ds(parts[0][1], sum(part[2] for part in parts))
        for ref, send, recv in (
            (self.from_chip.at[g, :, :, span], self.rsend.at[n], self.rrecv.at[n, 0, 0]),
            (self.from_core.at[g, :, :, span], self.rcsend.at[n], self.rcrecv.at[n, 0]),
        ):
            pltpu.make_async_remote_copy(
                ref, ref, send, recv, device_id=self.place(0, True), device_id_type=MESH
            ).wait_send()


def looped(count, body, events=()):
    events = list(events)

    @pl.loop(0, count)
    def _(i):
        body(i)
        for at in range(count):
            mine = events[len(events) * at // count : len(events) * (at + 1) // count]
            if mine:

                @pl.when(i == at)
                def _():
                    for event in mine:
                        event()


def layer_kernel(
    shape,
    linked,
    big_ref, small_ref, bvis_ref, svis_ref, bcot_ref, scot_ref, *refs,
):
    if linked:
        qkv_ref, mix_ref, up_ref, down_ref, norm_ref, up_bias_ref, *refs = refs
    else:
        w_ref, vec_ref, bias_ref, *refs = refs
    run_kernel(
        shape, linked, big_ref, small_ref, bvis_ref, svis_ref, bcot_ref, scot_ref,
        (qkv_ref, mix_ref, up_ref, down_ref, norm_ref, up_bias_ref) if linked else (w_ref, vec_ref, bias_ref), *refs,
    )


def run_kernel(
    shape,
    linked,
    big_ref, small_ref, bvis_ref, svis_ref, bcot_ref, scot_ref, weight_refs,
    out_ref, back_ref, share, vshare,
    few, w, gd, from_core, from_chip, x, n1, n2, qkv, prob, prob_small, heads, mid, acc, act, slope, cot, out_rows,
    vecs, bias, vgrad, bgrad, small, small_abs, small_sum, small_in,
    asend, arecv, acsend, acrecv, rsend, rrecv, rcsend, rcrecv, own, p_sem, c_sem, o_sem, s_sem,
):
    nb, bl, ns, sl = shape
    feat, wide = w.shape[2:]
    cut = nb * bl
    tokens = cut + ns * sl
    half = feat // 2
    pairs = half // 128
    d, t = lax.axis_index("dp"), lax.axis_index("tensor")
    block = 128
    steps = tokens // block
    tile = act.shape[2]
    tiles = act.shape[0]
    per = tiles // 2
    small_rows = ns * sl
    spans = [(i, i * bl, bl) for i in range(nb)] + [(nb, cut, small_rows)]
    chunk = 512
    strips = [(at, min(tile, feat - at)) for at in range(0, feat, tile)]

    cloads = [
        pltpu.make_async_copy(bcot_ref.at[t * nb + i], cot.at[pl.ds(i * bl, bl)], c_sem) for i in range(nb)
    ]
    cloads += [
        pltpu.make_async_copy(scot_ref.at[t * ns + i], cot.at[pl.ds(cut + i * sl, sl)], c_sem)
        for i in range(ns)
    ]
    big_len, small_len = big_ref.shape[1], small_ref.shape[1]
    ploads = []
    for i in range(nb):
        for at in range(big_len // chunk):
            source = big_ref.at[t * nb + i, pl.ds(at * chunk, chunk)]
            ploads.append((i, at, source, chunk, (bvis_ref, t * nb + i, i * bl, bl)))
    for i in range(ns):
        ploads.append((nb + i, 0, small_ref.at[t * ns + i], small_len, (svis_ref, t * ns + i, cut + i * sl, sl)))

    def pload(at):
        _, _, source, length, _ = ploads[at]
        return [
            pltpu.make_async_copy(
                source.at[:, pl.ds(start, width)],
                act.at[at % 2 * len(strips) + c, pl.ds(0, length), pl.ds(0, width)],
                p_sem.at[at, c],
            )
            for c, (start, width) in enumerate(strips)
        ]

    for copy in pload(0):
        copy.start()
    for copy in cloads:
        copy.start()

    if linked:
        qkv_ref, mix_ref, up_ref, down_ref, norm_ref, up_bias_ref = weight_refs
        greet(place)
        stage = [
            pltpu.make_async_copy(ref, share.at[g], own.at[g, 0]) for g, ref in ((1, up_ref), (2, down_ref))
        ]
        heads_in = [
            pltpu.make_async_copy(qkv_ref.at[c], share.at[0, :, pl.ds(c * half, half)], own.at[0, c % 2]) for c in range(3)
        ]
        heads_in.append(pltpu.make_async_copy(mix_ref, share.at[0, :, pl.ds(3 * half, half)], own.at[0, 1]))
        for copy in heads_in + stage:
            copy.start()
        few[...] = jnp.zeros_like(few)
        few[: norm_ref.shape[0], : norm_ref.shape[1]] = norm_ref[...]
        few[6:7, : up_bias_ref.shape[1]] = up_bias_ref[...]
        link = Links(
            mix_ref.shape[0], w, gd, from_core, from_chip, share,
            (asend, arecv, acsend, acrecv, rsend, rrecv, rcsend, rcrecv),
        )
        for k in range(2):
            both = share.at[0, :, pl.ds(0, 2 * half)]
            pltpu.make_async_copy(both, both, own.at[0, k]).wait()
        w[(0,) + link.at(0)] = share[0].astype(BF)
        for g in (1, 2):
            stage[g - 1].wait()
            w[(g,) + link.at(0)] = share[g].astype(BF)

        def small_place(code):
            return link.place(code >> 1, bool(code & 1))

        small[0] = few[...].astype(BF)
        await_greetings()
    else:
        w_ref, vec_ref, bias_ref = weight_refs
        wloads = [
            [pltpu.make_async_copy(w_ref.at[g, k], w.at[g, k], own.at[g, k]) for k in range(2)] for g in range(3)
        ]
        for copy in sum(wloads, []):
            copy.start()

    def small_move(k):
        return pltpu.make_async_remote_copy(
            small.at[pl.ds(0, 2**k)],
            small.at[pl.ds(2**k, 2**k)],
            s_sem.at[0, k],
            s_sem.at[1, k],
            device_id=small_place(2**k),
            device_id_type=MESH,
        )

    def small_step(k):
        def go():
            if k:
                small_move(k - 1).wait()
            if k < 5:
                small_move(k).start()

        return go

    def set_vectors():
        for code in range(32):
            pd, pt = small_place(code)
            small_abs[pt, pd] = small[code]
        vec_sum, bias_sum = 0.0, [0.0, 0.0]
        parts = feat // 48 if linked else 0
        for at in range(parts):
            for k in range(2):
                value = small_abs[k, at].astype(F32)
                if k == 0:
                    padded = jnp.concatenate([value, jnp.zeros((16, feat - 128), F32)], axis=1)
                    vec_sum = vec_sum + (pltpu.roll(padded, at * 48, 1) if at else padded)
                padded = jnp.concatenate([value[:8], jnp.zeros((8, wide - 128), F32)], axis=1)
                bias_sum[k] = bias_sum[k] + (pltpu.roll(padded, at * 96, 1) if at else padded)
        vecs[...] = vec_sum[:8]
        for k in range(2):
            bias[k] = bias_sum[k]

    def vec(i):
        return vecs[i : i + 1, :]

    def rows_of(i):
        return pl.ds(pl.multiple_of(i * block, block), block)

    def pick(at):
        def go():
            chip, part, _, length, (vis_ref, row, first_row, count) = ploads[at]
            for copy in pload(at):
                copy.wait()
            if at + 1 < len(ploads):
                for copy in pload(at + 1):
                    copy.start()
            column = column_of(vis_ref[pl.ds(row, 1), :]) - part * length
            lane = lax.broadcasted_iota(jnp.int32, column.shape, 1)
            hot = jnp.concatenate([(column == lane + k * 128).astype(BF) for k in range(length // 128)], axis=1)
            rows = pl.ds(first_row, count)
            for c, (start, width) in enumerate(strips):
                picked = dot(hot, act[at % 2 * len(strips) + c, :length, :width])
                span = pl.ds(start, width)
                if part:
                    picked = picked + x[rows, span].astype(F32)
                x[rows, span] = picked.astype(BF)

        return go

    picks = [pick(at) for at in range(len(ploads))]

    def weight_event(g, code):
        return lambda: link.weight_forward(g, code)

    if linked:
        order = sorted(
            [(bits(code) + AHEAD * g, g, n, code) for g in range(3) for n, code in enumerate([0] + RISING)]
        )
        sequence = [(g, weight_event(g, code)) for _, g, _, code in order]
        last = [max(i for i, (g, _) in enumerate(sequence) if g == k) for k in range(3)]
        weight_events = [[e for _, e in sequence[lo : hi + 1]] for lo, hi in zip([0] + [i + 1 for i in last], last)]
        smalls = [small_step(k) for k in range(6)]
        mixed = [weight_events[0][0], smalls[0], picks[0], picks[1]] + weight_events[0][1:3] + [smalls[1], picks[2]]
        mixed += weight_events[0][3:5] + [picks[3], smalls[2]] + weight_events[0][5:8] + [picks[4], smalls[3]]
        mixed += weight_events[0][8:11] + picks[5:] + [smalls[4]] + weight_events[0][11:14] + [smalls[5]]
        mixed += weight_events[0][14:]
        for event in mixed:
            event()
        set_vectors()
    else:
        weight_events = [[], [], []]
        for event in picks:
            event()
        vecs[...] = vec_ref[...]
        bias[...] = bias_ref[...]

    def weights_ready(g):
        if linked:
            link.weights_complete(g)
        else:
            for copy in wloads[g]:
                copy.wait()

    def norm_one(i):
        xhat, r = normed(x[rows_of(i), :].astype(F32))
        value = xhat * vec(0) + vec(1)
        n1[rows_of(i), :] = value.astype(BF)

    looped(steps, norm_one)
    weights_ready(0)
    events = weight_events[1]
    lot = len(events) // 3

    def make_qkv(i):
        k, c = i // 3, i % 3
        span = pl.ds(pl.multiple_of(c * half, half), half)
        qkv[k, :, span] = dot(n1[...], w[0, k, :, span]).astype(BF)

    looped(6, make_qkv, events[:lot])

    lane = lax.broadcasted_iota(jnp.int32, (1, 128), 1)
    first = lane < HD
    zero = jnp.zeros((), BF)

    def softmax(scores):
        e = jnp.exp(scores - jnp.max(scores, axis=-1, keepdims=True))
        return e / jnp.sum(e, axis=-1, keepdims=True)

    same = (
        lax.broadcasted_iota(jnp.int32, (small_rows, small_rows), 0) // sl
        == lax.broadcasted_iota(jnp.int32, (small_rows, small_rows), 1) // sl
    )

    def pair_spans(pair):
        k, j = pair // pairs, pair % pairs
        return k, [pl.ds(pl.multiple_of(c * half + j * 128, 128), 128) for c in range(3)]

    def attention(pair):
        k, lanes = pair_spans(pair)
        for i, start, count in spans:
            rows = pl.ds(start, count)
            q, key, value = (qkv[k, rows, lanes[c]] for c in range(3))
            mixed = []
            for h in range(2):
                q_head = jnp.where(first if h == 0 else ~first, q, zero)
                scores = dot_nt(q_head, key) * HD ** (-0.5)
                if i == nb:
                    scores = jnp.where(same, scores, -jnp.inf)
                p = softmax(scores).astype(BF)
                if i == nb:
                    prob_small[pair, h] = p
                else:
                    prob[pair, i, h] = p
                mixed.append(dot(p, value))
            heads[rows, pl.ds(pl.multiple_of(pair * 128, 128), 128)] = jnp.where(first, mixed[0], mixed[1]).astype(BF)

    looped(2 * pairs, attention, events[lot:])

    out_span = pl.ds(3 * half, half)

    def project(i):
        span = pl.ds(pl.multiple_of(i * 256, 256), 256)
        mid[:, span] = dot_nt(heads[:, :half], w[0, 0, span, out_span]) + dot_nt(heads[:, half:], w[0, 1, span, out_span])

    looped(feat // 256, project)

    def norm_two(i):
        middle = x[rows_of(i), :].astype(F32) + mid[rows_of(i), :] + vec(4)
        mid[rows_of(i), :] = middle
        xhat, r = normed(middle)
        value = xhat * vec(2) + vec(3)
        n2[rows_of(i), :] = value.astype(BF)
        acc[rows_of(i), :] = middle + vec(5)

    looped(steps, norm_two)
    pltpu.make_async_copy(cot, cot, c_sem).wait()

    weights_ready(1)
    events = weight_events[2]
    lot = len(events) * 2 // 3

    def grad_events(n, lo, hi):
        if not linked:
            return []
        return [functools.partial(link.grad_step, n, code) for code in FALLING[lo:hi]]

    def woven(*lists):
        keyed = [((n + 0.5) / len(events), at, event) for at, events in enumerate(lists) for n, event in enumerate(events)]
        return [event for _, _, event in sorted(keyed, key=lambda one: one[:2])]

    def tile_of(i):
        return i // per, pl.ds(pl.multiple_of((i % per) * tile, tile), tile)

    def up(i):
        at, here = i // 2, pl.ds(pl.multiple_of(i % 2 * 256, 256), 256)
        k, span = at // per, pl.ds(pl.multiple_of(at % per * tile + i % 2 * 256, 256), 256)
        pre = dot(n2[...], w[1, k, :, span]) + bias[k, 6:7, span]
        cdf = 0.5 * (1.0 + lax.erf(pre * 0.7071067811865476))
        act[at, :, here] = (pre * cdf).astype(BF)
        slope[at, :, here] = (cdf + pre * jnp.exp(-0.5 * pre * pre) * 0.3989422804014327).astype(BF)

    looped(tiles * 2, up, events[:lot])

    def grad_down(i):
        k, span = tile_of(i)
        gd[k, :, span] = dot_tn(cot[...], act[i]).astype(BF)

    looped(tiles, grad_down, events[lot:])
    if linked:
        link.grads_to_core(DOWN)
    weights_ready(2)

    def down(i):
        k, span = tile_of(i)
        acc[...] += dot_nt(act[i], w[2, k, :, span])

    looped(tiles, down, grad_events(DOWN, 0, 3))
    out_rows[...] = acc[...].astype(BF)

    def row_moves(kind, n):
        rows = pl.ds(n * 64, 64)
        source = (out_rows if kind == 0 else n2).at[rows]
        target = out_ref if kind == 0 else back_ref
        target = target.at[t, rows] if linked else target.at[rows]
        near = pltpu.make_async_copy(source, target, o_sem.at[0, kind])
        if not linked:
            return [near]
        far = pltpu.make_async_remote_copy(
            source, target, o_sem.at[1, kind], o_sem.at[2, kind], device_id=link.place(Y), device_id_type=MESH
        )
        return [near, far]

    def row_event(kind, n):
        def go():
            for move in row_moves(kind, n):
                move.start()

        return go

    outs = [row_event(0, n) for n in range(tokens // 64)]

    acc[...] = jnp.zeros_like(acc)
    if linked:
        for g in range(3):
            link.weights_sent(g)

    def back_up(i):
        k, span = tile_of(i)
        back = (slope[i].astype(F32) * dot(cot[...], w[2, k, :, span])).astype(BF)
        bgrad[k, 6:7, span] = jnp.sum(back.astype(F32), axis=0, keepdims=True)
        acc[...] += dot_nt(back, w[1, k, :, span])
        w[1, k, :, span] = dot_tn(n2[...], back).astype(BF)

    bgrad[...] = jnp.zeros_like(bgrad)
    looped(tiles, back_up, woven(grad_events(DOWN, 3, 9), outs[:5]))
    if linked:
        link.grads_to_core(UP)

    vgrad[...] = jnp.zeros_like(vgrad)

    def norm_two_back(i):
        e = acc[rows_of(i), :]
        xhat, r = normed(mid[rows_of(i), :])
        back_out = cot[rows_of(i), :].astype(F32)
        back_middle = back_out + norm_back(e, xhat, r, vec(2))
        acc[rows_of(i), :] = back_middle
        cot[rows_of(i), :] = back_middle.astype(BF)
        vgrad[2:3, :] += jnp.sum(e * xhat, axis=0, keepdims=True)
        vgrad[3:4, :] += jnp.sum(e, axis=0, keepdims=True)
        vgrad[4:5, :] += jnp.sum(back_middle, axis=0, keepdims=True)
        vgrad[5:6, :] += jnp.sum(back_out, axis=0, keepdims=True)

    looped(steps, norm_two_back, woven(grad_events(DOWN, 9, 12), outs[5:7]))

    dheads = heads
    for k in range(2):
        here = pl.ds(k * half, half)
        grad = dot_tn(cot[...], heads[:, here]).astype(BF)
        dheads[:, here] = dot(cot[...], w[0, k, :, out_span]).astype(BF)
        w[0, k, :, out_span] = grad

    if linked:
        link.grads_to_core(OUT)

    def attention_back(i, rows, some):
        stage = []
        for pair in some:
            k, lanes = pair_spans(pair)
            q, key, value = (qkv[k, rows, lanes[c]] for c in range(3))
            dh = dheads[rows, pl.ds(pl.multiple_of(pair * 128, 128), 128)]
            p = [prob_small[pair, h] if i == nb else prob[pair, i, h] for h in range(2)]
            dp = [dot_nt(jnp.where(first if h == 0 else ~first, dh, zero), value) for h in range(2)]
            ds = []
            for h in range(2):
                pf = p[h].astype(F32)
                ds.append((pf * (dp[h] - jnp.sum(pf * dp[h], axis=-1, keepdims=True))).astype(BF))
            stage.append((k, lanes, q, key, dh, p, ds))
        done = []
        scale = HD ** (-0.5)
        for k, lanes, q, key, dh, p, ds in stage:
            dq, dk, dv = [dot(one, key) for one in ds], [dot_tn(one, q) for one in ds], [dot_tn(one, dh) for one in p]
            done.append((k, lanes[0], jnp.where(first, dq[0], dq[1]) * scale))
            done.append((k, lanes[1], jnp.where(first, dk[0], dk[1]) * scale))
            done.append((k, lanes[2], jnp.where(first, dv[0], dv[1])))
        for k, here, value in done:
            qkv[k, rows, here] = value.astype(BF)

    during = [
        woven(grad_events(DOWN, 12, 16), outs[7:9]),
        woven(grad_events(UP, 0, 3), outs[9:]),
        grad_events(UP, 3, 5),
    ]
    backs = []
    for at, (i, start, count) in enumerate(spans):
        rows = pl.ds(start, count)
        looped(
            2,
            lambda n: attention_back(i, rows, [n * pairs + j for j in range(pairs)]),
            during[at] if at < 3 else [],
        )

        def back_first(n):
            span = pl.ds(pl.multiple_of(n * 256, 256), 256)
            both = pl.ds(0, 3 * half)
            mid[rows, span] = dot_nt(qkv[0, rows, both], w[0, 0, span, both]) + dot_nt(
                qkv[1, rows, both], w[0, 1, span, both]
            )

        looped(feat // 256, back_first)

        def norm_one_back(n):
            here = pl.ds(pl.multiple_of(start + n * block, block), block)
            e = mid[here, :]
            xhat, r = normed(x[here, :].astype(F32))
            back_in = acc[here, :] + norm_back(e, xhat, r, vec(0))
            n2[here, :] = back_in.astype(BF)
            vgrad[0:1, :] += jnp.sum(e * xhat, axis=0, keepdims=True)
            vgrad[1:2, :] += jnp.sum(e, axis=0, keepdims=True)

        looped(count // block, norm_one_back)
        mine = [row_event(1, n) for n in range(start // 64, (start + count) // 64)]
        mine[0]()
        backs += mine[1:]

    def grad_qkv(i):
        k, c = i // 3, i % 3
        span = pl.ds(pl.multiple_of(c * half, half), half)
        w[0, k, :, span] = dot_tn(n1[...], qkv[k, :, span]).astype(BF)

    looped(6, grad_qkv, woven(grad_events(UP, 5, 8), backs[:2]))

    def cut_small():
        low = lax.broadcasted_iota(jnp.int32, (8, 128), 1)
        row = lax.broadcasted_iota(jnp.int32, (8, 128), 0)
        for at in range(feat // 48):
            value = vgrad[...]
            if at:
                value = pltpu.roll(value, feat - at * 48, 1)
            value = jnp.where((low < 48) & (row < 6), value[:, :128], 0.0)
            for k in range(2):
                more = bgrad[k]
                if at:
                    more = pltpu.roll(more, wide - at * 96, 1)
                small_abs_sum[k, at] = value + jnp.where((low < 96) & (row == 6), more[:, :128], 0.0)
        for code in range(32):
            pd, pt = small_place(code)
            small_sum[code] = small_abs_sum[pt, pd]

    small_abs_sum = small_in[1]
    small_got = small_in[0]

    def sum_move(k):
        return pltpu.make_async_remote_copy(
            small_sum.at[pl.ds(2**k, 2**k)],
            small_got.at[pl.ds(2**k, 2**k)],
            s_sem.at[2, k],
            s_sem.at[3, k],
            device_id=small_place(2**k),
            device_id_type=MESH,
        )

    def sum_step(k):
        def go():
            if k < 4:
                sum_move(k + 1).wait()
                here = pl.ds(0, 2 ** (k + 1))
                small_sum[here] = small_sum[here] + small_got[pl.ds(2 ** (k + 1), 2 ** (k + 1))]
            if k >= 0:
                sum_move(k).start()

        return go

    if linked:
        link.grads_to_core(QKV)
        cut_small()
        sums = [sum_step(k) for k in range(4, -2, -1)]
        first_half = woven(grad_events(UP, 8, 16), grad_events(OUT, 0, 12), grad_events(QKV, 0, 5), sums[:3], backs[2:5])
        second = woven(grad_events(OUT, 12, 16) + grad_events(QKV, 5, 16), sums[3:], backs[5:])
        for event in first_half + second:
            event()
        vshare[...] = small_sum[0]
        for n in range(4):
            link.grads_sent(n)
    else:
        for event in backs:
            event()
        saves = []
        for g in range(3):
            for k in range(2):
                source = gd.at[k] if g == 2 else w.at[g, k]
                saves.append(pltpu.make_async_copy(source, share.at[g, k], own.at[g, k]))
        for copy in saves:
            copy.start()
        for copy in saves:
            copy.wait()
        vshare[pl.ds(0, 8), pl.ds(0, feat)] = vgrad[...]
        for k in range(2):
            vshare[pl.ds(8 + 8 * k, 8), :] = bgrad[k]
    for kind, ref in enumerate((out_rows, n2)):
        pltpu.make_async_copy(ref, ref, o_sem.at[0, kind]).wait()
        if linked:
            pltpu.make_async_remote_copy(
                ref, ref, o_sem.at[1, kind], o_sem.at[2, kind], device_id=link.place(Y), device_id_type=MESH
            ).wait()


VLIM = 60


def run_layer(linked, big, small, bvis, svis, bcot, scot, weights, parts, wide):
    nb, bl = bvis.shape[0] // parts, bvis.shape[1]
    ns, sl = svis.shape[0] // parts, svis.shape[1]
    tokens = nb * bl + ns * sl
    feat = big.shape[2]
    tile = wide // 3
    tiles = 6
    pairs = feat // 128
    rows = weights[1].shape[0] if linked else 48
    vm, hbm = pl.BlockSpec(memory_space=pltpu.VMEM), pl.BlockSpec(memory_space=pl.ANY)
    pair = (2, tokens, feat) if linked else (tokens, feat)
    dma = pltpu.SemaphoreType.DMA
    link = (lambda *shape: pltpu.VMEM(shape, BF)) if linked else (lambda *shape: pltpu.VMEM((16, 128), BF))
    loads = nb * (big.shape[1] // 512) + ns
    return pl.pallas_call(
        functools.partial(layer_kernel, (nb, bl, ns, sl), linked),
        out_shape=(
            jax.ShapeDtypeStruct(pair, BF),
            jax.ShapeDtypeStruct(pair, BF),
            jax.ShapeDtypeStruct((3, rows, wide) if linked else weights[0].shape, F32 if linked else BF),
            jax.ShapeDtypeStruct((8, 128) if linked else (24, wide), F32),
        ),
        in_specs=[hbm, hbm, vm, vm, hbm, hbm] + ([hbm] * 4 + [vm, vm] if linked else [hbm, vm, vm]),
        out_specs=(hbm, hbm, vm if linked else hbm, vm),
        scratch_shapes=[
            pltpu.VMEM((16, 128), F32),
            pltpu.VMEM((3, 2, feat, wide), BF),
            pltpu.VMEM((2, feat, wide), BF),
            link(3, 16, rows, wide),
            link(3, 15, rows, wide),
            pltpu.VMEM((tokens, feat), BF),
            pltpu.VMEM((tokens, feat), BF),
            pltpu.VMEM((tokens, feat), BF),
            pltpu.VMEM((2, tokens, 3 * feat // 2), BF),
            pltpu.VMEM((pairs, nb, 2, bl, bl), BF),
            pltpu.VMEM((pairs, 2, ns * sl, ns * sl), BF),
            pltpu.VMEM((tokens, feat), BF),
            pltpu.VMEM((tokens, feat), F32),
            pltpu.VMEM((tokens, feat), F32),
            pltpu.VMEM((tiles, tokens, tile), BF),
            pltpu.VMEM((tiles, tokens, tile), BF),
            pltpu.VMEM((tokens, feat), BF),
            pltpu.VMEM((tokens, feat), BF),
            pltpu.VMEM((8, feat), F32),
            pltpu.VMEM((2, 8, wide), F32),
            pltpu.VMEM((8, feat), F32),
            pltpu.VMEM((2, 8, wide), F32),
            pltpu.VMEM((32, 16, 128), BF),
            pltpu.VMEM((2, 16, 16, 128), BF),
            pltpu.VMEM((32, 8, 128), F32),
            [pltpu.VMEM((32, 8, 128), F32), pltpu.VMEM((2, 16, 8, 128), F32)],
            dma((3,)),
            dma((3, 16)),
            dma((3,)),
            dma((3,)),
            dma((4,)),
            dma((4, 2, 15)),
            dma((4,)),
            dma((4, 16)),
            dma((3, 2)),
            dma((loads, 2)),
            dma,
            dma((3, 2)),
            dma((4, 5)),
        ],
        compiler_params=pltpu.CompilerParams(
            collective_id=0 if linked else None, has_side_effects=linked, vmem_limit_bytes=VLIM * MIB
        ),
        name="layer",
    )(big, small, bvis, svis, bcot, scot, *weights)


def adam_step(weight, moment_one, moment_two, gradient, step_rate, decay_rate):
    moment_one = 0.9 * moment_one + 0.1 * gradient
    moment_two = 0.999 * moment_two + 0.001 * gradient * gradient
    fixed_one = moment_one / (1.0 - 0.9**STEP_NUMBER)
    fixed_two = moment_two / (1.0 - 0.999**STEP_NUMBER)
    update = fixed_one / (jnp.sqrt(fixed_two) + 1e-08) + decay_rate * weight
    return (weight - step_rate * update, moment_one, moment_two)


def finish_kernel(bvis_ref, svis_ref, orow_ref, osmall_ref, brow_ref, bsmall_ref, share_ref, few_ref, *refs):
    states, (bout_ref, sout_ref, big_ref, small_ref), new = refs[:18], refs[18:22], refs[22:]
    i = pl.program_id(0)

    def spread(vis, rows, length):
        hot = lax.broadcasted_iota(jnp.int32, (length, vis.shape[1]), 0) == vis
        return dot(hot.astype(BF), rows)

    bout_ref[...] = orow_ref[...]
    sout_ref[...] = osmall_ref[...]
    big_ref[...] = spread(bvis_ref[pl.ds(i, 1), :], brow_ref[...], big_ref.shape[0])
    small_ref[...] = spread(svis_ref[pl.ds(i, 1), :], bsmall_ref[...], small_ref.shape[0])

    def update(at, gradient, where=...):
        old = [ref[where] for ref in states[3 * at : 3 * at + 3]]
        for ref, value in zip(new[3 * at :], adam_step(*old, gradient, LEARN_RATES[at], DECAYS[at])):
            ref[where] = value

    half = states[3].shape[1]

    @pl.when(i == 0)
    def _():
        update(2, share_ref[1])

    @pl.when(i == 1)
    def _():
        update(3, share_ref[2])

    @pl.when(i == 2)
    def _():
        for c in range(3):
            update(0, share_ref[0, :, c * half : (c + 1) * half], c)

    @pl.when(i == 3)
    def _():
        update(1, share_ref[0, :, 3 * half :])
        update(4, few_ref[6:7, : states[12].shape[1]])
        update(5, few_ref[:6, : states[15].shape[1]])


def finish(bvis, svis, outs, backs, share, few, states, big_len, small_len):
    parts, _, feat = outs.shape
    nb, bl = bvis.shape
    ns, sl = svis.shape
    each = nb // parts
    first_small = each * bl // sl
    vm = pl.BlockSpec(memory_space=pltpu.VMEM)
    rows = [
        pl.BlockSpec((None, bl, feat), lambda i: (lax.div(i, each), lax.rem(i, each), 0)),
        pl.BlockSpec((None, sl, feat), lambda i: (lax.div(i, each), first_small + lax.rem(i, each), 0)),
    ]
    whole = [pl.BlockSpec(one.shape, lambda i, n=one.ndim: (0,) * n) for one in (share, few, *states)]

    def chip(length):
        return pl.BlockSpec((None, length, feat), lambda i: (i, 0, 0))

    return pl.pallas_call(
        finish_kernel,
        grid=(nb,),
        out_shape=(
            jax.ShapeDtypeStruct((nb, bl, feat), BF),
            jax.ShapeDtypeStruct((ns, sl, feat), BF),
            jax.ShapeDtypeStruct((nb, big_len, feat), F32),
            jax.ShapeDtypeStruct((ns, small_len, feat), F32),
            *(jax.ShapeDtypeStruct(one.shape, F32) for one in states),
        ),
        in_specs=[vm, vm] + rows + rows + whole,
        out_specs=(chip(bl), chip(sl), chip(big_len), chip(small_len), *whole[2:]),
        compiler_params=pltpu.CompilerParams(vmem_limit_bytes=48 * MIB),
        name="finish",
    )(bvis, svis, outs, outs, backs, backs, share, few, *states)


def on_device(
    special,
    big_patches, small_patches, big_visible, small_visible, big_cot, small_cot,
    qkv_weight, qkv_first, qkv_second, out_weight, out_first, out_second,
    up_weight, up_first, up_second, down_weight, down_first, down_second,
    up_bias, up_bias_first, up_bias_second, norm_vectors, norm_first, norm_second,
):
    rows, half = out_weight.shape
    wide = up_weight.shape[1]
    feat = big_patches.shape[2]
    parts = feat // half
    chips = (big_patches, small_patches, big_visible, small_visible, big_cot, small_cot)
    if special:
        weights = (jnp.swapaxes(qkv_weight, 0, 1), out_weight, up_weight, down_weight, norm_vectors, up_bias)
        outs, backs, share, few = run_layer(True, *chips, weights, parts, wide)
    else:
        attn = jnp.concatenate([qkv_weight.reshape(rows, 3 * half), out_weight], axis=1).astype(BF)
        piece = jnp.stack([attn, up_weight.astype(BF), down_weight.astype(BF)])
        w = lax.all_gather(lax.all_gather(piece, "dp", axis=1, tiled=True), "tensor", axis=1)
        vectors = lax.all_gather(norm_vectors.astype(BF), "dp", axis=1, tiled=True).astype(F32)
        bias = lax.all_gather(up_bias.astype(BF), "dp", axis=1, tiled=True)
        bias = lax.all_gather(bias, "tensor", axis=0).astype(F32)
        weights = (w, jnp.pad(vectors, ((0, 2), (0, 0))), jnp.pad(bias, ((0, 0), (6, 1), (0, 0))))
        out_rows, back_rows, grads, few = run_layer(False, *chips, weights, parts, wide)
        share = lax.psum_scatter(grads, "tensor", scatter_dimension=1)
        share = lax.psum_scatter(share, "dp", scatter_dimension=1, tiled=True).astype(F32)
        both = lax.all_gather(jnp.stack([out_rows, back_rows]), "tensor", axis=1)
        outs, backs = both[0], both[1]
        norm_share = lax.psum_scatter(lax.psum(few[:6, :feat], "tensor"), "dp", scatter_dimension=1, tiled=True)
        bias_share = lax.psum_scatter(few[14::8], "tensor", scatter_dimension=0, tiled=True)
        bias_share = lax.psum_scatter(bias_share, "dp", scatter_dimension=1, tiled=True)
        few = jnp.concatenate(
            [
                jnp.pad(norm_share, ((0, 0), (0, 128 - norm_share.shape[1]))),
                jnp.pad(bias_share, ((0, 1), (0, 128 - bias_share.shape[1]))),
            ]
        )
    states = (
        *(jnp.swapaxes(one, 0, 1) for one in (qkv_weight, qkv_first, qkv_second)), out_weight, out_first, out_second,
        up_weight, up_first, up_second, down_weight, down_first, down_second,
        up_bias, up_bias_first, up_bias_second, norm_vectors, norm_first, norm_second,
    )
    done = finish(
        big_visible, small_visible, outs, backs, share, few, states, big_patches.shape[1], small_patches.shape[1]
    )
    return (*done[:4], *(jnp.swapaxes(one, 0, 1) for one in done[4:7]), *done[7:])


def solution(mesh):
    special = mesh.shape["dp"] == 16 and mesh.shape["tensor"] == 2
    chips = P("dp", None, None)
    matrix, qkv = P("dp", "tensor"), P("dp", None, "tensor")
    states = (qkv,) * 3 + (matrix,) * 9 + (P("tensor", "dp"),) * 3 + (P(None, "dp"),) * 3
    return jax.shard_map(
        functools.partial(on_device, special),
        mesh=mesh,
        in_specs=(chips, chips, P("dp", None), P("dp", None), chips, chips) + states,
        out_specs=(chips,) * 4 + states,
        check_vma=False,
    )
```

```python
import functools

import jax
import jax.numpy as jnp
from jax import lax
from jax.experimental import pallas as pl
from jax.experimental.pallas import tpu as pltpu
from jax.sharding import PartitionSpec as P

HD = 64
STEP_NUMBER = 10
BF, F32 = jnp.bfloat16, jnp.float32
MESH = pl.DeviceIdType.MESH
MIB = 2**20

LEARN_RATES = (0.03, 0.1, 0.03, 0.015, 0.2, 0.2)
DECAYS = (0.05, 0.05, 0.05, 0.05, 0.0, 0.0)

Z1, Z2, X, Y = 1, 2, 4, 8
DIMS = (Z1, Z2, X, Y)
def place(code, other_core=False):
    d, t = lax.axis_index("dp"), lax.axis_index("tensor")
    z, x, c = lax.div(d, 4), lax.rem(lax.div(d, 2), 2), lax.rem(d, 2)
    if code & Z1:
        z = z + 1 - 2 * lax.rem(z, 2)
    if code & Z2:
        z = z + 2 - 4 * lax.div(z, 2)
    if code & X:
        x = 1 - x
    if code & Y:
        t = 1 - t
    if other_core:
        c = 1 - c
    return z * 4 + x * 2 + c, t


def greet(place):
    barrier = pltpu.get_barrier_semaphore()
    for dim in DIMS:
        pl.semaphore_signal(barrier, inc=1, device_id=place(dim), device_id_type=MESH)
    pl.semaphore_signal(barrier, inc=1, device_id=place(0, True), device_id_type=MESH)


def await_greetings():
    pl.semaphore_wait(pltpu.get_barrier_semaphore(), 5)


def bits(code):
    return bin(code).count("1")


def top_of(order, code):
    return max([order.index(k) for k in DIMS if code & k], default=-1)


def dot(a, b):
    return jnp.dot(a, b, preferred_element_type=F32)


def dot_nt(a, b):
    return lax.dot_general(a, b, (((1,), (1,)), ((), ())), preferred_element_type=F32)


def dot_tn(a, b):
    return lax.dot_general(a, b, (((0,), (0,)), ((), ())), preferred_element_type=F32)


def normed(v):
    centred = v - jnp.mean(v, axis=-1, keepdims=True)
    r = lax.rsqrt(jnp.mean(centred * centred, axis=-1, keepdims=True) + 1e-05)
    return centred * r, r


def norm_back(e, xhat, r, gain):
    eg = e * gain
    return r * (eg - jnp.mean(eg, axis=-1, keepdims=True) - xhat * jnp.mean(eg * xhat, axis=-1, keepdims=True))


def column_of(row):
    wide = jnp.broadcast_to(row.astype(F32), (128, row.shape[1]))
    return jnp.transpose(wide).astype(jnp.int32)


T, PP, Q, R = (Z2, Z1, X, Y), (Z2, Z1, Y, X), (Z2, Y, X, Z1), (Y, Z2, X, Z1)
GATHER_ORDERS = ((T, PP), (T, PP), (T, PP))
AHEAD = 2
DOWN, UP, OUT, QKV = range(4)
SUMS = (
    (2, ((PP, 0, 768), (R, 768, 768))),
    (1, ((PP, 0, 768), (R, 768, 768))),
    (0, ((PP, 1152, 256), (R, 1408, 128))),
    (0, ((PP, 0, 512), (R, 512, 640))),
)
SLOTS = {}
for _order in (T, PP, Q, R):
    SLOTS[_order] = {}
    for _at, _dim in enumerate(_order):
        for _code in range(16):
            if top_of(_order, _code) < _at:
                SLOTS[_order][_code, _dim] = len(SLOTS[_order])
RISING = sorted(range(1, 16), key=bits)
FALLING = sorted(range(16), key=lambda code: -bits(code))


def cut_columns(orders, cols):
    width = cols // len(orders)
    return [(order, pl.ds(at * width, width)) for at, order in enumerate(orders)]


class Links:
    def __init__(self, rows, w, gd, from_core, from_chip, share, sems):
        self.w, self.gd = w, gd
        self.from_core, self.from_chip, self.share = from_core, from_chip, share
        (
            self.asend, self.arecv, self.acsend, self.acrecv,
            self.rsend, self.rrecv, self.rcsend, self.rcrecv,
        ) = sems
        self.rows, self.cols = rows, w.shape[3]

        self.places = {(code, core): place(code, core) for code in range(16) for core in (False, True)}
        self.spans = {at: pl.ds(pl.multiple_of(d * self.rows, self.rows), self.rows) for at, (d, _) in self.places.items()}

    def place(self, code, core=False):
        return self.places[code, core]

    def at(self, code, core=False):
        return self.places[code, core][1], self.spans[code, core]

    def weight_move(self, g, part, code, dim):
        span = cut_columns(GATHER_ORDERS[g], self.cols)[part][1]
        target = self.w.at[(g,) + self.at(code) + (span,)]
        return pltpu.make_async_remote_copy(
            target,
            target,
            self.asend.at[g],
            self.arecv.at[g, code ^ dim],
            device_id=self.place(dim),
            device_id_type=MESH,
        )

    def weight_core_move(self, g, code, mine=True):
        target = self.w.at[(g,) + self.at(code, not mine)]
        return pltpu.make_async_remote_copy(
            target,
            target,
            self.acsend.at[g],
            self.acrecv.at[g],
            device_id=self.place(0, True),
            device_id_type=MESH,
        )

    def weight_forward(self, g, code):
        if code:
            target = self.w.at[(g,) + self.at(code)]
            pltpu.make_async_remote_copy(
                target, target, self.asend.at[g], self.arecv.at[g, code], device_id=self.place(Z1), device_id_type=MESH
            ).wait_recv()
        for part, order in enumerate(GATHER_ORDERS[g]):
            for dim in order[top_of(order, code) + 1 :]:
                self.weight_move(g, part, code, dim).start()
        self.weight_core_move(g, code).start()

    def weights_complete(self, g):
        target = self.w.at[g, 0]
        pltpu.make_async_remote_copy(
            target, target, self.acsend.at[g], self.acrecv.at[g], device_id=self.place(0, True), device_id_type=MESH
        ).wait_recv()

    def weights_sent(self, g):
        for ref, send, recv in (
            (self.from_chip.at[g], self.asend.at[g], self.arecv.at[g, 1]),
            (self.from_core.at[g], self.acsend.at[g], self.acrecv.at[g]),
        ):
            pltpu.make_async_remote_copy(
                ref, ref, send, recv, device_id=self.place(0, True), device_id_type=MESH
            ).wait_send()

    def grad(self, n, code, core, start, width):
        g = SUMS[n][0]
        where = self.at(code, core) + (pl.ds(start, width),)
        return (self.gd, where) if g == 2 else (self.w, (g,) + where)

    def grad_core_move(self, n, code):
        g, parts = SUMS[n]
        start, width = parts[0][1], sum(part[2] for part in parts)
        ref, where = self.grad(n, code, True, start, width)
        return pltpu.make_async_remote_copy(
            ref.at[where],
            self.from_core.at[g, code, :, pl.ds(start, width)],
            self.rcsend.at[n],
            self.rcrecv.at[n, code],
            device_id=self.place(0, True),
            device_id_type=MESH,
        )

    def grad_move(self, n, part, code, dim, sending):
        g, parts = SUMS[n]
        order, start, width = parts[part]
        ref, where = self.grad(n, code, False, start, width)
        slot = SLOTS[order][code ^ dim if sending else code, dim]
        return pltpu.make_async_remote_copy(
            ref.at[where],
            self.from_chip.at[g, slot, :, pl.ds(start, width)],
            self.rsend.at[n],
            self.rrecv.at[n, part, slot],
            device_id=self.place(dim),
            device_id_type=MESH,
        )

    def grads_to_core(self, n):
        for code in FALLING:
            self.grad_core_move(n, code).start()

    def grad_step(self, n, code):
        g, parts = SUMS[n]
        self.grad_core_move(n, code).wait_recv()
        for part, (order, start, width) in enumerate(parts):
            at = top_of(order, code)
            span = pl.ds(start, width)
            ref, where = self.grad(n, code, False, start, width)
            value = ref[where].astype(F32) + self.from_core[g, code, :, span].astype(F32)
            for dim in reversed(order[at + 1 :]):
                self.grad_move(n, part, code, dim, False).wait_recv()
                value = value + self.from_chip[g, SLOTS[order][code, dim], :, span].astype(F32)
            if code == 0:
                self.share[g, :, span] = value
            else:
                ref[where] = value.astype(BF)
                self.grad_move(n, part, code, order[at], True).start()

    def grads_sent(self, n):
        g, parts = SUMS[n]
        span = pl.ds(parts[0][1], sum(part[2] for part in parts))
        for ref, send, recv in (
            (self.from_chip.at[g, :, :, span], self.rsend.at[n], self.rrecv.at[n, 0, 0]),
            (self.from_core.at[g, :, :, span], self.rcsend.at[n], self.rcrecv.at[n, 0]),
        ):
            pltpu.make_async_remote_copy(
                ref, ref, send, recv, device_id=self.place(0, True), device_id_type=MESH
            ).wait_send()


def looped(count, body, events=()):
    events = list(events)

    @pl.loop(0, count)
    def _(i):
        body(i)
        for at in range(count):
            mine = events[len(events) * at // count : len(events) * (at + 1) // count]
            if mine:

                @pl.when(i == at)
                def _():
                    for event in mine:
                        event()


def layer_kernel(
    shape,
    linked,
    big_ref, small_ref, bvis_ref, svis_ref, bcot_ref, scot_ref, *refs,
):
    if linked:
        qkv_ref, mix_ref, up_ref, down_ref, norm_ref, up_bias_ref, *refs = refs
    else:
        w_ref, vec_ref, bias_ref, *refs = refs
    run_kernel(
        shape, linked, big_ref, small_ref, bvis_ref, svis_ref, bcot_ref, scot_ref,
        (qkv_ref, mix_ref, up_ref, down_ref, norm_ref, up_bias_ref) if linked else (w_ref, vec_ref, bias_ref), *refs,
    )


def run_kernel(
    shape,
    linked,
    big_ref, small_ref, bvis_ref, svis_ref, bcot_ref, scot_ref, weight_refs,
    out_ref, back_ref, share, vshare,
    few, w, gd, from_core, from_chip, x, n1, n2, qkv, prob, prob_small, heads, mid, acc, act, slope, cot, out_rows,
    vecs, bias, vgrad, bgrad, small, small_abs, small_sum, small_in,
    asend, arecv, acsend, acrecv, rsend, rrecv, rcsend, rcrecv, own, p_sem, c_sem, o_sem, s_sem,
):
    nb, bl, ns, sl = shape
    feat, wide = w.shape[2:]
    cut = nb * bl
    tokens = cut + ns * sl
    half = feat // 2
    pairs = half // 128
    d, t = lax.axis_index("dp"), lax.axis_index("tensor")
    block = 128
    steps = tokens // block
    tile = act.shape[2]
    tiles = act.shape[0]
    per = tiles // 2
    small_rows = ns * sl
    spans = [(i, i * bl, bl) for i in range(nb)] + [(nb, cut, small_rows)]
    chunk = 512
    strips = [(at, min(tile, feat - at)) for at in range(0, feat, tile)]

    cloads = [
        pltpu.make_async_copy(bcot_ref.at[t * nb + i], cot.at[pl.ds(i * bl, bl)], c_sem) for i in range(nb)
    ]
    cloads += [
        pltpu.make_async_copy(scot_ref.at[t * ns + i], cot.at[pl.ds(cut + i * sl, sl)], c_sem)
        for i in range(ns)
    ]
    big_len, small_len = big_ref.shape[1], small_ref.shape[1]
    ploads = []
    for i in range(nb):
        for at in range(big_len // chunk):
            source = big_ref.at[t * nb + i, pl.ds(at * chunk, chunk)]
            ploads.append((i, at, source, chunk, (bvis_ref, t * nb + i, i * bl, bl)))
    for i in range(ns):
        ploads.append((nb + i, 0, small_ref.at[t * ns + i], small_len, (svis_ref, t * ns + i, cut + i * sl, sl)))

    def pload(at):
        _, _, source, length, _ = ploads[at]
        return [
            pltpu.make_async_copy(
                source.at[:, pl.ds(start, width)],
                act.at[at % 2 * len(strips) + c, pl.ds(0, length), pl.ds(0, width)],
                p_sem.at[at, c],
            )
            for c, (start, width) in enumerate(strips)
        ]

    for copy in pload(0):
        copy.start()
    for copy in cloads:
        copy.start()

    if linked:
        qkv_ref, mix_ref, up_ref, down_ref, norm_ref, up_bias_ref = weight_refs
        greet(place)
        stage = [
            pltpu.make_async_copy(ref, share.at[g], own.at[g, 0]) for g, ref in ((1, up_ref), (2, down_ref))
        ]
        heads_in = [
            pltpu.make_async_copy(qkv_ref.at[c], share.at[0, :, pl.ds(c * half, half)], own.at[0, c % 2]) for c in range(3)
        ]
        heads_in.append(pltpu.make_async_copy(mix_ref, share.at[0, :, pl.ds(3 * half, half)], own.at[0, 1]))
        for copy in heads_in + stage:
            copy.start()
        few[...] = jnp.zeros_like(few)
        few[: norm_ref.shape[0], : norm_ref.shape[1]] = norm_ref[...]
        few[6:7, : up_bias_ref.shape[1]] = up_bias_ref[...]
        link = Links(
            mix_ref.shape[0], w, gd, from_core, from_chip, share,
            (asend, arecv, acsend, acrecv, rsend, rrecv, rcsend, rcrecv),
        )
        for k in range(2):
            both = share.at[0, :, pl.ds(0, 2 * half)]
            pltpu.make_async_copy(both, both, own.at[0, k]).wait()
        w[(0,) + link.at(0)] = share[0].astype(BF)
        for g in (1, 2):
            stage[g - 1].wait()
            w[(g,) + link.at(0)] = share[g].astype(BF)

        def small_place(code):
            return link.place(code >> 1, bool(code & 1))

        small[0] = few[...].astype(BF)
        await_greetings()
    else:
        w_ref, vec_ref, bias_ref = weight_refs
        wloads = [
            [pltpu.make_async_copy(w_ref.at[g, k], w.at[g, k], own.at[g, k]) for k in range(2)] for g in range(3)
        ]
        for copy in sum(wloads, []):
            copy.start()

    def small_move(k):
        return pltpu.make_async_remote_copy(
            small.at[pl.ds(0, 2**k)],
            small.at[pl.ds(2**k, 2**k)],
            s_sem.at[0, k],
            s_sem.at[1, k],
            device_id=small_place(2**k),
            device_id_type=MESH,
        )

    def small_step(k):
        def go():
            if k:
                small_move(k - 1).wait()
            if k < 5:
                small_move(k).start()

        return go

    def set_vectors():
        for code in range(32):
            pd, pt = small_place(code)
            small_abs[pt, pd] = small[code]
        vec_sum, bias_sum = 0.0, [0.0, 0.0]
        parts = feat // 48 if linked else 0
        for at in range(parts):
            for k in range(2):
                value = small_abs[k, at].astype(F32)
                if k == 0:
                    padded = jnp.concatenate([value, jnp.zeros((16, feat - 128), F32)], axis=1)
                    vec_sum = vec_sum + (pltpu.roll(padded, at * 48, 1) if at else padded)
                padded = jnp.concatenate([value[:8], jnp.zeros((8, wide - 128), F32)], axis=1)
                bias_sum[k] = bias_sum[k] + (pltpu.roll(padded, at * 96, 1) if at else padded)
        vecs[...] = vec_sum[:8]
        for k in range(2):
            bias[k] = bias_sum[k]

    def vec(i):
        return vecs[i : i + 1, :]

    def rows_of(i):
        return pl.ds(pl.multiple_of(i * block, block), block)

    def pick(at):
        def go():
            chip, part, _, length, (vis_ref, row, first_row, count) = ploads[at]
            for copy in pload(at):
                copy.wait()
            if at + 1 < len(ploads):
                for copy in pload(at + 1):
                    copy.start()
            column = column_of(vis_ref[pl.ds(row, 1), :]) - part * length
            lane = lax.broadcasted_iota(jnp.int32, column.shape, 1)
            hot = jnp.concatenate([(column == lane + k * 128).astype(BF) for k in range(length // 128)], axis=1)
            rows = pl.ds(first_row, count)
            for c, (start, width) in enumerate(strips):
                picked = dot(hot, act[at % 2 * len(strips) + c, :length, :width])
                span = pl.ds(start, width)
                if part:
                    picked = picked + x[rows, span].astype(F32)
                x[rows, span] = picked.astype(BF)

        return go

    picks = [pick(at) for at in range(len(ploads))]

    def weight_event(g, code):
        return lambda: link.weight_forward(g, code)

    if linked:
        order = sorted(
            [(bits(code) + AHEAD * g, g, n, code) for g in range(3) for n, code in enumerate([0] + RISING)]
        )
        sequence = [(g, weight_event(g, code)) for _, g, _, code in order]
        last = [max(i for i, (g, _) in enumerate(sequence) if g == k) for k in range(3)]
        weight_events = [[e for _, e in sequence[lo : hi + 1]] for lo, hi in zip([0] + [i + 1 for i in last], last)]
        smalls = [small_step(k) for k in range(6)]
        mixed = [weight_events[0][0], smalls[0], picks[0], picks[1]] + weight_events[0][1:3] + [smalls[1], picks[2]]
        mixed += weight_events[0][3:5] + [picks[3], smalls[2]] + weight_events[0][5:8] + [picks[4], smalls[3]]
        mixed += weight_events[0][8:11] + picks[5:] + [smalls[4]] + weight_events[0][11:14] + [smalls[5]]
        mixed += weight_events[0][14:]
        for event in mixed:
            event()
        set_vectors()
    else:
        weight_events = [[], [], []]
        for event in picks:
            event()
        vecs[...] = vec_ref[...]
        bias[...] = bias_ref[...]

    def weights_ready(g):
        if linked:
            link.weights_complete(g)
        else:
            for copy in wloads[g]:
                copy.wait()

    def norm_one(i):
        xhat, r = normed(x[rows_of(i), :].astype(F32))
        value = xhat * vec(0) + vec(1)
        n1[rows_of(i), :] = value.astype(BF)

    looped(steps, norm_one)
    weights_ready(0)
    events = weight_events[1]
    lot = len(events) // 3

    def make_qkv(i):
        k, c = i // 3, i % 3
        span = pl.ds(pl.multiple_of(c * half, half), half)
        qkv[k, :, span] = dot(n1[...], w[0, k, :, span]).astype(BF)

    looped(6, make_qkv, events[:lot])

    lane = lax.broadcasted_iota(jnp.int32, (1, 128), 1)
    first = lane < HD
    zero = jnp.zeros((), BF)

    def softmax(scores):
        e = jnp.exp(scores - jnp.max(scores, axis=-1, keepdims=True))
        return e / jnp.sum(e, axis=-1, keepdims=True)

    same = (
        lax.broadcasted_iota(jnp.int32, (small_rows, small_rows), 0) // sl
        == lax.broadcasted_iota(jnp.int32, (small_rows, small_rows), 1) // sl
    )

    def pair_spans(pair):
        k, j = pair // pairs, pair % pairs
        return k, [pl.ds(pl.multiple_of(c * half + j * 128, 128), 128) for c in range(3)]

    def attention(pair):
        k, lanes = pair_spans(pair)
        stage = []
        for i, start, count in spans:
            rows = pl.ds(start, count)
            q, key, value = (qkv[k, rows, lanes[c]] for c in range(3))
            scores = [dot_nt(jnp.where(first if h == 0 else ~first, q, zero), key) * HD ** (-0.5) for h in range(2)]
            stage.append((i, rows, value, scores))
        chances = []
        for i, rows, value, scores in stage:
            if i == nb:
                scores = [jnp.where(same, one, -jnp.inf) for one in scores]
            chances.append([softmax(one).astype(BF) for one in scores])
        here = pl.ds(pl.multiple_of(pair * 128, 128), 128)
        for (i, rows, value, _), p in zip(stage, chances):
            mixed = [dot(one, value) for one in p]
            heads[rows, here] = jnp.where(first, mixed[0], mixed[1]).astype(BF)
        for (i, _, _, _), p in zip(stage, chances):
            for h in range(2):
                if i == nb:
                    prob_small[pair, h] = p[h]
                else:
                    prob[pair, i, h] = p[h]

    looped(2 * pairs, attention, events[lot:])

    out_span = pl.ds(3 * half, half)

    def project(i):
        span = pl.ds(pl.multiple_of(i * 256, 256), 256)
        mid[:, span] = dot_nt(heads[:, :half], w[0, 0, span, out_span]) + dot_nt(heads[:, half:], w[0, 1, span, out_span])

    looped(feat // 256, project)

    def norm_two(i):
        middle = x[rows_of(i), :].astype(F32) + mid[rows_of(i), :] + vec(4)
        mid[rows_of(i), :] = middle
        xhat, r = normed(middle)
        value = xhat * vec(2) + vec(3)
        n2[rows_of(i), :] = value.astype(BF)
        acc[rows_of(i), :] = middle + vec(5)

    looped(steps, norm_two)
    pltpu.make_async_copy(cot, cot, c_sem).wait()

    weights_ready(1)
    events = weight_events[2]
    lot = len(events) * 2 // 3

    def grad_events(n, lo, hi):
        if not linked:
            return []
        return [functools.partial(link.grad_step, n, code) for code in FALLING[lo:hi]]

    def woven(*lists):
        keyed = [((n + 0.5) / len(events), at, event) for at, events in enumerate(lists) for n, event in enumerate(events)]
        return [event for _, _, event in sorted(keyed, key=lambda one: one[:2])]

    def tile_of(i):
        return i // per, pl.ds(pl.multiple_of((i % per) * tile, tile), tile)

    def up(i):
        at, here = i // 2, pl.ds(pl.multiple_of(i % 2 * 256, 256), 256)
        k, span = at // per, pl.ds(pl.multiple_of(at % per * tile + i % 2 * 256, 256), 256)
        pre = dot(n2[...], w[1, k, :, span]) + bias[k, 6:7, span]
        cdf = 0.5 * (1.0 + lax.erf(pre * 0.7071067811865476))
        act[at, :, here] = (pre * cdf).astype(BF)
        slope[at, :, here] = (cdf + pre * jnp.exp(-0.5 * pre * pre) * 0.3989422804014327).astype(BF)

    looped(tiles * 2, up, events[:lot])

    def grad_down(i):
        k, span = tile_of(i)
        gd[k, :, span] = dot_tn(cot[...], act[i]).astype(BF)

    looped(tiles, grad_down, events[lot:])
    if linked:
        link.grads_to_core(DOWN)
    weights_ready(2)

    def down(i):
        k, span = tile_of(i)
        acc[...] += dot_nt(act[i], w[2, k, :, span])

    looped(tiles, down, grad_events(DOWN, 0, 3))
    out_rows[...] = acc[...].astype(BF)

    def row_moves(kind, n):
        rows = pl.ds(n * 64, 64)
        source = (out_rows if kind == 0 else n2).at[rows]
        target = out_ref if kind == 0 else back_ref
        target = target.at[t, rows] if linked else target.at[rows]
        near = pltpu.make_async_copy(source, target, o_sem.at[0, kind])
        if not linked:
            return [near]
        far = pltpu.make_async_remote_copy(
            source, target, o_sem.at[1, kind], o_sem.at[2, kind], device_id=link.place(Y), device_id_type=MESH
        )
        return [near, far]

    def row_event(kind, n):
        def go():
            for move in row_moves(kind, n):
                move.start()

        return go

    outs = [row_event(0, n) for n in range(tokens // 64)]

    acc[...] = jnp.zeros_like(acc)
    if linked:
        for g in range(3):
            link.weights_sent(g)

    def back_up(i):
        k, span = tile_of(i)
        back = (slope[i].astype(F32) * dot(cot[...], w[2, k, :, span])).astype(BF)
        bgrad[k, 6:7, span] = jnp.sum(back.astype(F32), axis=0, keepdims=True)
        acc[...] += dot_nt(back, w[1, k, :, span])
        w[1, k, :, span] = dot_tn(n2[...], back).astype(BF)

    bgrad[...] = jnp.zeros_like(bgrad)
    looped(tiles, back_up, woven(grad_events(DOWN, 3, 9), outs[:5]))
    if linked:
        link.grads_to_core(UP)

    vgrad[...] = jnp.zeros_like(vgrad)

    def norm_two_back(i):
        e = acc[rows_of(i), :]
        xhat, r = normed(mid[rows_of(i), :])
        back_out = cot[rows_of(i), :].astype(F32)
        back_middle = back_out + norm_back(e, xhat, r, vec(2))
        acc[rows_of(i), :] = back_middle
        cot[rows_of(i), :] = back_middle.astype(BF)
        vgrad[2:3, :] += jnp.sum(e * xhat, axis=0, keepdims=True)
        vgrad[3:4, :] += jnp.sum(e, axis=0, keepdims=True)
        vgrad[4:5, :] += jnp.sum(back_middle, axis=0, keepdims=True)
        vgrad[5:6, :] += jnp.sum(back_out, axis=0, keepdims=True)

    looped(steps, norm_two_back, woven(grad_events(DOWN, 9, 12), grad_events(UP, 0, 3), outs[5:7]))

    dheads = heads
    for k in range(2):
        here = pl.ds(k * half, half)
        grad = dot_tn(cot[...], heads[:, here]).astype(BF)
        dheads[:, here] = dot(cot[...], w[0, k, :, out_span]).astype(BF)
        w[0, k, :, out_span] = grad

    if linked:
        link.grads_to_core(OUT)

    def attention_back(i, rows, some):
        stage = []
        for pair in some:
            k, lanes = pair_spans(pair)
            q, key, value = (qkv[k, rows, lanes[c]] for c in range(3))
            dh = dheads[rows, pl.ds(pl.multiple_of(pair * 128, 128), 128)]
            p = [prob_small[pair, h] if i == nb else prob[pair, i, h] for h in range(2)]
            dp = [dot_nt(jnp.where(first if h == 0 else ~first, dh, zero), value) for h in range(2)]
            ds = []
            for h in range(2):
                pf = p[h].astype(F32)
                ds.append((pf * (dp[h] - jnp.sum(pf * dp[h], axis=-1, keepdims=True))).astype(BF))
            stage.append((k, lanes, q, key, dh, p, ds))
        done = []
        scale = HD ** (-0.5)
        for k, lanes, q, key, dh, p, ds in stage:
            dq, dk, dv = [dot(one, key) for one in ds], [dot_tn(one, q) for one in ds], [dot_tn(one, dh) for one in p]
            done.append((k, lanes[0], jnp.where(first, dq[0], dq[1]) * scale))
            done.append((k, lanes[1], jnp.where(first, dk[0], dk[1]) * scale))
            done.append((k, lanes[2], jnp.where(first, dv[0], dv[1])))
        for k, here, value in done:
            qkv[k, rows, here] = value.astype(BF)

    during = [
        woven(grad_events(DOWN, 12, 16), grad_events(UP, 3, 6), outs[7:9]),
        woven(grad_events(UP, 6, 9), grad_events(OUT, 0, 3), outs[9:]),
        woven(grad_events(UP, 9, 11), grad_events(OUT, 3, 5)),
    ]
    backs = []
    for at, (i, start, count) in enumerate(spans):
        rows = pl.ds(start, count)
        looped(
            2,
            lambda n: attention_back(i, rows, [n * pairs + j for j in range(pairs)]),
            during[at][: len(during[at]) // 2] if at < 3 else [],
        )

        def back_first(n):
            span = pl.ds(pl.multiple_of(n * 256, 256), 256)
            both = pl.ds(0, 3 * half)
            mid[rows, span] = dot_nt(qkv[0, rows, both], w[0, 0, span, both]) + dot_nt(
                qkv[1, rows, both], w[0, 1, span, both]
            )

        looped(feat // 256, back_first, during[at][len(during[at]) // 2 :] if at < 3 else [])

        def norm_one_back(n):
            here = pl.ds(pl.multiple_of(start + n * block, block), block)
            e = mid[here, :]
            xhat, r = normed(x[here, :].astype(F32))
            back_in = acc[here, :] + norm_back(e, xhat, r, vec(0))
            n2[here, :] = back_in.astype(BF)
            vgrad[0:1, :] += jnp.sum(e * xhat, axis=0, keepdims=True)
            vgrad[1:2, :] += jnp.sum(e, axis=0, keepdims=True)

        looped(count // block, norm_one_back)
        mine = [row_event(1, n) for n in range(start // 64, (start + count) // 64)]
        mine[0]()
        backs += mine[1:]

    def grad_qkv(i):
        k, c = i // 3, i % 3
        span = pl.ds(pl.multiple_of(c * half, half), half)
        w[0, k, :, span] = dot_tn(n1[...], qkv[k, :, span]).astype(BF)

    looped(6, grad_qkv, woven(grad_events(UP, 11, 13), grad_events(OUT, 5, 8), backs[:3]))

    def cut_small():
        low = lax.broadcasted_iota(jnp.int32, (8, 128), 1)
        row = lax.broadcasted_iota(jnp.int32, (8, 128), 0)
        for at in range(feat // 48):
            value = vgrad[...]
            if at:
                value = pltpu.roll(value, feat - at * 48, 1)
            value = jnp.where((low < 48) & (row < 6), value[:, :128], 0.0)
            for k in range(2):
                more = bgrad[k]
                if at:
                    more = pltpu.roll(more, wide - at * 96, 1)
                small_abs_sum[k, at] = value + jnp.where((low < 96) & (row == 6), more[:, :128], 0.0)
        for code in range(32):
            pd, pt = small_place(code)
            small_sum[code] = small_abs_sum[pt, pd]

    small_abs_sum = small_in[1]
    small_got = small_in[0]

    def sum_move(k):
        return pltpu.make_async_remote_copy(
            small_sum.at[pl.ds(2**k, 2**k)],
            small_got.at[pl.ds(2**k, 2**k)],
            s_sem.at[2, k],
            s_sem.at[3, k],
            device_id=small_place(2**k),
            device_id_type=MESH,
        )

    def sum_step(k):
        def go():
            if k < 4:
                sum_move(k + 1).wait()
                here = pl.ds(0, 2 ** (k + 1))
                small_sum[here] = small_sum[here] + small_got[pl.ds(2 ** (k + 1), 2 ** (k + 1))]
            if k >= 0:
                sum_move(k).start()

        return go

    if linked:
        link.grads_to_core(QKV)
        cut_small()
        sums = [sum_step(k) for k in range(4, -2, -1)]
        first_half = grad_events(QKV, 0, 1) + woven(grad_events(UP, 13, 16), grad_events(OUT, 8, 12), grad_events(QKV, 1, 9), sums[:3], backs[3:5])
        second = woven(grad_events(OUT, 12, 16), grad_events(QKV, 9, 16), sums[3:], backs[5:])
        for event in first_half + second:
            event()
        vshare[...] = small_sum[0]
        for n in range(4):
            link.grads_sent(n)
    else:
        for event in backs:
            event()
        saves = []
        for g in range(3):
            for k in range(2):
                source = gd.at[k] if g == 2 else w.at[g, k]
                saves.append(pltpu.make_async_copy(source, share.at[g, k], own.at[g, k]))
        for copy in saves:
            copy.start()
        for copy in saves:
            copy.wait()
        vshare[pl.ds(0, 8), pl.ds(0, feat)] = vgrad[...]
        for k in range(2):
            vshare[pl.ds(8 + 8 * k, 8), :] = bgrad[k]
    for kind, ref in enumerate((out_rows, n2)):
        pltpu.make_async_copy(ref, ref, o_sem.at[0, kind]).wait()
        if linked:
            pltpu.make_async_remote_copy(
                ref, ref, o_sem.at[1, kind], o_sem.at[2, kind], device_id=link.place(Y), device_id_type=MESH
            ).wait()


VLIM = 60


def run_layer(linked, big, small, bvis, svis, bcot, scot, weights, parts, wide):
    nb, bl = bvis.shape[0] // parts, bvis.shape[1]
    ns, sl = svis.shape[0] // parts, svis.shape[1]
    tokens = nb * bl + ns * sl
    feat = big.shape[2]
    tile = wide // 3
    tiles = 6
    pairs = feat // 128
    rows = weights[1].shape[0] if linked else 48
    vm, hbm = pl.BlockSpec(memory_space=pltpu.VMEM), pl.BlockSpec(memory_space=pl.ANY)
    pair = (2, tokens, feat) if linked else (tokens, feat)
    dma = pltpu.SemaphoreType.DMA
    link = (lambda *shape: pltpu.VMEM(shape, BF)) if linked else (lambda *shape: pltpu.VMEM((16, 128), BF))
    loads = nb * (big.shape[1] // 512) + ns
    return pl.pallas_call(
        functools.partial(layer_kernel, (nb, bl, ns, sl), linked),
        out_shape=(
            jax.ShapeDtypeStruct(pair, BF),
            jax.ShapeDtypeStruct(pair, BF),
            jax.ShapeDtypeStruct((3, rows, wide) if linked else weights[0].shape, F32 if linked else BF),
            jax.ShapeDtypeStruct((8, 128) if linked else (24, wide), F32),
        ),
        in_specs=[hbm, hbm, vm, vm, hbm, hbm] + ([hbm] * 4 + [vm, vm] if linked else [hbm, vm, vm]),
        out_specs=(hbm, hbm, vm if linked else hbm, vm),
        scratch_shapes=[
            pltpu.VMEM((16, 128), F32),
            pltpu.VMEM((3, 2, feat, wide), BF),
            pltpu.VMEM((2, feat, wide), BF),
            link(3, 16, rows, wide),
            link(3, 15, rows, wide),
            pltpu.VMEM((tokens, feat), BF),
            pltpu.VMEM((tokens, feat), BF),
            pltpu.VMEM((tokens, feat), BF),
            pltpu.VMEM((2, tokens, 3 * feat // 2), BF),
            pltpu.VMEM((pairs, nb, 2, bl, bl), BF),
            pltpu.VMEM((pairs, 2, ns * sl, ns * sl), BF),
            pltpu.VMEM((tokens, feat), BF),
            pltpu.VMEM((tokens, feat), F32),
            pltpu.VMEM((tokens, feat), F32),
            pltpu.VMEM((tiles, tokens, tile), BF),
            pltpu.VMEM((tiles, tokens, tile), BF),
            pltpu.VMEM((tokens, feat), BF),
            pltpu.VMEM((tokens, feat), BF),
            pltpu.VMEM((8, feat), F32),
            pltpu.VMEM((2, 8, wide), F32),
            pltpu.VMEM((8, feat), F32),
            pltpu.VMEM((2, 8, wide), F32),
            pltpu.VMEM((32, 16, 128), BF),
            pltpu.VMEM((2, 16, 16, 128), BF),
            pltpu.VMEM((32, 8, 128), F32),
            [pltpu.VMEM((32, 8, 128), F32), pltpu.VMEM((2, 16, 8, 128), F32)],
            dma((3,)),
            dma((3, 16)),
            dma((3,)),
            dma((3,)),
            dma((4,)),
            dma((4, 2, 15)),
            dma((4,)),
            dma((4, 16)),
            dma((3, 2)),
            dma((loads, 2)),
            dma,
            dma((3, 2)),
            dma((4, 5)),
        ],
        compiler_params=pltpu.CompilerParams(
            collective_id=0 if linked else None, has_side_effects=linked, vmem_limit_bytes=VLIM * MIB
        ),
        name="layer",
    )(big, small, bvis, svis, bcot, scot, *weights)


def adam_step(weight, moment_one, moment_two, gradient, step_rate, decay_rate):
    moment_one = 0.9 * moment_one + 0.1 * gradient
    moment_two = 0.999 * moment_two + 0.001 * gradient * gradient
    fixed_one = moment_one / (1.0 - 0.9**STEP_NUMBER)
    fixed_two = moment_two / (1.0 - 0.999**STEP_NUMBER)
    update = fixed_one / (jnp.sqrt(fixed_two) + 1e-08) + decay_rate * weight
    return (weight - step_rate * update, moment_one, moment_two)


def finish_kernel(bvis_ref, svis_ref, orow_ref, osmall_ref, brow_ref, bsmall_ref, share_ref, few_ref, *refs):
    states, (bout_ref, sout_ref, big_ref, small_ref), new = refs[:18], refs[18:22], refs[22:]
    i = pl.program_id(0)

    def spread(vis, rows, length):
        hot = lax.broadcasted_iota(jnp.int32, (length, vis.shape[1]), 0) == vis
        return dot(hot.astype(BF), rows)

    bout_ref[...] = orow_ref[...]
    sout_ref[...] = osmall_ref[...]
    big_ref[...] = spread(bvis_ref[pl.ds(i, 1), :], brow_ref[...], big_ref.shape[0])
    small_ref[...] = spread(svis_ref[pl.ds(i, 1), :], bsmall_ref[...], small_ref.shape[0])

    def update(at, gradient, where=...):
        old = [ref[where] for ref in states[3 * at : 3 * at + 3]]
        for ref, value in zip(new[3 * at :], adam_step(*old, gradient, LEARN_RATES[at], DECAYS[at])):
            ref[where] = value

    half = states[3].shape[1]

    @pl.when(i == 0)
    def _():
        update(2, share_ref[1])

    @pl.when(i == 1)
    def _():
        update(3, share_ref[2])

    @pl.when(i == 2)
    def _():
        for c in range(3):
            update(0, share_ref[0, :, c * half : (c + 1) * half], c)

    @pl.when(i == 3)
    def _():
        update(1, share_ref[0, :, 3 * half :])
        update(4, few_ref[6:7, : states[12].shape[1]])
        update(5, few_ref[:6, : states[15].shape[1]])


def finish(bvis, svis, outs, backs, share, few, states, big_len, small_len):
    parts, _, feat = outs.shape
    nb, bl = bvis.shape
    ns, sl = svis.shape
    each = nb // parts
    first_small = each * bl // sl
    vm = pl.BlockSpec(memory_space=pltpu.VMEM)
    rows = [
        pl.BlockSpec((None, bl, feat), lambda i: (lax.div(i, each), lax.rem(i, each), 0)),
        pl.BlockSpec((None, sl, feat), lambda i: (lax.div(i, each), first_small + lax.rem(i, each), 0)),
    ]
    whole = [pl.BlockSpec(one.shape, lambda i, n=one.ndim: (0,) * n) for one in (share, few, *states)]

    def chip(length):
        return pl.BlockSpec((None, length, feat), lambda i: (i, 0, 0))

    return pl.pallas_call(
        finish_kernel,
        grid=(nb,),
        out_shape=(
            jax.ShapeDtypeStruct((nb, bl, feat), BF),
            jax.ShapeDtypeStruct((ns, sl, feat), BF),
            jax.ShapeDtypeStruct((nb, big_len, feat), F32),
            jax.ShapeDtypeStruct((ns, small_len, feat), F32),
            *(jax.ShapeDtypeStruct(one.shape, F32) for one in states),
        ),
        in_specs=[vm, vm] + rows + rows + whole,
        out_specs=(chip(bl), chip(sl), chip(big_len), chip(small_len), *whole[2:]),
        compiler_params=pltpu.CompilerParams(vmem_limit_bytes=48 * MIB),
        name="finish",
    )(bvis, svis, outs, outs, backs, backs, share, few, *states)


def on_device(
    special,
    big_patches, small_patches, big_visible, small_visible, big_cot, small_cot,
    qkv_weight, qkv_first, qkv_second, out_weight, out_first, out_second,
    up_weight, up_first, up_second, down_weight, down_first, down_second,
    up_bias, up_bias_first, up_bias_second, norm_vectors, norm_first, norm_second,
):
    rows, half = out_weight.shape
    wide = up_weight.shape[1]
    feat = big_patches.shape[2]
    parts = feat // half
    chips = (big_patches, small_patches, big_visible, small_visible, big_cot, small_cot)
    if special:
        weights = (jnp.swapaxes(qkv_weight, 0, 1), out_weight, up_weight, down_weight, norm_vectors, up_bias)
        outs, backs, share, few = run_layer(True, *chips, weights, parts, wide)
    else:
        attn = jnp.concatenate([qkv_weight.reshape(rows, 3 * half), out_weight], axis=1).astype(BF)
        piece = jnp.stack([attn, up_weight.astype(BF), down_weight.astype(BF)])
        w = lax.all_gather(lax.all_gather(piece, "dp", axis=1, tiled=True), "tensor", axis=1)
        vectors = lax.all_gather(norm_vectors.astype(BF), "dp", axis=1, tiled=True).astype(F32)
        bias = lax.all_gather(up_bias.astype(BF), "dp", axis=1, tiled=True)
        bias = lax.all_gather(bias, "tensor", axis=0).astype(F32)
        weights = (w, jnp.pad(vectors, ((0, 2), (0, 0))), jnp.pad(bias, ((0, 0), (6, 1), (0, 0))))
        out_rows, back_rows, grads, few = run_layer(False, *chips, weights, parts, wide)
        share = lax.psum_scatter(grads, "tensor", scatter_dimension=1)
        share = lax.psum_scatter(share, "dp", scatter_dimension=1, tiled=True).astype(F32)
        both = lax.all_gather(jnp.stack([out_rows, back_rows]), "tensor", axis=1)
        outs, backs = both[0], both[1]
        norm_share = lax.psum_scatter(lax.psum(few[:6, :feat], "tensor"), "dp", scatter_dimension=1, tiled=True)
        bias_share = lax.psum_scatter(few[14::8], "tensor", scatter_dimension=0, tiled=True)
        bias_share = lax.psum_scatter(bias_share, "dp", scatter_dimension=1, tiled=True)
        few = jnp.concatenate(
            [
                jnp.pad(norm_share, ((0, 0), (0, 128 - norm_share.shape[1]))),
                jnp.pad(bias_share, ((0, 1), (0, 128 - bias_share.shape[1]))),
            ]
        )
    states = (
        *(jnp.swapaxes(one, 0, 1) for one in (qkv_weight, qkv_first, qkv_second)), out_weight, out_first, out_second,
        up_weight, up_first, up_second, down_weight, down_first, down_second,
        up_bias, up_bias_first, up_bias_second, norm_vectors, norm_first, norm_second,
    )
    done = finish(
        big_visible, small_visible, outs, backs, share, few, states, big_patches.shape[1], small_patches.shape[1]
    )
    return (*done[:4], *(jnp.swapaxes(one, 0, 1) for one in done[4:7]), *done[7:])


def solution(mesh):
    special = mesh.shape["dp"] == 16 and mesh.shape["tensor"] == 2
    chips = P("dp", None, None)
    matrix, qkv = P("dp", "tensor"), P("dp", None, "tensor")
    states = (qkv,) * 3 + (matrix,) * 9 + (P("tensor", "dp"),) * 3 + (P(None, "dp"),) * 3
    return jax.shard_map(
        functools.partial(on_device, special),
        mesh=mesh,
        in_specs=(chips, chips, P("dp", None), P("dp", None), chips, chips) + states,
        out_specs=(chips,) * 4 + states,
        check_vma=False,
    )
```

```python
import functools

import jax
import jax.numpy as jnp
from jax import lax
from jax.experimental import pallas as pl
from jax.experimental.pallas import tpu as pltpu
from jax.sharding import PartitionSpec as P

HD = 64
STEP_NUMBER = 10
BF, F32 = jnp.bfloat16, jnp.float32
MESH = pl.DeviceIdType.MESH
MIB = 2**20

LEARN_RATES = (0.03, 0.1, 0.03, 0.015, 0.2, 0.2)
DECAYS = (0.05, 0.05, 0.05, 0.05, 0.0, 0.0)

Z1, Z2, X, Y = 1, 2, 4, 8
DIMS = (Z1, Z2, X, Y)
def place(code, other_core=False):
    d, t = lax.axis_index("dp"), lax.axis_index("tensor")
    z, x, c = lax.div(d, 4), lax.rem(lax.div(d, 2), 2), lax.rem(d, 2)
    if code & Z1:
        z = z + 1 - 2 * lax.rem(z, 2)
    if code & Z2:
        z = z + 2 - 4 * lax.div(z, 2)
    if code & X:
        x = 1 - x
    if code & Y:
        t = 1 - t
    if other_core:
        c = 1 - c
    return z * 4 + x * 2 + c, t


def greet(place):
    barrier = pltpu.get_barrier_semaphore()
    for dim in DIMS:
        pl.semaphore_signal(barrier, inc=1, device_id=place(dim), device_id_type=MESH)
    pl.semaphore_signal(barrier, inc=1, device_id=place(0, True), device_id_type=MESH)


def await_greetings():
    pl.semaphore_wait(pltpu.get_barrier_semaphore(), 5)


def bits(code):
    return bin(code).count("1")


def top_of(order, code):
    return max([order.index(k) for k in DIMS if code & k], default=-1)


def dot(a, b):
    return jnp.dot(a, b, preferred_element_type=F32)


def dot_nt(a, b):
    return lax.dot_general(a, b, (((1,), (1,)), ((), ())), preferred_element_type=F32)


def dot_tn(a, b):
    return lax.dot_general(a, b, (((0,), (0,)), ((), ())), preferred_element_type=F32)


def normed(v):
    centred = v - jnp.mean(v, axis=-1, keepdims=True)
    r = lax.rsqrt(jnp.mean(centred * centred, axis=-1, keepdims=True) + 1e-05)
    return centred * r, r


def norm_back(e, xhat, r, gain):
    eg = e * gain
    return r * (eg - jnp.mean(eg, axis=-1, keepdims=True) - xhat * jnp.mean(eg * xhat, axis=-1, keepdims=True))


def column_of(row):
    wide = jnp.broadcast_to(row.astype(F32), (128, row.shape[1]))
    return jnp.transpose(wide).astype(jnp.int32)


T, PP, Q, R = (Z2, Z1, X, Y), (Z2, Z1, Y, X), (Z2, Y, X, Z1), (Y, Z2, X, Z1)
GATHER_ORDERS = ((T, PP), (T, PP), (T, PP))
AHEAD = 2
DOWN, UP, OUT, QKV = range(4)
SUMS = (
    (2, ((PP, 0, 640), (R, 640, 896))),
    (1, ((PP, 0, 640), (R, 640, 896))),
    (0, ((PP, 1152, 256), (R, 1408, 128))),
    (0, ((PP, 0, 512), (R, 512, 640))),
)
SLOTS = {}
for _order in (T, PP, Q, R):
    SLOTS[_order] = {}
    for _at, _dim in enumerate(_order):
        for _code in range(16):
            if top_of(_order, _code) < _at:
                SLOTS[_order][_code, _dim] = len(SLOTS[_order])
RISING = sorted(range(1, 16), key=bits)
FALLING = sorted(range(16), key=lambda code: -bits(code))


def cut_columns(orders, cols):
    width = cols // len(orders)
    return [(order, pl.ds(at * width, width)) for at, order in enumerate(orders)]


class Links:
    def __init__(self, rows, w, gd, from_core, from_chip, share, sems):
        self.w, self.gd = w, gd
        self.from_core, self.from_chip, self.share = from_core, from_chip, share
        (
            self.asend, self.arecv, self.acsend, self.acrecv,
            self.rsend, self.rrecv, self.rcsend, self.rcrecv,
        ) = sems
        self.rows, self.cols = rows, w.shape[3]

        self.places = {(code, core): place(code, core) for code in range(16) for core in (False, True)}
        self.spans = {at: pl.ds(pl.multiple_of(d * self.rows, self.rows), self.rows) for at, (d, _) in self.places.items()}

    def place(self, code, core=False):
        return self.places[code, core]

    def at(self, code, core=False):
        return self.places[code, core][1], self.spans[code, core]

    def weight_move(self, g, part, code, dim):
        span = cut_columns(GATHER_ORDERS[g], self.cols)[part][1]
        target = self.w.at[(g,) + self.at(code) + (span,)]
        return pltpu.make_async_remote_copy(
            target,
            target,
            self.asend.at[g],
            self.arecv.at[g, code ^ dim],
            device_id=self.place(dim),
            device_id_type=MESH,
        )

    def weight_core_move(self, g, code, mine=True):
        target = self.w.at[(g,) + self.at(code, not mine)]
        return pltpu.make_async_remote_copy(
            target,
            target,
            self.acsend.at[g],
            self.acrecv.at[g],
            device_id=self.place(0, True),
            device_id_type=MESH,
        )

    def weight_forward(self, g, code):
        if code:
            target = self.w.at[(g,) + self.at(code)]
            pltpu.make_async_remote_copy(
                target, target, self.asend.at[g], self.arecv.at[g, code], device_id=self.place(Z1), device_id_type=MESH
            ).wait_recv()
        for part, order in enumerate(GATHER_ORDERS[g]):
            for dim in order[top_of(order, code) + 1 :]:
                self.weight_move(g, part, code, dim).start()
        self.weight_core_move(g, code).start()

    def weights_complete(self, g):
        target = self.w.at[g, 0]
        pltpu.make_async_remote_copy(
            target, target, self.acsend.at[g], self.acrecv.at[g], device_id=self.place(0, True), device_id_type=MESH
        ).wait_recv()

    def weights_sent(self, g):
        for ref, send, recv in (
            (self.from_chip.at[g], self.asend.at[g], self.arecv.at[g, 1]),
            (self.from_core.at[g], self.acsend.at[g], self.acrecv.at[g]),
        ):
            pltpu.make_async_remote_copy(
                ref, ref, send, recv, device_id=self.place(0, True), device_id_type=MESH
            ).wait_send()

    def grad(self, n, code, core, start, width):
        g = SUMS[n][0]
        where = self.at(code, core) + (pl.ds(start, width),)
        return (self.gd, where) if g == 2 else (self.w, (g,) + where)

    def grad_core_move(self, n, code):
        g, parts = SUMS[n]
        start, width = parts[0][1], sum(part[2] for part in parts)
        ref, where = self.grad(n, code, True, start, width)
        return pltpu.make_async_remote_copy(
            ref.at[where],
            self.from_core.at[g, code, :, pl.ds(start, width)],
            self.rcsend.at[n],
            self.rcrecv.at[n, code],
            device_id=self.place(0, True),
            device_id_type=MESH,
        )

    def grad_move(self, n, part, code, dim, sending):
        g, parts = SUMS[n]
        order, start, width = parts[part]
        ref, where = self.grad(n, code, False, start, width)
        slot = SLOTS[order][code ^ dim if sending else code, dim]
        return pltpu.make_async_remote_copy(
            ref.at[where],
            self.from_chip.at[g, slot, :, pl.ds(start, width)],
            self.rsend.at[n],
            self.rrecv.at[n, part, slot],
            device_id=self.place(dim),
            device_id_type=MESH,
        )

    def grads_to_core(self, n):
        for code in FALLING:
            self.grad_core_move(n, code).start()

    def grad_step(self, n, code):
        g, parts = SUMS[n]
        self.grad_core_move(n, code).wait_recv()
        for part, (order, start, width) in enumerate(parts):
            at = top_of(order, code)
            span = pl.ds(start, width)
            ref, where = self.grad(n, code, False, start, width)
            value = ref[where].astype(F32) + self.from_core[g, code, :, span].astype(F32)
            for dim in reversed(order[at + 1 :]):
                self.grad_move(n, part, code, dim, False).wait_recv()
                value = value + self.from_chip[g, SLOTS[order][code, dim], :, span].astype(F32)
            if code == 0:
                self.share[g, :, span] = value
            else:
                ref[where] = value.astype(BF)
                self.grad_move(n, part, code, order[at], True).start()

    def grads_sent(self, n):
        g, parts = SUMS[n]
        span = pl.ds(parts[0][1], sum(part[2] for part in parts))
        for ref, send, recv in (
            (self.from_chip.at[g, :, :, span], self.rsend.at[n], self.rrecv.at[n, 0, 0]),
            (self.from_core.at[g, :, :, span], self.rcsend.at[n], self.rcrecv.at[n, 0]),
        ):
            pltpu.make_async_remote_copy(
                ref, ref, send, recv, device_id=self.place(0, True), device_id_type=MESH
            ).wait_send()


def looped(count, body, events=()):
    events = list(events)

    @pl.loop(0, count)
    def _(i):
        body(i)
        for at in range(count):
            mine = events[len(events) * at // count : len(events) * (at + 1) // count]
            if mine:

                @pl.when(i == at)
                def _():
                    for event in mine:
                        event()


def layer_kernel(
    shape,
    linked,
    big_ref, small_ref, bvis_ref, svis_ref, bcot_ref, scot_ref, *refs,
):
    if linked:
        qkv_ref, mix_ref, up_ref, down_ref, norm_ref, up_bias_ref, *refs = refs
    else:
        w_ref, vec_ref, bias_ref, *refs = refs
    run_kernel(
        shape, linked, big_ref, small_ref, bvis_ref, svis_ref, bcot_ref, scot_ref,
        (qkv_ref, mix_ref, up_ref, down_ref, norm_ref, up_bias_ref) if linked else (w_ref, vec_ref, bias_ref), *refs,
    )


def run_kernel(
    shape,
    linked,
    big_ref, small_ref, bvis_ref, svis_ref, bcot_ref, scot_ref, weight_refs,
    out_ref, back_ref, share, vshare,
    few, w, gd, from_core, from_chip, x, n1, n2, qkv, prob, prob_small, heads, mid, acc, act, slope, cot, out_rows,
    vecs, bias, vgrad, bgrad, small, small_abs, small_sum, small_in,
    asend, arecv, acsend, acrecv, rsend, rrecv, rcsend, rcrecv, own, p_sem, c_sem, o_sem, s_sem,
):
    nb, bl, ns, sl = shape
    feat, wide = w.shape[2:]
    cut = nb * bl
    tokens = cut + ns * sl
    half = feat // 2
    pairs = half // 128
    d, t = lax.axis_index("dp"), lax.axis_index("tensor")
    block = 128
    steps = tokens // block
    tile = act.shape[2]
    tiles = act.shape[0]
    per = tiles // 2
    small_rows = ns * sl
    spans = [(i, i * bl, bl) for i in range(nb)] + [(nb, cut, small_rows)]
    chunk = 512
    strips = [(at, min(tile, feat - at)) for at in range(0, feat, tile)]

    cloads = [
        pltpu.make_async_copy(bcot_ref.at[t * nb + i], cot.at[pl.ds(i * bl, bl)], c_sem) for i in range(nb)
    ]
    cloads += [
        pltpu.make_async_copy(scot_ref.at[t * ns + i], cot.at[pl.ds(cut + i * sl, sl)], c_sem)
        for i in range(ns)
    ]
    big_len, small_len = big_ref.shape[1], small_ref.shape[1]
    ploads = []
    for i in range(nb):
        for at in range(big_len // chunk):
            source = big_ref.at[t * nb + i, pl.ds(at * chunk, chunk)]
            ploads.append((i, at, source, chunk, (bvis_ref, t * nb + i, i * bl, bl)))
    for i in range(ns):
        ploads.append((nb + i, 0, small_ref.at[t * ns + i], small_len, (svis_ref, t * ns + i, cut + i * sl, sl)))

    def pload(at):
        _, _, source, length, _ = ploads[at]
        return [
            pltpu.make_async_copy(
                source.at[:, pl.ds(start, width)],
                act.at[at % 2 * len(strips) + c, pl.ds(0, length), pl.ds(0, width)],
                p_sem.at[at, c],
            )
            for c, (start, width) in enumerate(strips)
        ]

    for copy in pload(0):
        copy.start()
    for copy in cloads:
        copy.start()

    if linked:
        qkv_ref, mix_ref, up_ref, down_ref, norm_ref, up_bias_ref = weight_refs
        greet(place)
        stage = [
            pltpu.make_async_copy(ref, share.at[g], own.at[g, 0]) for g, ref in ((1, up_ref), (2, down_ref))
        ]
        heads_in = [
            pltpu.make_async_copy(qkv_ref.at[c], share.at[0, :, pl.ds(c * half, half)], own.at[0, c % 2]) for c in range(3)
        ]
        heads_in.append(pltpu.make_async_copy(mix_ref, share.at[0, :, pl.ds(3 * half, half)], own.at[0, 1]))
        for copy in heads_in + stage:
            copy.start()
        few[...] = jnp.zeros_like(few)
        few[: norm_ref.shape[0], : norm_ref.shape[1]] = norm_ref[...]
        few[6:7, : up_bias_ref.shape[1]] = up_bias_ref[...]
        link = Links(
            mix_ref.shape[0], w, gd, from_core, from_chip, share,
            (asend, arecv, acsend, acrecv, rsend, rrecv, rcsend, rcrecv),
        )
        for k in range(2):
            both = share.at[0, :, pl.ds(0, 2 * half)]
            pltpu.make_async_copy(both, both, own.at[0, k]).wait()
        w[(0,) + link.at(0)] = share[0].astype(BF)
        for g in (1, 2):
            stage[g - 1].wait()
            w[(g,) + link.at(0)] = share[g].astype(BF)

        def small_place(code):
            return link.place(code >> 1, bool(code & 1))

        small[0] = few[...].astype(BF)
        await_greetings()
    else:
        w_ref, vec_ref, bias_ref = weight_refs
        wloads = [
            [pltpu.make_async_copy(w_ref.at[g, k], w.at[g, k], own.at[g, k]) for k in range(2)] for g in range(3)
        ]
        for copy in sum(wloads, []):
            copy.start()

    def small_move(k):
        return pltpu.make_async_remote_copy(
            small.at[pl.ds(0, 2**k)],
            small.at[pl.ds(2**k, 2**k)],
            s_sem.at[0, k],
            s_sem.at[1, k],
            device_id=small_place(2**k),
            device_id_type=MESH,
        )

    def small_step(k):
        def go():
            if k:
                small_move(k - 1).wait()
            if k < 5:
                small_move(k).start()

        return go

    def set_vectors():
        for code in range(32):
            pd, pt = small_place(code)
            small_abs[pt, pd] = small[code]
        vec_sum, bias_sum = 0.0, [0.0, 0.0]
        parts = feat // 48 if linked else 0
        for at in range(parts):
            for k in range(2):
                value = small_abs[k, at].astype(F32)
                if k == 0:
                    padded = jnp.concatenate([value, jnp.zeros((16, feat - 128), F32)], axis=1)
                    vec_sum = vec_sum + (pltpu.roll(padded, at * 48, 1) if at else padded)
                padded = jnp.concatenate([value[:8], jnp.zeros((8, wide - 128), F32)], axis=1)
                bias_sum[k] = bias_sum[k] + (pltpu.roll(padded, at * 96, 1) if at else padded)
        vecs[...] = vec_sum[:8]
        for k in range(2):
            bias[k] = bias_sum[k]

    def vec(i):
        return vecs[i : i + 1, :]

    def rows_of(i):
        return pl.ds(pl.multiple_of(i * block, block), block)

    def pick(at):
        def go():
            chip, part, _, length, (vis_ref, row, first_row, count) = ploads[at]
            for copy in pload(at):
                copy.wait()
            if at + 1 < len(ploads):
                for copy in pload(at + 1):
                    copy.start()
            column = column_of(vis_ref[pl.ds(row, 1), :]) - part * length
            lane = lax.broadcasted_iota(jnp.int32, column.shape, 1)
            hot = jnp.concatenate([(column == lane + k * 128).astype(BF) for k in range(length // 128)], axis=1)
            rows = pl.ds(first_row, count)
            for c, (start, width) in enumerate(strips):
                picked = dot(hot, act[at % 2 * len(strips) + c, :length, :width])
                span = pl.ds(start, width)
                if part:
                    picked = picked + x[rows, span].astype(F32)
                x[rows, span] = picked.astype(BF)

        return go

    picks = [pick(at) for at in range(len(ploads))]

    def weight_event(g, code):
        return lambda: link.weight_forward(g, code)

    if linked:
        order = sorted(
            [(bits(code) + AHEAD * g, g, n, code) for g in range(3) for n, code in enumerate([0] + RISING)]
        )
        sequence = [(g, weight_event(g, code)) for _, g, _, code in order]
        last = [max(i for i, (g, _) in enumerate(sequence) if g == k) for k in range(3)]
        weight_events = [[e for _, e in sequence[lo : hi + 1]] for lo, hi in zip([0] + [i + 1 for i in last], last)]
        smalls = [small_step(k) for k in range(6)]
        mixed = [weight_events[0][0], smalls[0], picks[0], picks[1]] + weight_events[0][1:3] + [smalls[1], picks[2]]
        mixed += weight_events[0][3:5] + [picks[3], smalls[2]] + weight_events[0][5:8] + [picks[4], smalls[3]]
        mixed += weight_events[0][8:11] + picks[5:] + [smalls[4]] + weight_events[0][11:14] + [smalls[5]]
        mixed += weight_events[0][14:]
        for event in mixed:
            event()
        set_vectors()
    else:
        weight_events = [[], [], []]
        for event in picks:
            event()
        vecs[...] = vec_ref[...]
        bias[...] = bias_ref[...]

    def weights_ready(g):
        if linked:
            link.weights_complete(g)
        else:
            for copy in wloads[g]:
                copy.wait()

    def norm_one(i):
        xhat, r = normed(x[rows_of(i), :].astype(F32))
        value = xhat * vec(0) + vec(1)
        n1[rows_of(i), :] = value.astype(BF)

    looped(steps, norm_one)
    weights_ready(0)
    events = weight_events[1]
    lot = len(events) // 3

    def make_qkv(i):
        k, c = i // 3, i % 3
        span = pl.ds(pl.multiple_of(c * half, half), half)
        qkv[k, :, span] = dot(n1[...], w[0, k, :, span]).astype(BF)

    looped(6, make_qkv, events[:lot])

    lane = lax.broadcasted_iota(jnp.int32, (1, 128), 1)
    first = lane < HD
    zero = jnp.zeros((), BF)

    def softmax(scores):
        e = jnp.exp(scores - jnp.max(scores, axis=-1, keepdims=True))
        return e / jnp.sum(e, axis=-1, keepdims=True)

    same = (
        lax.broadcasted_iota(jnp.int32, (small_rows, small_rows), 0) // sl
        == lax.broadcasted_iota(jnp.int32, (small_rows, small_rows), 1) // sl
    )

    def pair_spans(pair):
        k, j = pair // pairs, pair % pairs
        return k, [pl.ds(pl.multiple_of(c * half + j * 128, 128), 128) for c in range(3)]

    def attention(pair):
        k, lanes = pair_spans(pair)
        stage = []
        for i, start, count in spans:
            rows = pl.ds(start, count)
            q, key, value = (qkv[k, rows, lanes[c]] for c in range(3))
            scores = [dot_nt(jnp.where(first if h == 0 else ~first, q, zero), key) * HD ** (-0.5) for h in range(2)]
            stage.append((i, rows, value, scores))
        chances = []
        for i, rows, value, scores in stage:
            if i == nb:
                scores = [jnp.where(same, one, -jnp.inf) for one in scores]
            chances.append([softmax(one).astype(BF) for one in scores])
        here = pl.ds(pl.multiple_of(pair * 128, 128), 128)
        for (i, rows, value, _), p in zip(stage, chances):
            mixed = [dot(one, value) for one in p]
            heads[rows, here] = jnp.where(first, mixed[0], mixed[1]).astype(BF)
        for (i, _, _, _), p in zip(stage, chances):
            for h in range(2):
                if i == nb:
                    prob_small[pair, h] = p[h]
                else:
                    prob[pair, i, h] = p[h]

    looped(2 * pairs, attention, events[lot:])

    out_span = pl.ds(3 * half, half)

    def project(i):
        span = pl.ds(pl.multiple_of(i * 256, 256), 256)
        mid[:, span] = dot_nt(heads[:, :half], w[0, 0, span, out_span]) + dot_nt(heads[:, half:], w[0, 1, span, out_span])

    looped(feat // 256, project)

    def norm_two(i):
        middle = x[rows_of(i), :].astype(F32) + mid[rows_of(i), :] + vec(4)
        mid[rows_of(i), :] = middle
        xhat, r = normed(middle)
        value = xhat * vec(2) + vec(3)
        n2[rows_of(i), :] = value.astype(BF)
        acc[rows_of(i), :] = middle + vec(5)

    looped(steps, norm_two)
    pltpu.make_async_copy(cot, cot, c_sem).wait()

    weights_ready(1)
    events = weight_events[2]
    lot = len(events) * 2 // 3

    def grad_events(n, lo, hi):
        if not linked:
            return []
        return [functools.partial(link.grad_step, n, code) for code in FALLING[lo:hi]]

    def woven(*lists):
        keyed = [((n + 0.5) / len(events), at, event) for at, events in enumerate(lists) for n, event in enumerate(events)]
        return [event for _, _, event in sorted(keyed, key=lambda one: one[:2])]

    def tile_of(i):
        return i // per, pl.ds(pl.multiple_of((i % per) * tile, tile), tile)

    def up(i):
        at, here = i // 2, pl.ds(pl.multiple_of(i % 2 * 256, 256), 256)
        k, span = at // per, pl.ds(pl.multiple_of(at % per * tile + i % 2 * 256, 256), 256)
        pre = dot(n2[...], w[1, k, :, span]) + bias[k, 6:7, span]
        cdf = 0.5 * (1.0 + lax.erf(pre * 0.7071067811865476))
        act[at, :, here] = (pre * cdf).astype(BF)
        slope[at, :, here] = (cdf + pre * jnp.exp(-0.5 * pre * pre) * 0.3989422804014327).astype(BF)

    looped(tiles * 2, up, events[:lot])

    def grad_down(i):
        k, span = tile_of(i)
        gd[k, :, span] = dot_tn(cot[...], act[i]).astype(BF)

    looped(tiles, grad_down, events[lot:])
    if linked:
        link.grads_to_core(DOWN)
    weights_ready(2)

    def down(i):
        k, span = tile_of(i)
        acc[...] += dot_nt(act[i], w[2, k, :, span])

    looped(tiles, down, grad_events(DOWN, 0, 3))
    out_rows[...] = acc[...].astype(BF)

    def row_moves(kind, n):
        rows = pl.ds(n * 64, 64)
        source = (out_rows if kind == 0 else n2).at[rows]
        target = out_ref if kind == 0 else back_ref
        target = target.at[t, rows] if linked else target.at[rows]
        near = pltpu.make_async_copy(source, target, o_sem.at[0, kind])
        if not linked:
            return [near]
        far = pltpu.make_async_remote_copy(
            source, target, o_sem.at[1, kind], o_sem.at[2, kind], device_id=link.place(Y), device_id_type=MESH
        )
        return [near, far]

    def row_event(kind, n):
        def go():
            for move in row_moves(kind, n):
                move.start()

        return go

    outs = [row_event(0, n) for n in range(tokens // 64)]

    acc[...] = jnp.zeros_like(acc)
    if linked:
        for g in range(3):
            link.weights_sent(g)

    def back_up(i):
        k, span = tile_of(i)
        back = (slope[i].astype(F32) * dot(cot[...], w[2, k, :, span])).astype(BF)
        bgrad[k, 6:7, span] = jnp.sum(back.astype(F32), axis=0, keepdims=True)
        acc[...] += dot_nt(back, w[1, k, :, span])
        w[1, k, :, span] = dot_tn(n2[...], back).astype(BF)

    bgrad[...] = jnp.zeros_like(bgrad)
    looped(tiles, back_up, woven(grad_events(DOWN, 3, 9), outs[:5]))
    if linked:
        link.grads_to_core(UP)

    vgrad[...] = jnp.zeros_like(vgrad)

    def norm_two_back(i):
        e = acc[rows_of(i), :]
        xhat, r = normed(mid[rows_of(i), :])
        back_out = cot[rows_of(i), :].astype(F32)
        back_middle = back_out + norm_back(e, xhat, r, vec(2))
        acc[rows_of(i), :] = back_middle
        cot[rows_of(i), :] = back_middle.astype(BF)
        vgrad[2:3, :] += jnp.sum(e * xhat, axis=0, keepdims=True)
        vgrad[3:4, :] += jnp.sum(e, axis=0, keepdims=True)
        vgrad[4:5, :] += jnp.sum(back_middle, axis=0, keepdims=True)
        vgrad[5:6, :] += jnp.sum(back_out, axis=0, keepdims=True)

    looped(steps, norm_two_back, woven(grad_events(DOWN, 9, 12), grad_events(UP, 0, 3), outs[5:7]))

    dheads = heads
    for k in range(2):
        here = pl.ds(k * half, half)
        grad = dot_tn(cot[...], heads[:, here]).astype(BF)
        dheads[:, here] = dot(cot[...], w[0, k, :, out_span]).astype(BF)
        w[0, k, :, out_span] = grad

    if linked:
        link.grads_to_core(OUT)

    def attention_back(i, rows, some):
        stage = []
        for pair in some:
            k, lanes = pair_spans(pair)
            q, key, value = (qkv[k, rows, lanes[c]] for c in range(3))
            dh = dheads[rows, pl.ds(pl.multiple_of(pair * 128, 128), 128)]
            p = [prob_small[pair, h] if i == nb else prob[pair, i, h] for h in range(2)]
            dp = [dot_nt(jnp.where(first if h == 0 else ~first, dh, zero), value) for h in range(2)]
            ds = []
            for h in range(2):
                pf = p[h].astype(F32)
                ds.append((pf * (dp[h] - jnp.sum(pf * dp[h], axis=-1, keepdims=True))).astype(BF))
            stage.append((k, lanes, q, key, dh, p, ds))
        done = []
        scale = HD ** (-0.5)
        for k, lanes, q, key, dh, p, ds in stage:
            dq, dk, dv = [dot(one, key) for one in ds], [dot_tn(one, q) for one in ds], [dot_tn(one, dh) for one in p]
            done.append((k, lanes[0], jnp.where(first, dq[0], dq[1]) * scale))
            done.append((k, lanes[1], jnp.where(first, dk[0], dk[1]) * scale))
            done.append((k, lanes[2], jnp.where(first, dv[0], dv[1])))
        for k, here, value in done:
            qkv[k, rows, here] = value.astype(BF)

    during = [
        woven(grad_events(DOWN, 12, 16), grad_events(UP, 3, 6), outs[7:9]),
        woven(grad_events(UP, 6, 9), grad_events(OUT, 0, 3), outs[9:]),
        woven(grad_events(UP, 9, 11), grad_events(OUT, 3, 5)),
    ]
    backs = []
    for at, (i, start, count) in enumerate(spans):
        rows = pl.ds(start, count)
        looped(
            2,
            lambda n: attention_back(i, rows, [n * pairs + j for j in range(pairs)]),
            during[at][: len(during[at]) // 2] if at < 3 else [],
        )

        def back_first(n):
            span = pl.ds(pl.multiple_of(n * 256, 256), 256)
            both = pl.ds(0, 3 * half)
            mid[rows, span] = dot_nt(qkv[0, rows, both], w[0, 0, span, both]) + dot_nt(
                qkv[1, rows, both], w[0, 1, span, both]
            )

        looped(feat // 256, back_first, during[at][len(during[at]) // 2 :] if at < 3 else [])

        def norm_one_back(n):
            here = pl.ds(pl.multiple_of(start + n * block, block), block)
            e = mid[here, :]
            xhat, r = normed(x[here, :].astype(F32))
            back_in = acc[here, :] + norm_back(e, xhat, r, vec(0))
            n2[here, :] = back_in.astype(BF)
            vgrad[0:1, :] += jnp.sum(e * xhat, axis=0, keepdims=True)
            vgrad[1:2, :] += jnp.sum(e, axis=0, keepdims=True)

        looped(count // block, norm_one_back)
        mine = [row_event(1, n) for n in range(start // 64, (start + count) // 64)]
        mine[0]()
        backs += mine[1:]

    def grad_qkv(i):
        k, c = i // 3, i % 3
        span = pl.ds(pl.multiple_of(c * half, half), half)
        w[0, k, :, span] = dot_tn(n1[...], qkv[k, :, span]).astype(BF)

    looped(6, grad_qkv, woven(grad_events(UP, 11, 13), grad_events(OUT, 5, 8), backs[:3]))

    def cut_small():
        low = lax.broadcasted_iota(jnp.int32, (8, 128), 1)
        row = lax.broadcasted_iota(jnp.int32, (8, 128), 0)
        for at in range(feat // 48):
            value = vgrad[...]
            if at:
                value = pltpu.roll(value, feat - at * 48, 1)
            value = jnp.where((low < 48) & (row < 6), value[:, :128], 0.0)
            for k in range(2):
                more = bgrad[k]
                if at:
                    more = pltpu.roll(more, wide - at * 96, 1)
                small_abs_sum[k, at] = value + jnp.where((low < 96) & (row == 6), more[:, :128], 0.0)
        for code in range(32):
            pd, pt = small_place(code)
            small_sum[code] = small_abs_sum[pt, pd]

    small_abs_sum = small_in[1]
    small_got = small_in[0]

    def sum_move(k):
        return pltpu.make_async_remote_copy(
            small_sum.at[pl.ds(2**k, 2**k)],
            small_got.at[pl.ds(2**k, 2**k)],
            s_sem.at[2, k],
            s_sem.at[3, k],
            device_id=small_place(2**k),
            device_id_type=MESH,
        )

    def sum_step(k):
        def go():
            if k < 4:
                sum_move(k + 1).wait()
                here = pl.ds(0, 2 ** (k + 1))
                small_sum[here] = small_sum[here] + small_got[pl.ds(2 ** (k + 1), 2 ** (k + 1))]
            if k >= 0:
                sum_move(k).start()

        return go

    if linked:
        link.grads_to_core(QKV)
        cut_small()
        sums = [sum_step(k) for k in range(4, -2, -1)]
        first_half = grad_events(QKV, 0, 1) + woven(grad_events(UP, 13, 16), grad_events(OUT, 8, 12), grad_events(QKV, 1, 9), sums[:3], backs[3:5])
        second = woven(grad_events(OUT, 12, 16), grad_events(QKV, 9, 16), sums[3:], backs[5:])
        for event in first_half + second:
            event()
        vshare[...] = small_sum[0]
        for n in range(4):
            link.grads_sent(n)
    else:
        for event in backs:
            event()
        saves = []
        for g in range(3):
            for k in range(2):
                source = gd.at[k] if g == 2 else w.at[g, k]
                saves.append(pltpu.make_async_copy(source, share.at[g, k], own.at[g, k]))
        for copy in saves:
            copy.start()
        for copy in saves:
            copy.wait()
        vshare[pl.ds(0, 8), pl.ds(0, feat)] = vgrad[...]
        for k in range(2):
            vshare[pl.ds(8 + 8 * k, 8), :] = bgrad[k]
    for kind, ref in enumerate((out_rows, n2)):
        pltpu.make_async_copy(ref, ref, o_sem.at[0, kind]).wait()
        if linked:
            pltpu.make_async_remote_copy(
                ref, ref, o_sem.at[1, kind], o_sem.at[2, kind], device_id=link.place(Y), device_id_type=MESH
            ).wait()


VLIM = 60


def run_layer(linked, big, small, bvis, svis, bcot, scot, weights, parts, wide):
    nb, bl = bvis.shape[0] // parts, bvis.shape[1]
    ns, sl = svis.shape[0] // parts, svis.shape[1]
    tokens = nb * bl + ns * sl
    feat = big.shape[2]
    tile = wide // 3
    tiles = 6
    pairs = feat // 128
    rows = weights[1].shape[0] if linked else 48
    vm, hbm = pl.BlockSpec(memory_space=pltpu.VMEM), pl.BlockSpec(memory_space=pl.ANY)
    pair = (2, tokens, feat) if linked else (tokens, feat)
    dma = pltpu.SemaphoreType.DMA
    link = (lambda *shape: pltpu.VMEM(shape, BF)) if linked else (lambda *shape: pltpu.VMEM((16, 128), BF))
    loads = nb * (big.shape[1] // 512) + ns
    return pl.pallas_call(
        functools.partial(layer_kernel, (nb, bl, ns, sl), linked),
        out_shape=(
            jax.ShapeDtypeStruct(pair, BF),
            jax.ShapeDtypeStruct(pair, BF),
            jax.ShapeDtypeStruct((3, rows, wide) if linked else weights[0].shape, F32 if linked else BF),
            jax.ShapeDtypeStruct((8, 128) if linked else (24, wide), F32),
        ),
        in_specs=[hbm, hbm, vm, vm, hbm, hbm] + ([hbm] * 4 + [vm, vm] if linked else [hbm, vm, vm]),
        out_specs=(hbm, hbm, vm if linked else hbm, vm),
        scratch_shapes=[
            pltpu.VMEM((16, 128), F32),
            pltpu.VMEM((3, 2, feat, wide), BF),
            pltpu.VMEM((2, feat, wide), BF),
            link(3, 16, rows, wide),
            link(3, 15, rows, wide),
            pltpu.VMEM((tokens, feat), BF),
            pltpu.VMEM((tokens, feat), BF),
            pltpu.VMEM((tokens, feat), BF),
            pltpu.VMEM((2, tokens, 3 * feat // 2), BF),
            pltpu.VMEM((pairs, nb, 2, bl, bl), BF),
            pltpu.VMEM((pairs, 2, ns * sl, ns * sl), BF),
            pltpu.VMEM((tokens, feat), BF),
            pltpu.VMEM((tokens, feat), F32),
            pltpu.VMEM((tokens, feat), F32),
            pltpu.VMEM((tiles, tokens, tile), BF),
            pltpu.VMEM((tiles, tokens, tile), BF),
            pltpu.VMEM((tokens, feat), BF),
            pltpu.VMEM((tokens, feat), BF),
            pltpu.VMEM((8, feat), F32),
            pltpu.VMEM((2, 8, wide), F32),
            pltpu.VMEM((8, feat), F32),
            pltpu.VMEM((2, 8, wide), F32),
            pltpu.VMEM((32, 16, 128), BF),
            pltpu.VMEM((2, 16, 16, 128), BF),
            pltpu.VMEM((32, 8, 128), F32),
            [pltpu.VMEM((32, 8, 128), F32), pltpu.VMEM((2, 16, 8, 128), F32)],
            dma((3,)),
            dma((3, 16)),
            dma((3,)),
            dma((3,)),
            dma((4,)),
            dma((4, 2, 15)),
            dma((4,)),
            dma((4, 16)),
            dma((3, 2)),
            dma((loads, 2)),
            dma,
            dma((3, 2)),
            dma((4, 5)),
        ],
        compiler_params=pltpu.CompilerParams(
            collective_id=0 if linked else None, has_side_effects=linked, vmem_limit_bytes=VLIM * MIB
        ),
        name="layer",
    )(big, small, bvis, svis, bcot, scot, *weights)


def adam_step(weight, moment_one, moment_two, gradient, step_rate, decay_rate):
    moment_one = 0.9 * moment_one + 0.1 * gradient
    moment_two = 0.999 * moment_two + 0.001 * gradient * gradient
    fixed_one = moment_one / (1.0 - 0.9**STEP_NUMBER)
    fixed_two = moment_two / (1.0 - 0.999**STEP_NUMBER)
    update = fixed_one / (jnp.sqrt(fixed_two) + 1e-08) + decay_rate * weight
    return (weight - step_rate * update, moment_one, moment_two)


def finish_kernel(bvis_ref, svis_ref, orow_ref, osmall_ref, brow_ref, bsmall_ref, share_ref, few_ref, *refs):
    states, (bout_ref, sout_ref, big_ref, small_ref), new = refs[:18], refs[18:22], refs[22:]
    i = pl.program_id(0)

    def spread(vis, rows, length):
        hot = lax.broadcasted_iota(jnp.int32, (length, vis.shape[1]), 0) == vis
        return dot(hot.astype(BF), rows)

    bout_ref[...] = orow_ref[...]
    sout_ref[...] = osmall_ref[...]
    big_ref[...] = spread(bvis_ref[pl.ds(i, 1), :], brow_ref[...], big_ref.shape[0])
    small_ref[...] = spread(svis_ref[pl.ds(i, 1), :], bsmall_ref[...], small_ref.shape[0])

    def update(at, gradient, where=...):
        old = [ref[where] for ref in states[3 * at : 3 * at + 3]]
        for ref, value in zip(new[3 * at :], adam_step(*old, gradient, LEARN_RATES[at], DECAYS[at])):
            ref[where] = value

    half = states[3].shape[1]

    @pl.when(i == 0)
    def _():
        update(2, share_ref[1])

    @pl.when(i == 1)
    def _():
        update(3, share_ref[2])

    @pl.when(i == 2)
    def _():
        for c in range(3):
            update(0, share_ref[0, :, c * half : (c + 1) * half], c)

    @pl.when(i == 3)
    def _():
        update(1, share_ref[0, :, 3 * half :])
        update(4, few_ref[6:7, : states[12].shape[1]])
        update(5, few_ref[:6, : states[15].shape[1]])


def finish(bvis, svis, outs, backs, share, few, states, big_len, small_len):
    parts, _, feat = outs.shape
    nb, bl = bvis.shape
    ns, sl = svis.shape
    each = nb // parts
    first_small = each * bl // sl
    vm = pl.BlockSpec(memory_space=pltpu.VMEM)
    rows = [
        pl.BlockSpec((None, bl, feat), lambda i: (lax.div(i, each), lax.rem(i, each), 0)),
        pl.BlockSpec((None, sl, feat), lambda i: (lax.div(i, each), first_small + lax.rem(i, each), 0)),
    ]
    whole = [pl.BlockSpec(one.shape, lambda i, n=one.ndim: (0,) * n) for one in (share, few, *states)]

    def chip(length):
        return pl.BlockSpec((None, length, feat), lambda i: (i, 0, 0))

    return pl.pallas_call(
        finish_kernel,
        grid=(nb,),
        out_shape=(
            jax.ShapeDtypeStruct((nb, bl, feat), BF),
            jax.ShapeDtypeStruct((ns, sl, feat), BF),
            jax.ShapeDtypeStruct((nb, big_len, feat), F32),
            jax.ShapeDtypeStruct((ns, small_len, feat), F32),
            *(jax.ShapeDtypeStruct(one.shape, F32) for one in states),
        ),
        in_specs=[vm, vm] + rows + rows + whole,
        out_specs=(chip(bl), chip(sl), chip(big_len), chip(small_len), *whole[2:]),
        compiler_params=pltpu.CompilerParams(vmem_limit_bytes=48 * MIB),
        name="finish",
    )(bvis, svis, outs, outs, backs, backs, share, few, *states)


def on_device(
    special,
    big_patches, small_patches, big_visible, small_visible, big_cot, small_cot,
    qkv_weight, qkv_first, qkv_second, out_weight, out_first, out_second,
    up_weight, up_first, up_second, down_weight, down_first, down_second,
    up_bias, up_bias_first, up_bias_second, norm_vectors, norm_first, norm_second,
):
    rows, half = out_weight.shape
    wide = up_weight.shape[1]
    feat = big_patches.shape[2]
    parts = feat // half
    chips = (big_patches, small_patches, big_visible, small_visible, big_cot, small_cot)
    if special:
        weights = (jnp.swapaxes(qkv_weight, 0, 1), out_weight, up_weight, down_weight, norm_vectors, up_bias)
        outs, backs, share, few = run_layer(True, *chips, weights, parts, wide)
    else:
        attn = jnp.concatenate([qkv_weight.reshape(rows, 3 * half), out_weight], axis=1).astype(BF)
        piece = jnp.stack([attn, up_weight.astype(BF), down_weight.astype(BF)])
        w = lax.all_gather(lax.all_gather(piece, "dp", axis=1, tiled=True), "tensor", axis=1)
        vectors = lax.all_gather(norm_vectors.astype(BF), "dp", axis=1, tiled=True).astype(F32)
        bias = lax.all_gather(up_bias.astype(BF), "dp", axis=1, tiled=True)
        bias = lax.all_gather(bias, "tensor", axis=0).astype(F32)
        weights = (w, jnp.pad(vectors, ((0, 2), (0, 0))), jnp.pad(bias, ((0, 0), (6, 1), (0, 0))))
        out_rows, back_rows, grads, few = run_layer(False, *chips, weights, parts, wide)
        share = lax.psum_scatter(grads, "tensor", scatter_dimension=1)
        share = lax.psum_scatter(share, "dp", scatter_dimension=1, tiled=True).astype(F32)
        both = lax.all_gather(jnp.stack([out_rows, back_rows]), "tensor", axis=1)
        outs, backs = both[0], both[1]
        norm_share = lax.psum_scatter(lax.psum(few[:6, :feat], "tensor"), "dp", scatter_dimension=1, tiled=True)
        bias_share = lax.psum_scatter(few[14::8], "tensor", scatter_dimension=0, tiled=True)
        bias_share = lax.psum_scatter(bias_share, "dp", scatter_dimension=1, tiled=True)
        few = jnp.concatenate(
            [
                jnp.pad(norm_share, ((0, 0), (0, 128 - norm_share.shape[1]))),
                jnp.pad(bias_share, ((0, 1), (0, 128 - bias_share.shape[1]))),
            ]
        )
    states = (
        *(jnp.swapaxes(one, 0, 1) for one in (qkv_weight, qkv_first, qkv_second)), out_weight, out_first, out_second,
        up_weight, up_first, up_second, down_weight, down_first, down_second,
        up_bias, up_bias_first, up_bias_second, norm_vectors, norm_first, norm_second,
    )
    done = finish(
        big_visible, small_visible, outs, backs, share, few, states, big_patches.shape[1], small_patches.shape[1]
    )
    return (*done[:4], *(jnp.swapaxes(one, 0, 1) for one in done[4:7]), *done[7:])


def solution(mesh):
    special = mesh.shape["dp"] == 16 and mesh.shape["tensor"] == 2
    chips = P("dp", None, None)
    matrix, qkv = P("dp", "tensor"), P("dp", None, "tensor")
    states = (qkv,) * 3 + (matrix,) * 9 + (P("tensor", "dp"),) * 3 + (P(None, "dp"),) * 3
    return jax.shard_map(
        functools.partial(on_device, special),
        mesh=mesh,
        in_specs=(chips, chips, P("dp", None), P("dp", None), chips, chips) + states,
        out_specs=(chips,) * 4 + states,
        check_vma=False,
    )
```
